32 devices in a mesh: wide: 16 (over z, x, core), narrow: 2 (over y).
Axes of the slice: x: 2, y: 2, z: 4, core: 2. Of those that a mesh axis runs over, the one named last changes fastest.
Arguments:
- solution: float32 [640, 320, 320], P('wide', 'narrow'), may hold values from -6 to 6
- residual: float32 [640, 320, 320], P('wide', 'narrow'), may hold values from -45 to 45
- direction: float32 [640, 320, 320], P('wide', 'narrow'), may hold values from -14 to 14
- previous_product: float32 [1], replicated, may hold values from 9830400 to 98304000
- basis_x: float32 [640, 640], P('wide'), may hold values from -0.25 to 0.25
- basis_y: float32 [320, 320], P('narrow'), may hold values from -0.3125 to 0.3125
- basis_z: float32 [320, 320], P('narrow'), may hold values from -0.3125 to 0.3125
- eigen_x: float32 [640], replicated, may hold values from 0.2 to 4
- eigen_y: float32 [320], replicated, may hold values from 0.2 to 4
- eigen_z: float32 [320], replicated, may hold values from 0.2 to 4
Outputs:
- solution: float32 [640, 320, 320], P('wide', 'narrow')
- residual: float32 [640, 320, 320], P('wide', 'narrow')
- direction: float32 [640, 320, 320], P('wide', 'narrow')
The draws below stay inside these ranges and needn't reach their ends.
All inputs are finite; a program needn't handle non-finite values.
Results may differ from the reference program's by a relative error of at most 0.00021.
Values sent between devices are 32-bit elements; how exact they have to be, the bound alone decides.
No kernel may reach another device: no remote copies, remote signals or barrier semaphores. Data moves between devices by JAX's collectives and lax.ppermute only.
A program may use at most 192 MiB of HBM per device.

```python
import math
import jax
import jax.numpy as jnp
from jax import lax

NX = 640
NY = 320
NZ = 320
ITERS = 1


def scaled_field(key, amplitude):
    noise_key = jax.random.fold_in(key, 0)
    along_x = jnp.arange(NX, dtype=jnp.float32) / (NX - 1)
    along_y = jnp.arange(NY, dtype=jnp.float32) / (NY - 1)
    ramp = (0.5 + along_x)[:, None, None] * (0.7 + 0.6 * along_y)[None, :, None]
    values = jax.random.truncated_normal(noise_key, -4.0, 4.0, (NX, NY, NZ), jnp.float32) * ramp
    return (amplitude * values).astype(jnp.float32)


def draw_residual(key, part):
    return scaled_field(jax.random.fold_in(key, 11), 1.0)


def draw_direction(key, part):
    return scaled_field(jax.random.fold_in(key, 23), 0.3)


def steps_of(key, extent, cuts, smallest, largest):
    loudness = 1.0
    for axis_at, shards_of in cuts:
        heights = jax.random.uniform(jax.random.fold_in(jax.random.fold_in(key, 6), axis_at), (shards_of,), jnp.float32, smallest / len(cuts), largest / len(cuts))
        loudness = loudness * jnp.repeat(jnp.exp(heights), extent[axis_at] // shards_of).reshape((-1,) + (1,) * (len(extent) - 1 - axis_at))
    return loudness


def centred(own_key, dims, scale, limit, shards=(), kind=jnp.bfloat16):
    loudness = steps_of(own_key, dims, shards, -0.22, 0.18) if shards else 1.0
    drawn = jax.random.normal(own_key, dims, jnp.float32) * scale * loudness
    return jnp.minimum(jnp.maximum(drawn, -limit), limit).astype(kind)


def setup_inputs(seed: int = 0) -> dict:
    arg_keys = jax.random.split(jax.random.key(seed), 11)
    return {
        "solution": centred(arg_keys[0], (NX, NY, NZ), 1.0, 6.0, ((0, 16), (1, 2)), jnp.float32),
        "residual": draw_residual(jax.random.fold_in(arg_keys[10], 71), 0),
        "direction": draw_direction(jax.random.fold_in(arg_keys[10], 71), 0),
        "previous_product": jnp.clip(jnp.exp(jax.random.uniform(arg_keys[3], (1,), jnp.float32, math.log(9830400), math.log(98304000))), 9830400, 98304000),
        "basis_x": centred(arg_keys[4], (NX, NX), NX ** -0.5, 0.25, ((0, 16),), jnp.float32),
        "basis_y": centred(arg_keys[5], (NY, NY), NY ** -0.5, 0.3125, ((0, 2),), jnp.float32),
        "basis_z": centred(arg_keys[6], (NZ, NZ), NZ ** -0.5, 0.3125, ((0, 2),), jnp.float32),
        "eigen_x": jnp.clip(jnp.exp(jax.random.uniform(arg_keys[7], (NX,), jnp.float32, math.log(0.2), math.log(4.0))), 0.2, 4.0),
        "eigen_y": jnp.clip(jnp.exp(jax.random.uniform(arg_keys[8], (NY,), jnp.float32, math.log(0.2), math.log(4.0))), 0.2, 4.0),
        "eigen_z": jnp.clip(jnp.exp(jax.random.uniform(arg_keys[9], (NZ,), jnp.float32, math.log(0.2), math.log(4.0))), 0.2, 4.0),
    }


mass_band = (1.0 / 5040.0, 1.0 / 42.0, 397.0 / 1680.0, 151.0 / 315.0, 397.0 / 1680.0, 1.0 / 42.0, 1.0 / 5040.0)
stiff_band = (-1.0 / 120.0, -0.2, -0.125, 2.0 / 3.0, -0.125, -0.2, -1.0 / 120.0)
highest = lax.Precision.HIGHEST


def banded(field, coeffs, axis, length):
    total = coeffs[0] * lax.slice_in_dim(field, 0, length, axis=axis)
    for offset in range(1, 7):
        total = total + coeffs[offset] * lax.slice_in_dim(field, offset, offset + length, axis=axis)
    return total


def apply_padded(padded, length_x, length_y):
    length_z = padded.shape[2]
    along_z = jnp.pad(padded, ((0, 0), (0, 0), (3, 3)))
    mass_z = banded(along_z, mass_band, 2, length_z)
    stiff_z = banded(along_z, stiff_band, 2, length_z)
    first = banded(mass_z, mass_band, 1, length_y)
    second = banded(mass_z, stiff_band, 1, length_y) + banded(stiff_z, mass_band, 1, length_y)
    return banded(first, stiff_band, 0, length_x) + banded(second, mass_band, 0, length_x)


def precondition(field, basis_x, basis_y, basis_z, eigen_x, eigen_y, eigen_z):
    spectral = jnp.einsum('xyz,zc->xyc', field, basis_z, precision=highest)
    spectral = jnp.einsum('xyc,yb->xbc', spectral, basis_y, precision=highest)
    spectral = jnp.einsum('xbc,xa->abc', spectral, basis_x, precision=highest)
    spectral = spectral / (eigen_x[:, None, None] + eigen_y[None, :, None] + eigen_z[None, None, :])
    spectral = jnp.einsum('abc,xa->xbc', spectral, basis_x, precision=highest)
    spectral = jnp.einsum('xbc,yb->xyc', spectral, basis_y, precision=highest)
    return jnp.einsum('xyc,zc->xyz', spectral, basis_z, precision=highest)


def reference(solution, residual, direction, previous_product, basis_x, basis_y, basis_z, eigen_x, eigen_y, eigen_z):
    product_before = previous_product[0]
    for iteration in range(ITERS):
        precond = precondition(residual, basis_x, basis_y, basis_z, eigen_x, eigen_y, eigen_z)
        product_now = jnp.sum(residual * precond)
        direction = precond + (product_now / product_before) * direction
        image = apply_padded(jnp.pad(direction, ((3, 3), (3, 3), (0, 0))), NX, NY)
        alpha = product_now / jnp.sum(direction * image)
        solution = solution + alpha * direction
        residual = residual - alpha * image
        product_before = product_now
    return solution, residual, direction
```

```python
import functools

import jax
import jax.numpy as jnp
from jax import lax
from jax.experimental import pallas as pl
from jax.experimental.pallas import tpu as pltpu
from jax.sharding import PartitionSpec as P

mass_band = (
    1.0 / 5040.0,
    1.0 / 42.0,
    397.0 / 1680.0,
    151.0 / 315.0,
    397.0 / 1680.0,
    1.0 / 42.0,
    1.0 / 5040.0,
)
stiff_band = (-1.0 / 120.0, -0.2, -0.125, 2.0 / 3.0, -0.125, -0.2, -1.0 / 120.0)
highest = lax.Precision.HIGHEST
LANES = 128
HALO = 3
EDGE = 8
both = ("wide", "narrow")
budget = 100 * 1024 * 1024 // 2


def split(x):
    high = x.astype(jnp.bfloat16)
    low = (x - high.astype(jnp.float32)).astype(jnp.bfloat16)
    return high, low


def dot3(left, right, over):
    dims = ((over[:1], over[1:]), ((), ()))
    one = functools.partial(
        lax.dot_general, dimension_numbers=dims, preferred_element_type=jnp.float32
    )
    return one(left[0], right[0]) + one(left[1], right[0]) + one(left[0], right[1])


class Plan:
    def __init__(self, cells_x, cells_y, cells_z, total_x, total_y, wide, narrow):
        self.cells_x, self.cells_y, self.cells_z = cells_x, cells_y, cells_z
        self.total_x, self.total_y = total_x, total_y
        self.wide, self.narrow, self.count = wide, narrow, wide * narrow
        self.rest = cells_y - LANES
        self.fits = (
            cells_z % self.count == 0
            and cells_x % 8 == 0
            and self.rest > 0
            and LANES % self.rest == 0
            and self.rest < LANES
            and total_y % LANES == LANES // 2
            and wide % 2 == 0
            and (total_x // 2) % 16 == 0
            and self.count % 8 == 0
        )
        if not self.fits:
            return
        self.share = cells_z // self.count
        self.group = LANES // self.rest
        self.tiles = cells_x // 8
        self.chunks = [
            (start, min(self.group, self.share - start))
            for start in range(0, self.share, self.group)
        ]
        self.fits = (
            self.group % 2 == 0
            and self.share % 2 == 0
            and len(self.chunks) > 1
            and self.chunks[-1][1] < self.group
        )

    def rows(self, chunk):
        start, size = self.chunks[chunk]
        return start * self.count, size * self.count

    def message(self, chunk):
        return (self.count, self.tiles, self.chunks[chunk][1] + 1, 8, LANES)


def forward_kernel(plan, field_ref, basis_ref, *refs):
    outs = refs[: len(plan.chunks)]
    high_ref, low_ref, stage_ref = refs[len(plan.chunks) :]

    @pl.when(pl.program_id(0) == 0)
    def _():
        high_ref[...], low_ref[...] = split(basis_ref[...])

    basis = (high_ref[...], low_ref[...])
    for i in range(8):
        stage_ref[i] = dot3(basis, split(field_ref[i]), (1, 1))
    for chunk, (start, size) in enumerate(plan.chunks):
        rests = []
        for j in range(size):
            at = (start + j) * plan.count
            turned = jnp.swapaxes(stage_ref[:, at : at + plan.count, :], 0, 1)
            outs[chunk][:, 0, j] = turned[:, :, :LANES]
            rests.append(turned[:, :, LANES:])
        while len(rests) < plan.group:
            rests.append(jnp.zeros_like(rests[0]))
        outs[chunk][:, 0, size] = jnp.concatenate(rests, axis=2)


def forward_z(plan, field, basis):
    shapes = [jax.ShapeDtypeStruct(plan.message(k), jnp.float32) for k in range(len(plan.chunks))]
    return pl.pallas_call(
        functools.partial(forward_kernel, plan),
        grid=(plan.tiles,),
        in_specs=[
            pl.BlockSpec((8, plan.cells_y, plan.cells_z), lambda t: (t, 0, 0)),
            pl.BlockSpec(basis.shape, lambda t: (0, 0)),
        ],
        out_specs=[
            pl.BlockSpec((s.shape[0], 1) + s.shape[2:], lambda t: (0, t, 0, 0, 0)) for s in shapes
        ],
        out_shape=shapes,
        scratch_shapes=[
            pltpu.VMEM(basis.shape, jnp.bfloat16),
            pltpu.VMEM(basis.shape, jnp.bfloat16),
            pltpu.VMEM((8, plan.cells_z, plan.cells_y), jnp.float32),
        ],
        compiler_params=pltpu.CompilerParams(vmem_limit_bytes=budget),
        cost_estimate=pl.CostEstimate(
            flops=6 * field.size * plan.cells_z, bytes_accessed=8 * field.size, transcendentals=0
        ),
        name="forward_z",
    )(field, basis)


def inverse_kernel(plan, chunks, final, *refs):
    refs = list(refs)
    parts = [refs.pop(0) for _ in chunks]
    basis_ref = refs.pop(0)
    if final:
        base_ref, old_ref, before_ref = refs.pop(0), refs.pop(0), refs.pop(0)
        out_ref, now_ref = refs.pop(0), refs.pop(0)
    else:
        out_ref = refs.pop(0)
    high_ref, low_ref, stage_ref = refs

    @pl.when(pl.program_id(0) == 0)
    def _():
        high_ref[...], low_ref[...] = split(basis_ref[...])

    at = 0
    for part, chunk in zip(parts, chunks):
        size = plan.chunks[chunk][1]
        rests = part[:, 0, size]
        for q in range(size):
            stage_ref[:, at : at + plan.count, :LANES] = jnp.swapaxes(part[:, 0, q], 0, 1)
            stage_ref[:, at : at + plan.count, LANES:] = jnp.swapaxes(
                rests[:, :, q * plan.rest : (q + 1) * plan.rest], 0, 1
            )
            at += plan.count
    if final:
        sums = parts[-1][:, 0, plan.chunks[chunks[-1]][1], 0, LANES - 1 :]
        now = jnp.sum(sums, axis=0, keepdims=True)
        now_ref[...] = jnp.broadcast_to(now, now_ref.shape)
        beta = now / before_ref[...]
    basis = (high_ref[...], low_ref[...])
    for i in range(8):
        value = dot3(split(stage_ref[i].T), basis, (1, 0))
        if final:
            value = base_ref[i] + value + beta * old_ref[i]
        out_ref[i] = value


def inverse_z(plan, parts, chunks, basis, base=None, old=None, before=None):
    final = base is not None
    brick = pl.BlockSpec((8, plan.cells_y, plan.cells_z), lambda t: (t, 0, 0))
    shape = jax.ShapeDtypeStruct((plan.cells_x, plan.cells_y, plan.cells_z), jnp.float32)
    low = plan.rows(chunks[0])[0]
    high = sum(plan.rows(chunks[-1]))
    basis = basis[low:high]
    one = pl.BlockSpec((1, 1), lambda t: (0, 0))
    in_specs = [
        pl.BlockSpec((p.shape[0], 1) + p.shape[2:], lambda t: (0, t, 0, 0, 0)) for p in parts
    ] + [pl.BlockSpec(basis.shape, lambda t: (0, 0))]
    operands = list(parts) + [basis]
    out_specs, out_shape = brick, shape
    if final:
        in_specs += [brick, brick, one]
        operands += [base, old, before.reshape(1, 1)]
        out_specs = [brick, pl.BlockSpec((8, LANES), lambda t: (0, 0))]
        out_shape = [shape, jax.ShapeDtypeStruct((8, LANES), jnp.float32)]
    return pl.pallas_call(
        functools.partial(inverse_kernel, plan, chunks, final),
        grid=(plan.tiles,),
        in_specs=in_specs,
        out_specs=out_specs,
        out_shape=out_shape,
        scratch_shapes=[
            pltpu.VMEM(basis.shape, jnp.bfloat16),
            pltpu.VMEM(basis.shape, jnp.bfloat16),
            pltpu.VMEM((8, high - low, plan.cells_y), jnp.float32),
        ],
        compiler_params=pltpu.CompilerParams(vmem_limit_bytes=budget),
        cost_estimate=pl.CostEstimate(
            flops=6 * shape.size * (high - low),
            bytes_accessed=8 * shape.size,
            transcendentals=0,
        ),
        name="inverse_z",
    )(*operands)


def middle_kernel(plan, chunk, *refs):
    (
        in_ref,
        basis_x_ref,
        turned_x_ref,
        main_y_ref,
        rest_y_ref,
        eigen_x_ref,
        shift_ref,
        total_ref,
        out_ref,
        sum_ref,
        bx_high,
        bx_low,
        tx_high,
        tx_low,
        my_high,
        my_low,
        ry_high,
        ry_low,
        u_high,
        u_low,
        q_high,
        q_low,
        rest_acc,
    ) = refs
    size = plan.chunks[chunk][1]
    last = chunk == len(plan.chunks) - 1
    wide, narrow, tiles = plan.wide, plan.narrow, plan.tiles
    half = plan.total_x // 2
    lump = wide // 2
    span = plan.total_y + LANES // 2
    width = 2 * plan.total_y
    bx_high[...], bx_low[...] = split(basis_x_ref[...])
    tx_high[...], tx_low[...] = split(turned_x_ref[...])
    my_high[...], my_low[...] = split(main_y_ref[...])
    ry_high[...], ry_low[...] = split(rest_y_ref[...])
    rest_acc[...] = jnp.zeros_like(rest_acc)

    def gathered(piece, h):
        rows = pl.ds(h * lump, lump)
        return jnp.concatenate(
            [in_ref[rows, n, :, piece].reshape(half, LANES) for n in range(narrow)], axis=1
        )

    def pair(p, total):
        for h in range(2):
            rest = split(gathered(size, h))
            parts = []
            for s in range(2):
                j = 2 * p + s
                parts.append(
                    dot3(split(gathered(j, h)), (my_high[s], my_low[s]), (1, 0))
                    + dot3(rest, (ry_high[j], ry_low[j]), (1, 0))
                )
            cut = span - LANES
            joined = jnp.concatenate(
                [
                    parts[0][:, :cut],
                    parts[0][:, cut:] + parts[1][:, :LANES],
                    parts[1][:, LANES:],
                ],
                axis=1,
            )
            rows = pl.ds(h * half, half)
            u_high[rows, :], u_low[rows, :] = split(joined)
        shift = shift_ref[p]
        for h in range(2):
            rows = pl.ds(h * half, half)
            spectral = dot3(
                (tx_high[rows, :], tx_low[rows, :]), (u_high[...], u_low[...]), (1, 0)
            )
            scaled = spectral / (eigen_x_ref[rows, :] + shift)
            total = total + jnp.sum((spectral * scaled).reshape(half // 8, 8, width), axis=0)
            q_high[rows, :], q_low[rows, :] = split(scaled)
        for h in range(2):
            rows = pl.ds(h * half, half)
            value = dot3((bx_high[rows, :], bx_low[rows, :]), (q_high[...], q_low[...]), (1, 0))
            for s in range(2):
                j = 2 * p + s
                mine = split(value[:, s * (width - span) : s * (width - span) + span])
                main = dot3(mine, (my_high[s], my_low[s]), (1, 1))
                rest_acc[rows, :] += dot3(mine, (ry_high[j], ry_low[j]), (1, 1))
                for n in range(narrow):
                    out_ref[pl.ds(h * lump, lump), n, :, j] = main[
                        :, n * LANES : (n + 1) * LANES
                    ].reshape(lump, tiles, 8, LANES)
        return total

    total = lax.fori_loop(0, size // 2, pair, jnp.zeros((8, width), jnp.float32))
    value = total_ref[...] + jnp.sum(total)
    sum_ref[...] = value
    for n in range(narrow):
        rest = rest_acc[:, n * LANES : (n + 1) * LANES]
        if last:
            lane = lax.broadcasted_iota(jnp.int32, rest.shape, 1)
            rest = jnp.where(lane >= size * plan.rest, value[:1, :], rest)
        out_ref[:, n, :, size] = rest.reshape(wide, tiles, 8, LANES)


def middle(plan, chunk, message, basis_x, turned_x, main_y, rest_y, eigen_x, shift, total):
    size = plan.chunks[chunk][1]
    shape = (plan.wide, plan.narrow) + message.shape[1:]
    square = (plan.total_x, plan.total_x)
    pencil = (plan.total_x, 2 * plan.total_y)
    half = jnp.bfloat16
    out, total = pl.pallas_call(
        functools.partial(middle_kernel, plan, chunk),
        out_shape=[
            jax.ShapeDtypeStruct(shape, jnp.float32),
            jax.ShapeDtypeStruct((8, LANES), jnp.float32),
        ],
        in_specs=[pl.BlockSpec(memory_space=pltpu.VMEM)] * 8,
        out_specs=[pl.BlockSpec(memory_space=pltpu.VMEM)] * 2,
        scratch_shapes=[
            pltpu.VMEM(square, half),
            pltpu.VMEM(square, half),
            pltpu.VMEM(square, half),
            pltpu.VMEM(square, half),
            pltpu.VMEM(main_y.shape, half),
            pltpu.VMEM(main_y.shape, half),
            pltpu.VMEM(rest_y.shape, half),
            pltpu.VMEM(rest_y.shape, half),
            pltpu.VMEM(pencil, half),
            pltpu.VMEM(pencil, half),
            pltpu.VMEM(pencil, half),
            pltpu.VMEM(pencil, half),
            pltpu.VMEM((plan.total_x, plan.narrow * LANES), jnp.float32),
        ],
        compiler_params=pltpu.CompilerParams(vmem_limit_bytes=budget),
        cost_estimate=pl.CostEstimate(
            flops=12 * size * plan.total_x * plan.total_y * (plan.total_x + plan.total_y),
            bytes_accessed=8 * message.size,
            transcendentals=0,
        ),
        name="middle",
    )(message.reshape(shape), basis_x, turned_x, main_y, rest_y, eigen_x, shift, total)
    return out.reshape(message.shape), total


def shifted(x, step_wide, step_narrow):
    wide, narrow = lax.axis_size("wide"), lax.axis_size("narrow")
    pairs = []
    for w in range(wide):
        for n in range(narrow):
            v, m = w + step_wide, n + step_narrow
            if 0 <= v < wide and 0 <= m < narrow:
                pairs.append((v * narrow + m, w * narrow + n))
    return lax.ppermute(x, both, pairs)


def stencil_kernel(plan, *refs):
    pieces = refs[:9]
    bands_ref, image_ref, sum_ref, field, high_a, low_a, h_a, h_b, total, sems = refs[9:]
    cells_x, cells_y, cells_z = plan.cells_x, plan.cells_y, plan.cells_z
    xs = (pl.ds(0, HALO), pl.ds(HALO, cells_x), pl.ds(HALO + cells_x, HALO))
    ys = (pl.ds(0, EDGE), pl.ds(EDGE, cells_y), pl.ds(EDGE + cells_y, EDGE))
    step = pl.program_id(0)

    @pl.when(step == 0)
    def _():
        copies = [
            pltpu.make_async_copy(
                pieces[3 * a + b], field.at[xs[a], ys[b], :], sems.at[3 * a + b]
            )
            for a in range(3)
            for b in range(3)
        ]
        for copy in copies:
            copy.start()
        total[...] = jnp.zeros_like(total)
        high_a[...], low_a[...] = split(bands_ref[...])
        for copy in copies:
            copy.wait()

    mass_z = (high_a[0], low_a[0])
    stiff_z = (high_a[1], low_a[1])
    padded_y = cells_y + 2 * EDGE
    blocks = -(-cells_z // LANES)

    def plane(i, carry):
        x = step * 8 + i
        middle_plane = field[x + HALO]
        first = stiff_band[HALO] * middle_plane
        second = mass_band[HALO] * middle_plane
        for o in range(1, HALO + 1):
            around = field[x + HALO - o] + field[x + HALO + o]
            first = first + stiff_band[HALO + o] * around
            second = second + mass_band[HALO + o] * around
        first, second = split(first), split(second)
        a = dot3(first, mass_z, (1, 0)) + dot3(second, stiff_z, (1, 0))
        b = dot3(second, mass_z, (1, 0))
        for k in range(blocks):
            lanes = min(LANES, cells_z - k * LANES)
            h_a[k, :, :lanes] = a[:, k * LANES : k * LANES + lanes]
            h_b[k, :, :lanes] = b[:, k * LANES : k * LANES + lanes]
        for k in range(blocks):
            lanes = min(LANES, cells_z - k * LANES)
            at = lambda ref, o: ref[k, pl.ds(EDGE + o, cells_y), :]
            image = mass_band[HALO] * at(h_a, 0) + stiff_band[HALO] * at(h_b, 0)
            for o in range(1, HALO + 1):
                image = image + mass_band[HALO + o] * (at(h_a, -o) + at(h_a, o))
                image = image + stiff_band[HALO + o] * (at(h_b, -o) + at(h_b, o))
            here = pl.ds(k * LANES, lanes)
            image_ref[i, :, here] = image[:, :lanes]
            product = image[:, :lanes] * field[x + HALO, pl.ds(EDGE, cells_y), here]
            total[:, here] += jnp.sum(product.reshape(cells_y // 8, 8, lanes), axis=0)
        return carry

    lax.fori_loop(0, 8, plane, 0)

    @pl.when(step == pl.num_programs(0) - 1)
    def _():
        sum_ref[...] = jnp.full(sum_ref.shape, jnp.sum(total[...]), jnp.float32)


def stencil(plan, direction):
    cells_x, cells_y, cells_z = direction.shape
    low_x, high_x = direction[:HALO], direction[cells_x - HALO :]
    low_y, high_y = direction[:, :EDGE], direction[:, cells_y - EDGE :]
    pieces = [
        shifted(high_x[:, cells_y - EDGE :], -1, -1),
        shifted(high_x, -1, 0),
        shifted(high_x[:, :EDGE], -1, 1),
        shifted(high_y, 0, -1),
        direction,
        shifted(low_y, 0, 1),
        shifted(low_x[:, cells_y - EDGE :], 1, -1),
        shifted(low_x, 1, 0),
        shifted(low_x[:, :EDGE], 1, 1),
    ]
    rows = lax.broadcasted_iota(jnp.int32, (cells_z, cells_z), 0)
    columns = lax.broadcasted_iota(jnp.int32, (cells_z, cells_z), 1)
    bands = []
    for band in (mass_band, stiff_band):
        matrix = jnp.zeros((cells_z, cells_z), jnp.float32)
        for o in range(-HALO, HALO + 1):
            matrix = jnp.where(rows - columns == o, band[o + HALO], matrix)
        bands.append(matrix)
    bands = jnp.stack(bands)
    padded_y = cells_y + 2 * EDGE
    blocks = -(-cells_z // LANES)
    return pl.pallas_call(
        functools.partial(stencil_kernel, plan),
        grid=(cells_x // 8,),
        in_specs=[pl.BlockSpec(memory_space=pl.ANY)] * 9
        + [pl.BlockSpec(bands.shape, lambda t: (0, 0, 0))],
        out_specs=[
            pl.BlockSpec((8, cells_y, cells_z), lambda t: (t, 0, 0)),
            pl.BlockSpec((8, LANES), lambda t: (0, 0)),
        ],
        out_shape=[
            jax.ShapeDtypeStruct(direction.shape, jnp.float32),
            jax.ShapeDtypeStruct((8, LANES), jnp.float32),
        ],
        scratch_shapes=[
            pltpu.VMEM((cells_x + 2 * HALO, padded_y, cells_z), jnp.float32),
            pltpu.VMEM(bands.shape, jnp.bfloat16),
            pltpu.VMEM(bands.shape, jnp.bfloat16),
            pltpu.VMEM((blocks, padded_y, LANES), jnp.float32),
            pltpu.VMEM((blocks, padded_y, LANES), jnp.float32),
            pltpu.VMEM((8, cells_z), jnp.float32),
            pltpu.SemaphoreType.DMA((9,)),
        ],
        compiler_params=pltpu.CompilerParams(vmem_limit_bytes=budget),
        cost_estimate=pl.CostEstimate(
            flops=18 * direction.size * cells_z, bytes_accessed=8 * direction.size, transcendentals=0
        ),
        name="stencil",
    )(*pieces, bands)


def scatter(x):
    return lax.all_to_all(x, both, split_axis=0, concat_axis=0, tiled=True)


def dealt(plan, whole_z):
    columns = whole_z.T.reshape(plan.count, plan.share, plan.cells_z)
    return jnp.swapaxes(columns, 0, 1).reshape(plan.cells_z, plan.cells_z)


def basis_y_blocks(plan, whole_y):
    by_owner = whole_y.reshape(plan.narrow, plan.cells_y, plan.total_y)
    main = by_owner[:, :LANES].reshape(plan.narrow * LANES, plan.total_y)
    rest = by_owner[:, LANES:]
    half = LANES // 2
    sides = [(0, half), (half, 0)]
    mains = jnp.stack([jnp.pad(main, ((0, 0), s)) for s in sides])
    rests = []
    for q in range(plan.group):
        after = LANES - (q + 1) * plan.rest
        padded = jnp.pad(rest, ((0, 0), (q * plan.rest, after), sides[q % 2]))
        rests.append(padded.reshape(plan.narrow * LANES, plan.total_y + half))
    return mains, jnp.stack(rests)


def by_pencils(
    plan,
    solution,
    residual,
    direction,
    previous_product,
    basis_x,
    basis_y,
    basis_z,
    eigen_x,
    eigen_y,
    eigen_z,
):
    whole_z = lax.all_gather(basis_z, "narrow", axis=0, tiled=True)
    whole_y = lax.all_gather(basis_y, "narrow", axis=0, tiled=True)
    whole_x = lax.all_gather(basis_x, "wide", axis=0, tiled=True)
    turned_z = dealt(plan, whole_z)
    messages = forward_z(plan, residual, turned_z)
    main_y, rest_y = basis_y_blocks(plan, whole_y)
    turned_x = whole_x.T
    index = lax.axis_index("wide") * plan.narrow + lax.axis_index("narrow")
    mine_z = lax.dynamic_slice_in_dim(eigen_z, index * plan.share, plan.share)
    shifts = (mine_z[:, None] + eigen_y[None, :]).reshape(plan.share // 2, 1, 2 * plan.total_y)
    arrived = [scatter(m) for m in messages]
    total = jnp.zeros((8, LANES), jnp.float32)
    returned = []
    for k, (start, size) in enumerate(plan.chunks):
        shift = shifts[start // 2 : (start + size) // 2]
        back, total = middle(
            plan,
            k,
            arrived[k],
            whole_x,
            turned_x,
            main_y,
            rest_y,
            eigen_x.reshape(-1, 1),
            shift,
            total,
        )
        returned.append(scatter(back))
    last = len(plan.chunks) - 1
    base = inverse_z(plan, returned[:last], tuple(range(last)), turned_z)
    direction, now = inverse_z(
        plan, returned[last:], (last,), turned_z, base, direction, previous_product
    )
    image, part = stencil(plan, direction)
    parts = lax.all_gather(part, both, axis=0, tiled=False)
    alpha = now[0, 0] / jnp.sum(parts[:, 0, 0])
    return solution + alpha * direction, residual - alpha * image, direction


def padded_2(x, sides, width):
    for axis, dim in sides:
        count, length = (lax.axis_size(axis), x.shape[dim])
        up = [(i, (i + 1) % count) for i in range(count - 1)]
        down = [(j, i) for i, j in up]
        last = lax.slice_in_dim(x, length - width, length, axis=dim)
        leading = lax.slice_in_dim(x, 0, width, axis=dim)
        before = lax.ppermute(last, axis, up)
        after = lax.ppermute(leading, axis, down)
        x = jnp.concatenate([before, x, after], axis=dim)
    return x


def banded(field, coeffs, axis, length):
    total = coeffs[0] * lax.slice_in_dim(field, 0, length, axis=axis)
    for offset in range(1, 7):
        total = total + coeffs[offset] * lax.slice_in_dim(field, offset, offset + length, axis=axis)
    return total


def apply_padded(padded, length_x, length_y):
    length_z = padded.shape[2]
    along_z = jnp.pad(padded, ((0, 0), (0, 0), (3, 3)))
    mass_z = banded(along_z, mass_band, 2, length_z)
    stiff_z = banded(along_z, stiff_band, 2, length_z)
    first = banded(mass_z, mass_band, 1, length_y)
    second = banded(mass_z, stiff_band, 1, length_y) + banded(stiff_z, mass_band, 1, length_y)
    return banded(first, stiff_band, 0, length_x) + banded(second, mass_band, 0, length_x)


def contract_first(left, right):
    return lax.dot_general(left, right, (((0,), (0,)), ((), ())), precision=highest)


def contract_last(left, right):
    return lax.dot_general(left, right, (((1,), (1,)), ((), ())), precision=highest)


def general(
    solution,
    residual,
    direction,
    previous_product,
    basis_x,
    basis_y,
    basis_z,
    eigen_x,
    eigen_y,
    eigen_z,
):
    whole_x = lax.all_gather(basis_x, "wide", axis=0, tiled=True)
    whole_y, whole_z = (
        lax.all_gather(basis_y, "narrow", axis=0, tiled=True),
        lax.all_gather(basis_z, "narrow", axis=0, tiled=True),
    )
    count_wide = lax.axis_size("wide")
    count_narrow = lax.axis_size("narrow")
    index_wide = lax.axis_index("wide")
    index_narrow = lax.axis_index("narrow")
    cells_x, cells_y, cells_z = residual.shape
    total_x = whole_x.shape[0]
    total_y = whole_y.shape[0]
    product_before = previous_product[0]
    spectral = jnp.dot(residual.reshape(cells_x * cells_y, cells_z), whole_z, precision=highest)
    flat = jnp.transpose(spectral.reshape(cells_x, cells_y, cells_z), (1, 2, 0)).reshape(
        cells_y, cells_z * cells_x
    )
    pencil = contract_first(
        whole_y, lax.all_to_all(flat, "narrow", split_axis=1, concat_axis=0, tiled=True)
    )
    rows_y = total_y // count_wide
    part_z = cells_z // count_narrow
    moved = lax.all_to_all(pencil, "wide", split_axis=0, concat_axis=1, tiled=True)
    lined = jnp.transpose(moved.reshape(rows_y, count_wide, part_z, cells_x), (0, 2, 1, 3))
    lined = lined.reshape(rows_y * part_z, total_x)
    spectral_x = jnp.dot(lined, whole_x, precision=highest)
    shift_y = lax.dynamic_slice_in_dim(eigen_y, index_wide * rows_y, rows_y)
    shift_z = lax.dynamic_slice_in_dim(eigen_z, index_narrow * part_z, part_z)
    shift_yz = (shift_y[:, None] + shift_z[None, :]).reshape(rows_y * part_z, 1)
    scaled = spectral_x / (eigen_x[None, :] + shift_yz)
    inverse_x = contract_last(scaled, whole_x)
    unlined = jnp.transpose(inverse_x.reshape(rows_y, part_z, count_wide, cells_x), (0, 2, 1, 3))
    unlined = unlined.reshape(rows_y, count_wide * part_z * cells_x)
    pencil = lax.all_to_all(unlined, "wide", split_axis=1, concat_axis=0, tiled=True)
    pencil = jnp.dot(whole_y, pencil, precision=highest)
    back = lax.all_to_all(pencil, "narrow", split_axis=0, concat_axis=1, tiled=True)
    brick = jnp.transpose(back.reshape(cells_y, cells_z, cells_x), (2, 0, 1))
    result = contract_last(brick.reshape(cells_x * cells_y, cells_z), whole_z)
    precond = result.reshape(cells_x, cells_y, cells_z)
    product_now = lax.psum(jnp.sum(residual * precond), ("wide", "narrow"))
    direction = precond + product_now / product_before * direction
    padded = padded_2(direction, (("wide", 0), ("narrow", 1)), 3)
    image = apply_padded(padded, cells_x, cells_y)
    curvature = lax.psum(jnp.sum(direction * image), ("wide", "narrow"))
    alpha = product_now / curvature
    solution = solution + alpha * direction
    residual = residual - alpha * image
    return (solution, residual, direction)


def per_device(*arrays):
    residual, basis_x, basis_y = arrays[1], arrays[4], arrays[5]
    wide, narrow = lax.axis_size("wide"), lax.axis_size("narrow")
    plan = Plan(*residual.shape, basis_x.shape[1], basis_y.shape[1], wide, narrow)
    if plan.fits:
        return by_pencils(plan, *arrays)
    return general(*arrays)


def solution(mesh):
    placed = (
        P("wide", "narrow", None),
        P("wide", "narrow", None),
        P("wide", "narrow", None),
        P(),
        P("wide", None),
        P("narrow", None),
        P("narrow", None),
        P(),
        P(),
        P(),
    )
    return jax.shard_map(
        per_device,
        mesh=mesh,
        in_specs=placed,
        out_specs=(P("wide", "narrow", None), P("wide", "narrow", None), P("wide", "narrow", None)),
        check_vma=False,
    )
```

```python
import functools

import jax
import jax.numpy as jnp
import ml_dtypes
import numpy as np
from jax import lax
from jax.experimental import pallas as pl
from jax.experimental.pallas import tpu as pltpu
from jax.sharding import PartitionSpec as P

mass_band = (
    1.0 / 5040.0,
    1.0 / 42.0,
    397.0 / 1680.0,
    151.0 / 315.0,
    397.0 / 1680.0,
    1.0 / 42.0,
    1.0 / 5040.0,
)
stiff_band = (-1.0 / 120.0, -0.2, -0.125, 2.0 / 3.0, -0.125, -0.2, -1.0 / 120.0)
highest = lax.Precision.HIGHEST
LANES = 128
HALO = 3
EDGE = 8
both = ("wide", "narrow")
MIB = 1024 * 1024


def split(x):
    high = x.astype(jnp.bfloat16)
    low = (x - high.astype(jnp.float32)).astype(jnp.bfloat16)
    return high, low


def dot3(left, right, over):
    dims = ((over[:1], over[1:]), ((), ()))
    one = functools.partial(
        lax.dot_general, dimension_numbers=dims, preferred_element_type=jnp.float32
    )
    return one(left[0], right[0]) + one(left[1], right[0]) + one(left[0], right[1])


class Plan:
    def __init__(self, cells_x, cells_y, cells_z, total_x, total_y, wide, narrow):
        self.cells_x, self.cells_y, self.cells_z = cells_x, cells_y, cells_z
        self.total_x, self.total_y = total_x, total_y
        self.wide, self.narrow, self.count = wide, narrow, wide * narrow
        self.rest = cells_y - LANES
        self.fits = (
            cells_z % self.count == 0
            and cells_x % 8 == 0
            and self.rest > 0
            and LANES % self.rest == 0
            and self.rest < LANES
            and total_y % LANES == LANES // 2
            and wide % 2 == 0
            and (total_x // 2) % 16 == 0
            and self.count % 8 == 0
        )
        if not self.fits:
            return
        self.share = cells_z // self.count
        self.group = LANES // self.rest
        self.tiles = cells_x // 8
        self.chunks = [(0, self.group), (self.group, self.share - self.group)]
        self.fits = (
            self.group % 2 == 0
            and self.share % 2 == 0
            and self.share > self.group
            and self.share % self.group != 0
            and self.tiles >= 3
            and 2 * LANES < cells_z <= 3 * LANES
        )

    def rows(self, chunk):
        start, size = self.chunks[chunk]
        return start * self.count, size * self.count

    def message(self, chunk):
        return (self.count, self.tiles, self.pieces(chunk), 8, LANES)

    def pieces(self, chunk):
        size = self.chunks[chunk][1]
        return size - (-size // self.group)


def forward_kernel(plan, size, field_ref, basis_ref, out_ref, high_ref, low_ref, stage_ref):

    @pl.when(pl.program_id(0) == 0)
    def _():
        high_ref[...], low_ref[...] = split(basis_ref[...])

    basis = (high_ref[...], low_ref[...])
    for i in range(8):
        stage_ref[i] = dot3(basis, split(field_ref[i]), (1, 1))
    rests = []
    for j in range(size):
        at = j * plan.count
        turned = jnp.swapaxes(stage_ref[:, at : at + plan.count, :], 0, 1)
        out_ref[:, 0, j] = turned[:, :, :LANES]
        rests.append(turned[:, :, LANES:])
    for piece, first in enumerate(range(0, size, plan.group)):
        some = rests[first : first + plan.group]
        some += [jnp.zeros_like(some[0])] * (plan.group - len(some))
        out_ref[:, 0, size + piece] = jnp.concatenate(some, axis=2)


def forward_z(plan, chunk, field, basis):
    start, rows = plan.rows(chunk)
    basis = basis[start : start + rows]
    message = plan.message(chunk)
    return pl.pallas_call(
        functools.partial(forward_kernel, plan, plan.chunks[chunk][1]),
        grid=(plan.tiles,),
        in_specs=[
            pl.BlockSpec((8, plan.cells_y, plan.cells_z), lambda t: (t, 0, 0)),
            pl.BlockSpec(basis.shape, lambda t: (0, 0)),
        ],
        out_specs=pl.BlockSpec((message[0], 1) + message[2:], lambda t: (0, t, 0, 0, 0)),
        out_shape=jax.ShapeDtypeStruct(message, jnp.float32),
        scratch_shapes=[
            pltpu.VMEM(basis.shape, jnp.bfloat16),
            pltpu.VMEM(basis.shape, jnp.bfloat16),
            pltpu.VMEM((8, rows, plan.cells_y), jnp.float32),
        ],
        compiler_params=pltpu.CompilerParams(vmem_limit_bytes=24 * MIB),
        cost_estimate=pl.CostEstimate(
            flops=6 * field.size * rows, bytes_accessed=8 * field.size, transcendentals=0
        ),
        name="forward_z",
    )(field, basis)


def add_chunk(plan, size, part, stage_ref):
    for j in range(size):
        at, q = j * plan.count, j % plan.group
        stage_ref[:, at : at + plan.count, :LANES] = jnp.swapaxes(part[:, 0, j], 0, 1)
        stage_ref[:, at : at + plan.count, LANES:] = jnp.swapaxes(
            part[:, 0, size + j // plan.group, :, q * plan.rest : (q + 1) * plan.rest], 0, 1
        )


def base_kernel(plan, size, part_ref, basis_ref, out_ref, high_ref, low_ref, stage_ref):
    @pl.when(pl.program_id(0) == 0)
    def _():
        high_ref[...], low_ref[...] = split(basis_ref[...])

    add_chunk(plan, size, part_ref, stage_ref)
    basis = (high_ref[...], low_ref[...])
    for i in range(8):
        out_ref[i] = dot3(split(stage_ref[i].T), basis, (1, 0))


def final_kernel(plan, size, ends, part_ref, basis_ref, base_ref, old_ref, before_ref, *refs):
    if ends:
        out_ref, now_ref, high_ref, low_ref, stage_ref = refs
    else:
        done_ref, out_ref, high_ref, low_ref, stage_ref = refs
    step = pl.program_id(0)

    @pl.when(step == 0)
    def _():
        high_ref[...], low_ref[...] = split(basis_ref[...])

    def work():
        add_chunk(plan, size, part_ref, stage_ref)
        sums = part_ref[:, 0, part_ref.shape[2] - 1, 0, LANES - 1 :]
        now = jnp.sum(sums, axis=0, keepdims=True)
        beta = now / before_ref[...]
        basis = (high_ref[...], low_ref[...])
        for i in range(8):
            value = dot3(split(stage_ref[i].T), basis, (1, 0))
            out_ref[i] = base_ref[i] + value + beta * old_ref[i]
        if ends:
            now_ref[...] = jnp.broadcast_to(now, now_ref.shape)

    if ends:
        work()
    else:
        inner = (step > 0) & (step < plan.tiles - 1)
        pl.when(inner)(work)

        @pl.when(jnp.logical_not(inner))
        def _():
            out_ref[...] = done_ref[...]


def inverse_scratch(plan, basis):
    return [
        pltpu.VMEM(basis.shape, jnp.bfloat16),
        pltpu.VMEM(basis.shape, jnp.bfloat16),
        pltpu.VMEM((8, basis.shape[0], plan.cells_y), jnp.float32),
    ]


def inverse_cost(plan, basis, tiles):
    size = tiles * 8 * plan.cells_y * plan.cells_z
    return pl.CostEstimate(
        flops=6 * size * basis.shape[0], bytes_accessed=12 * size, transcendentals=0
    )


def inverse_base(plan, chunk, part, basis):
    start, rows = plan.rows(chunk)
    basis = basis[start : start + rows]
    return pl.pallas_call(
        functools.partial(base_kernel, plan, plan.chunks[chunk][1]),
        grid=(plan.tiles,),
        in_specs=[
            pl.BlockSpec((part.shape[0], 1) + part.shape[2:], lambda t: (0, t, 0, 0, 0)),
            pl.BlockSpec(basis.shape, lambda t: (0, 0)),
        ],
        out_specs=pl.BlockSpec((8, plan.cells_y, plan.cells_z), lambda t: (t, 0, 0)),
        out_shape=jax.ShapeDtypeStruct((plan.cells_x, plan.cells_y, plan.cells_z), jnp.float32),
        scratch_shapes=inverse_scratch(plan, basis),
        compiler_params=pltpu.CompilerParams(vmem_limit_bytes=24 * MIB),
        cost_estimate=inverse_cost(plan, basis, plan.tiles),
        name="inverse_base",
    )(part, basis)


def inverse_final(plan, chunk, part, basis, base, old, before, done=None):
    ends = done is None
    start, rows = plan.rows(chunk)
    basis = basis[start : start + rows]
    last = plan.tiles - 1
    if ends:
        pick = lambda t: t * last
    else:
        pick = lambda t: jnp.clip(t, 1, last - 1)
    tile = (8, plan.cells_y, plan.cells_z)
    brick = pl.BlockSpec(tile, lambda t: (pick(t), 0, 0))
    in_specs = [
        pl.BlockSpec((part.shape[0], 1) + part.shape[2:], lambda t: (0, pick(t), 0, 0, 0)),
        pl.BlockSpec(basis.shape, lambda t: (0, 0)),
        brick,
        brick,
        pl.BlockSpec((1, 1), lambda t: (0, 0)),
    ]
    operands = [part, basis, base, old, before.reshape(1, 1)]
    out_specs = pl.BlockSpec(tile, lambda t: (t, 0, 0))
    if ends:
        out_specs = [out_specs, pl.BlockSpec((8, LANES), lambda t: (0, 0))]
        out_shape = [
            jax.ShapeDtypeStruct((16,) + base.shape[1:], jnp.float32),
            jax.ShapeDtypeStruct((8, LANES), jnp.float32),
        ]
    else:
        in_specs.append(pl.BlockSpec(tile, lambda t: (t // last, 0, 0)))
        operands.append(done)
        out_shape = jax.ShapeDtypeStruct(base.shape, jnp.float32)
    return pl.pallas_call(
        functools.partial(final_kernel, plan, plan.chunks[chunk][1], ends),
        grid=(2 if ends else plan.tiles,),
        in_specs=in_specs,
        out_specs=out_specs,
        out_shape=out_shape,
        scratch_shapes=inverse_scratch(plan, basis),
        compiler_params=pltpu.CompilerParams(vmem_limit_bytes=28 * MIB),
        cost_estimate=inverse_cost(plan, basis, 2 if ends else plan.tiles - 2),
        name="inverse_ends" if ends else "inverse_inner",
    )(*operands)


def middle_kernel(plan, chunk, *refs):
    (
        in_ref,
        basis_x_ref,
        turned_x_ref,
        main_y_ref,
        rest_y_ref,
        eigen_x_ref,
        shift_ref,
        total_ref,
        out_ref,
        sum_ref,
        bx_high,
        bx_low,
        tx_high,
        tx_low,
        my_high,
        my_low,
        ry_high,
        ry_low,
        u_high,
        u_low,
        q_high,
        q_low,
        rest_acc,
    ) = refs
    size = plan.chunks[chunk][1]
    last = chunk == len(plan.chunks) - 1
    wide, narrow, tiles = plan.wide, plan.narrow, plan.tiles
    half = plan.total_x // 2
    lump = wide // 2
    span = plan.total_y + LANES // 2
    width = 2 * plan.total_y
    bx_high[...], bx_low[...] = split(basis_x_ref[...])
    tx_high[...], tx_low[...] = split(turned_x_ref[...])
    my_high[...], my_low[...] = split(main_y_ref[...])
    ry_high[...], ry_low[...] = split(rest_y_ref[...])
    rest_acc[...] = jnp.zeros_like(rest_acc)

    def gathered(piece, h):
        rows = pl.ds(h * lump, lump)
        return jnp.concatenate(
            [in_ref[rows, n, :, piece].reshape(half, LANES) for n in range(narrow)], axis=1
        )

    def pair(p, total):
        for h in range(2):
            rest = split(gathered(size + 2 * p // plan.group, h))
            parts = []
            for s in range(2):
                j = 2 * p + s
                q = lax.rem(j, plan.group)
                parts.append(
                    dot3(split(gathered(j, h)), (my_high[s], my_low[s]), (1, 0))
                    + dot3(rest, (ry_high[q], ry_low[q]), (1, 0))
                )
            cut = span - LANES
            joined = jnp.concatenate(
                [
                    parts[0][:, :cut],
                    parts[0][:, cut:] + parts[1][:, :LANES],
                    parts[1][:, LANES:],
                ],
                axis=1,
            )
            rows = pl.ds(h * half, half)
            u_high[rows, :], u_low[rows, :] = split(joined)
        shift = shift_ref[p]
        for h in range(2):
            rows = pl.ds(h * half, half)
            spectral = dot3(
                (tx_high[rows, :], tx_low[rows, :]), (u_high[...], u_low[...]), (1, 0)
            )
            scaled = spectral / (eigen_x_ref[rows, :] + shift)
            total = total + jnp.sum((spectral * scaled).reshape(half // 8, 8, width), axis=0)
            q_high[rows, :], q_low[rows, :] = split(scaled)
        for h in range(2):
            rows = pl.ds(h * half, half)
            value = dot3((bx_high[rows, :], bx_low[rows, :]), (q_high[...], q_low[...]), (1, 0))
            for s in range(2):
                j = 2 * p + s
                mine = split(value[:, s * (width - span) : s * (width - span) + span])
                main = dot3(mine, (my_high[s], my_low[s]), (1, 1))
                q = lax.rem(j, plan.group)
                rest_acc[2 * p // plan.group, rows, :] += dot3(
                    mine, (ry_high[q], ry_low[q]), (1, 1)
                )
                for n in range(narrow):
                    out_ref[pl.ds(h * lump, lump), n, :, j] = main[
                        :, n * LANES : (n + 1) * LANES
                    ].reshape(lump, tiles, 8, LANES)
        return total

    total = lax.fori_loop(0, size // 2, pair, jnp.zeros((8, width), jnp.float32))
    value = total_ref[...] + jnp.sum(total)
    sum_ref[...] = value
    pieces = in_ref.shape[3] - size
    for piece in range(pieces):
        for n in range(narrow):
            rest = rest_acc[piece, :, n * LANES : (n + 1) * LANES]
            if last and piece == pieces - 1:
                lane = lax.broadcasted_iota(jnp.int32, rest.shape, 1)
                rest = jnp.where(lane == LANES - 1, value[:1, :], rest)
            out_ref[:, n, :, size + piece] = rest.reshape(wide, tiles, 8, LANES)


def middle(plan, chunk, message, basis_x, turned_x, main_y, rest_y, eigen_x, shift, total):
    size = plan.chunks[chunk][1]
    shape = (plan.wide, plan.narrow) + message.shape[1:]
    square = (plan.total_x, plan.total_x)
    pencil = (plan.total_x, 2 * plan.total_y)
    half = jnp.bfloat16
    out, total = pl.pallas_call(
        functools.partial(middle_kernel, plan, chunk),
        out_shape=[
            jax.ShapeDtypeStruct(shape, jnp.float32),
            jax.ShapeDtypeStruct((8, LANES), jnp.float32),
        ],
        in_specs=[pl.BlockSpec(memory_space=pltpu.VMEM)] * 8,
        out_specs=[pl.BlockSpec(memory_space=pltpu.VMEM)] * 2,
        scratch_shapes=[
            pltpu.VMEM(square, half),
            pltpu.VMEM(square, half),
            pltpu.VMEM(square, half),
            pltpu.VMEM(square, half),
            pltpu.VMEM(main_y.shape, half),
            pltpu.VMEM(main_y.shape, half),
            pltpu.VMEM(rest_y.shape, half),
            pltpu.VMEM(rest_y.shape, half),
            pltpu.VMEM(pencil, half),
            pltpu.VMEM(pencil, half),
            pltpu.VMEM(pencil, half),
            pltpu.VMEM(pencil, half),
            pltpu.VMEM((plan.pieces(chunk) - size, plan.total_x, plan.narrow * LANES), jnp.float32),
        ],
        compiler_params=pltpu.CompilerParams(vmem_limit_bytes=44 * MIB),
        cost_estimate=pl.CostEstimate(
            flops=12 * size * plan.total_x * plan.total_y * (plan.total_x + plan.total_y),
            bytes_accessed=8 * message.size,
            transcendentals=0,
        ),
        name="middle",
    )(message.reshape(shape), basis_x, turned_x, main_y, rest_y, eigen_x, shift, total)
    return out.reshape(message.shape), total


def shifted(x, step, axis):
    count = lax.axis_size(axis)
    pairs = [(i + step, i) for i in range(count) if 0 <= i + step < count]
    return lax.ppermute(x, axis, pairs)


def from_sides(low, high, axis):
    if lax.axis_size(axis) != 2:
        return shifted(high, -1, axis), shifted(low, 1, axis)
    second = lax.axis_index(axis) == 1
    got = lax.ppermute(jnp.where(second, low, high), axis, [(0, 1), (1, 0)])
    return jnp.where(second, got, 0.0), jnp.where(second, 0.0, got)


mass_scale, stiff_scale = 5040.0, 120.0
CUT = LANES + LANES // 2
GROUP = 4


def band_matrices(cells_z):
    offset = np.arange(cells_z)[:, None] - np.arange(cells_z)[None, :]
    near = np.abs(offset) <= HALO
    tables = []
    for band, scale in ((mass_band, mass_scale), (stiff_band, stiff_scale)):
        whole = np.rint(np.asarray(band) * scale)
        full = np.where(near, whole[np.clip(offset + HALO, 0, 2 * HALO)], 0.0)
        first = np.zeros((2 * LANES, 2 * LANES))
        first[:, :CUT] = full[: 2 * LANES, :CUT]
        second = np.zeros((2 * LANES, 2 * LANES))
        second[: cells_z - LANES, CUT - LANES : cells_z - LANES] = full[LANES:, CUT:]
        tables.append(np.stack([first, second]).astype(np.float32))
    mass, stiff = tables
    high = mass.astype(ml_dtypes.bfloat16)
    low = (mass - high.astype(np.float32)).astype(ml_dtypes.bfloat16)
    return np.stack([high, low, stiff.astype(ml_dtypes.bfloat16)])


def stencil_kernel(plan, *refs):
    pieces = refs[:5]
    bands_ref, image_ref, sum_ref, field, f_high, f_low, s_high, s_low, h_a, h_b, total, sems = refs[5:]
    cells_x, cells_y, cells_z = plan.cells_x, plan.cells_y, plan.cells_z
    padded_y = cells_y + 2 * EDGE
    own_y = pl.ds(EDGE, cells_y)
    places = (
        (pl.ds(HALO, cells_x), own_y),
        (pl.ds(0, HALO), own_y),
        (pl.ds(HALO + cells_x, HALO), own_y),
        (pl.ds(0, cells_x + 2 * HALO), pl.ds(0, EDGE)),
        (pl.ds(0, cells_x + 2 * HALO), pl.ds(EDGE + cells_y, EDGE)),
    )
    step = pl.program_id(0)

    @pl.when(step == 0)
    def _():
        copies = [
            pltpu.make_async_copy(piece, field.at[xs, ys, :], sems.at[i])
            for i, (piece, (xs, ys)) in enumerate(zip(pieces, places))
        ]
        for copy in copies:
            copy.start()
        total[...] = jnp.zeros_like(total)
        for copy in copies:
            copy.wait()

    blocks = h_a.shape[0]
    ratio = stiff_scale / mass_scale

    def one(left, right):
        return lax.dot_general(
            left, right, (((1,), (0,)), ((), ())), preferred_element_type=jnp.float32
        )

    def planes(g, carry):
        for i in range(GROUP):
            x = step * 8 + g * GROUP + i
            middle_plane = field[x + HALO]
            first = ratio * stiff_band[HALO] * middle_plane
            second = mass_band[HALO] * middle_plane
            for o in range(1, HALO + 1):
                around = field[x + HALO - o] + field[x + HALO + o]
                first = first + ratio * stiff_band[HALO + o] * around
                second = second + mass_band[HALO + o] * around
            rows = pl.ds(i * padded_y, padded_y)
            f_high[rows, :], f_low[rows, :] = split(first)
            s_high[rows, :], s_low[rows, :] = split(second)
        window_a, window_b = [], []
        for w, lanes in enumerate((pl.ds(0, 2 * LANES), pl.ds(LANES, cells_z - LANES))):
            high, low, stiff = (bands_ref[k, w, : lanes.size, :] for k in range(3))
            fh, fl, sh, sl = (ref[:, lanes] for ref in (f_high, f_low, s_high, s_low))
            window_a.append(
                one(fh, high) + one(fl, high) + one(fh, low) + one(sh, stiff) + one(sl, stiff)
            )
            window_b.append(one(sh, high) + one(sl, high) + one(sh, low))
        for ref, (left, right) in ((h_a, window_a), (h_b, window_b)):
            ref[0] = left[:, :LANES]
            ref[1] = left[:, LANES:] + right[:, :LANES]
            ref[2] = right[:, LANES:]
        for i in range(GROUP):
            plane = g * GROUP + i
            for k in range(blocks):
                lanes = min(LANES, cells_z - k * LANES)
                at = lambda ref, o: ref[k, pl.ds(i * padded_y + EDGE + o, cells_y), :]
                image = (mass_band[HALO] / stiff_scale) * at(h_a, 0)
                image = image + (stiff_band[HALO] / mass_scale) * at(h_b, 0)
                for o in range(1, HALO + 1):
                    image = image + (mass_band[HALO + o] / stiff_scale) * (at(h_a, -o) + at(h_a, o))
                    image = image + (stiff_band[HALO + o] / mass_scale) * (at(h_b, -o) + at(h_b, o))
                here = pl.ds(k * LANES, lanes)
                image_ref[plane, :, here] = image[:, :lanes]
                product = image[:, :lanes] * field[step * 8 + plane + HALO, own_y, here]
                total[:, here] += jnp.sum(product.reshape(cells_y // 8, 8, lanes), axis=0)
        return carry

    lax.fori_loop(0, 8 // GROUP, planes, 0)

    @pl.when(step == pl.num_programs(0) - 1)
    def _():
        sum_ref[...] = jnp.full(sum_ref.shape, jnp.sum(total[...]), jnp.float32)


def stencil(plan, direction, before_x, after_x):
    cells_x, cells_y, cells_z = direction.shape

    def strip(rows):
        return jnp.concatenate([before_x[:, rows], direction[:, rows], after_x[:, rows]], axis=0)

    before_y, after_y = from_sides(
        strip(slice(0, EDGE)), strip(slice(cells_y - EDGE, cells_y)), "narrow"
    )
    bands = band_matrices(cells_z)
    padded_y = cells_y + 2 * EDGE
    blocks = -(-cells_z // LANES)
    lump = (GROUP * padded_y, cells_z)
    return pl.pallas_call(
        functools.partial(stencil_kernel, plan),
        grid=(cells_x // 8,),
        in_specs=[pl.BlockSpec(memory_space=pl.ANY)] * 5
        + [pl.BlockSpec(bands.shape, lambda t: (0, 0, 0, 0))],
        out_specs=[
            pl.BlockSpec((8, cells_y, cells_z), lambda t: (t, 0, 0)),
            pl.BlockSpec((8, LANES), lambda t: (0, 0)),
        ],
        out_shape=[
            jax.ShapeDtypeStruct(direction.shape, jnp.float32),
            jax.ShapeDtypeStruct((8, LANES), jnp.float32),
        ],
        scratch_shapes=[
            pltpu.VMEM((cells_x + 2 * HALO, padded_y, cells_z), jnp.float32),
            pltpu.VMEM(lump, jnp.bfloat16),
            pltpu.VMEM(lump, jnp.bfloat16),
            pltpu.VMEM(lump, jnp.bfloat16),
            pltpu.VMEM(lump, jnp.bfloat16),
            pltpu.VMEM((blocks, GROUP * padded_y, LANES), jnp.float32),
            pltpu.VMEM((blocks, GROUP * padded_y, LANES), jnp.float32),
            pltpu.VMEM((8, cells_z), jnp.float32),
            pltpu.SemaphoreType.DMA((5,)),
        ],
        compiler_params=pltpu.CompilerParams(vmem_limit_bytes=36 * MIB),
        cost_estimate=pl.CostEstimate(
            flops=8 * direction.size * cells_z, bytes_accessed=8 * direction.size, transcendentals=0
        ),
        name="stencil",
    )(direction, before_x, after_x, before_y, after_y, bands)


def scatter(x):
    return lax.all_to_all(x, both, split_axis=0, concat_axis=0, tiled=True)


def dealt(plan, whole_z):
    columns = whole_z.T.reshape(plan.count, plan.share, plan.cells_z)
    return jnp.swapaxes(columns, 0, 1).reshape(plan.cells_z, plan.cells_z)


def basis_y_blocks(plan, whole_y):
    by_owner = whole_y.reshape(plan.narrow, plan.cells_y, plan.total_y)
    main = by_owner[:, :LANES].reshape(plan.narrow * LANES, plan.total_y)
    rest = by_owner[:, LANES:]
    half = LANES // 2
    sides = [(0, half), (half, 0)]
    mains = jnp.stack([jnp.pad(main, ((0, 0), s)) for s in sides])
    rests = []
    for q in range(plan.group):
        after = LANES - (q + 1) * plan.rest
        padded = jnp.pad(rest, ((0, 0), (q * plan.rest, after), sides[q % 2]))
        rests.append(padded.reshape(plan.narrow * LANES, plan.total_y + half))
    return mains, jnp.stack(rests)


def by_pencils(
    plan,
    solution,
    residual,
    direction,
    previous_product,
    basis_x,
    basis_y,
    basis_z,
    eigen_x,
    eigen_y,
    eigen_z,
):
    whole_z = lax.all_gather(basis_z, "narrow", axis=0, tiled=True)
    turned_z = dealt(plan, whole_z)
    whole_y = lax.all_gather(basis_y, "narrow", axis=0, tiled=True)
    whole_x = lax.all_gather(basis_x, "wide", axis=0, tiled=True)
    sent = [forward_z(plan, k, residual, turned_z) for k in range(2)]
    arrived = [scatter(sent[0])]
    later, whole_x, whole_y = lax.optimization_barrier((sent[1], whole_x, whole_y))
    arrived.append(scatter(later))
    main_y, rest_y = basis_y_blocks(plan, whole_y)
    turned_x = whole_x.T
    index = lax.axis_index("wide") * plan.narrow + lax.axis_index("narrow")
    mine_z = lax.dynamic_slice_in_dim(eigen_z, index * plan.share, plan.share)
    shifts = (mine_z[:, None] + eigen_y[None, :]).reshape(plan.share // 2, 1, 2 * plan.total_y)
    total = jnp.zeros((8, LANES), jnp.float32)
    returned = []
    for k, (start, size) in enumerate(plan.chunks):
        shift = shifts[start // 2 : (start + size) // 2]
        back, total = middle(
            plan,
            k,
            arrived[k],
            whole_x,
            turned_x,
            main_y,
            rest_y,
            eigen_x.reshape(-1, 1),
            shift,
            total,
        )
        returned.append(scatter(back))
    base = inverse_base(plan, 0, returned[0], turned_z)
    inverse = functools.partial(
        inverse_final, plan, 1, returned[1], turned_z, base, direction, previous_product
    )
    ends, now = inverse()
    before_x = shifted(ends[16 - HALO :], -1, "wide")
    after_x = shifted(ends[:HALO], 1, "wide")
    direction = inverse(ends)
    image, part = stencil(plan, direction, before_x, after_x)
    parts = scatter(jnp.broadcast_to(part[None], (plan.count,) + part.shape))
    alpha = now[0, 0] / jnp.sum(parts[:, 0, 0])
    return solution + alpha * direction, residual - alpha * image, direction


def padded_2(x, sides, width):
    for axis, dim in sides:
        count, length = (lax.axis_size(axis), x.shape[dim])
        up = [(i, (i + 1) % count) for i in range(count - 1)]
        down = [(j, i) for i, j in up]
        last = lax.slice_in_dim(x, length - width, length, axis=dim)
        leading = lax.slice_in_dim(x, 0, width, axis=dim)
        before = lax.ppermute(last, axis, up)
        after = lax.ppermute(leading, axis, down)
        x = jnp.concatenate([before, x, after], axis=dim)
    return x


def banded(field, coeffs, axis, length):
    total = coeffs[0] * lax.slice_in_dim(field, 0, length, axis=axis)
    for offset in range(1, 7):
        total = total + coeffs[offset] * lax.slice_in_dim(field, offset, offset + length, axis=axis)
    return total


def apply_padded(padded, length_x, length_y):
    length_z = padded.shape[2]
    along_z = jnp.pad(padded, ((0, 0), (0, 0), (3, 3)))
    mass_z = banded(along_z, mass_band, 2, length_z)
    stiff_z = banded(along_z, stiff_band, 2, length_z)
    first = banded(mass_z, mass_band, 1, length_y)
    second = banded(mass_z, stiff_band, 1, length_y) + banded(stiff_z, mass_band, 1, length_y)
    return banded(first, stiff_band, 0, length_x) + banded(second, mass_band, 0, length_x)


def contract_first(left, right):
    return lax.dot_general(left, right, (((0,), (0,)), ((), ())), precision=highest)


def contract_last(left, right):
    return lax.dot_general(left, right, (((1,), (1,)), ((), ())), precision=highest)


def general(
    solution,
    residual,
    direction,
    previous_product,
    basis_x,
    basis_y,
    basis_z,
    eigen_x,
    eigen_y,
    eigen_z,
):
    whole_x = lax.all_gather(basis_x, "wide", axis=0, tiled=True)
    whole_y, whole_z = (
        lax.all_gather(basis_y, "narrow", axis=0, tiled=True),
        lax.all_gather(basis_z, "narrow", axis=0, tiled=True),
    )
    count_wide = lax.axis_size("wide")
    count_narrow = lax.axis_size("narrow")
    index_wide = lax.axis_index("wide")
    index_narrow = lax.axis_index("narrow")
    cells_x, cells_y, cells_z = residual.shape
    total_x = whole_x.shape[0]
    total_y = whole_y.shape[0]
    product_before = previous_product[0]
    spectral = jnp.dot(residual.reshape(cells_x * cells_y, cells_z), whole_z, precision=highest)
    flat = jnp.transpose(spectral.reshape(cells_x, cells_y, cells_z), (1, 2, 0)).reshape(
        cells_y, cells_z * cells_x
    )
    pencil = contract_first(
        whole_y, lax.all_to_all(flat, "narrow", split_axis=1, concat_axis=0, tiled=True)
    )
    rows_y = total_y // count_wide
    part_z = cells_z // count_narrow
    moved = lax.all_to_all(pencil, "wide", split_axis=0, concat_axis=1, tiled=True)
    lined = jnp.transpose(moved.reshape(rows_y, count_wide, part_z, cells_x), (0, 2, 1, 3))
    lined = lined.reshape(rows_y * part_z, total_x)
    spectral_x = jnp.dot(lined, whole_x, precision=highest)
    shift_y = lax.dynamic_slice_in_dim(eigen_y, index_wide * rows_y, rows_y)
    shift_z = lax.dynamic_slice_in_dim(eigen_z, index_narrow * part_z, part_z)
    shift_yz = (shift_y[:, None] + shift_z[None, :]).reshape(rows_y * part_z, 1)
    scaled = spectral_x / (eigen_x[None, :] + shift_yz)
    inverse_x = contract_last(scaled, whole_x)
    unlined = jnp.transpose(inverse_x.reshape(rows_y, part_z, count_wide, cells_x), (0, 2, 1, 3))
    unlined = unlined.reshape(rows_y, count_wide * part_z * cells_x)
    pencil = lax.all_to_all(unlined, "wide", split_axis=1, concat_axis=0, tiled=True)
    pencil = jnp.dot(whole_y, pencil, precision=highest)
    back = lax.all_to_all(pencil, "narrow", split_axis=0, concat_axis=1, tiled=True)
    brick = jnp.transpose(back.reshape(cells_y, cells_z, cells_x), (2, 0, 1))
    result = contract_last(brick.reshape(cells_x * cells_y, cells_z), whole_z)
    precond = result.reshape(cells_x, cells_y, cells_z)
    product_now = lax.psum(jnp.sum(residual * precond), ("wide", "narrow"))
    direction = precond + product_now / product_before * direction
    padded = padded_2(direction, (("wide", 0), ("narrow", 1)), 3)
    image = apply_padded(padded, cells_x, cells_y)
    curvature = lax.psum(jnp.sum(direction * image), ("wide", "narrow"))
    alpha = product_now / curvature
    solution = solution + alpha * direction
    residual = residual - alpha * image
    return (solution, residual, direction)


def per_device(*arrays):
    residual, basis_x, basis_y = arrays[1], arrays[4], arrays[5]
    wide, narrow = lax.axis_size("wide"), lax.axis_size("narrow")
    plan = Plan(*residual.shape, basis_x.shape[1], basis_y.shape[1], wide, narrow)
    if plan.fits:
        return by_pencils(plan, *arrays)
    return general(*arrays)


def solution(mesh):
    placed = (
        P("wide", "narrow", None),
        P("wide", "narrow", None),
        P("wide", "narrow", None),
        P(),
        P("wide", None),
        P("narrow", None),
        P("narrow", None),
        P(),
        P(),
        P(),
    )
    return jax.shard_map(
        per_device,
        mesh=mesh,
        in_specs=placed,
        out_specs=(P("wide", "narrow", None), P("wide", "narrow", None), P("wide", "narrow", None)),
        check_vma=False,
    )
```

```python
import functools

import jax
import jax.numpy as jnp
import ml_dtypes
import numpy as np
from jax import lax
from jax.experimental import pallas as pl
from jax.experimental.pallas import tpu as pltpu
from jax.sharding import PartitionSpec as P

mass_band = (
    1.0 / 5040.0,
    1.0 / 42.0,
    397.0 / 1680.0,
    151.0 / 315.0,
    397.0 / 1680.0,
    1.0 / 42.0,
    1.0 / 5040.0,
)
stiff_band = (-1.0 / 120.0, -0.2, -0.125, 2.0 / 3.0, -0.125, -0.2, -1.0 / 120.0)
highest = lax.Precision.HIGHEST
LANES = 128
HALO = 3
EDGE = 8
both = ("wide", "narrow")
MIB = 1024 * 1024


def split(x):
    high = x.astype(jnp.bfloat16)
    low = (x - high.astype(jnp.float32)).astype(jnp.bfloat16)
    return high, low


def dot3(left, right, over):
    dims = ((over[:1], over[1:]), ((), ()))
    one = functools.partial(
        lax.dot_general, dimension_numbers=dims, preferred_element_type=jnp.float32
    )
    return one(left[0], right[0]) + one(left[1], right[0]) + one(left[0], right[1])


class Plan:
    def __init__(self, cells_x, cells_y, cells_z, total_x, total_y, wide, narrow):
        self.cells_x, self.cells_y, self.cells_z = cells_x, cells_y, cells_z
        self.total_x, self.total_y = total_x, total_y
        self.wide, self.narrow, self.count = wide, narrow, wide * narrow
        self.rest = cells_y - LANES
        self.fits = (
            cells_z % self.count == 0
            and cells_x % 8 == 0
            and self.rest > 0
            and LANES % self.rest == 0
            and self.rest < LANES
            and total_y % LANES == LANES // 2
            and wide % 2 == 0
            and (total_x // 2) % 16 == 0
            and self.count % 8 == 0
        )
        if not self.fits:
            return
        self.share = cells_z // self.count
        self.group = LANES // self.rest
        self.tiles = cells_x // 8
        self.chunks = [(0, self.group), (self.group, self.share - self.group)]
        self.fits = (
            self.group % 2 == 0
            and self.share % 2 == 0
            and self.share > self.group
            and self.share % self.group != 0
            and self.tiles >= 3
            and 2 * LANES < cells_z <= 3 * LANES
        )
        if self.fits:
            _, _, _, _, fit, width = self.shape_of(1)
            self.fits = self.tiles % fit != 0 or fit * width < LANES

    def rows(self, chunk):
        start, size = self.chunks[chunk]
        return start * self.count, size * self.count

    def shape_of(self, chunk):
        size = self.chunks[chunk][1]
        part = size % self.group
        width = part * self.rest
        fit = LANES // width if part else 1
        tails = -(-self.tiles // fit) if part else 0
        return size, size + size // self.group, part, tails, fit, width

    def message(self, chunk):
        _, per, _, tails, _, _ = self.shape_of(chunk)
        return (self.count, self.tiles * per + tails, 8, LANES)


def forward_kernel(plan, chunk, field_ref, basis_ref, out_ref, high_ref, low_ref, stage_ref):
    size, per, part, tails, fit, width = plan.shape_of(chunk)
    step = pl.program_id(0)

    @pl.when(step == 0)
    def _():
        high_ref[...], low_ref[...] = split(basis_ref[...])
        if tails:
            out_ref[:, plan.tiles * per :] = jnp.zeros((plan.count, tails, 8, LANES), jnp.float32)

    basis = (high_ref[...], low_ref[...])
    for i in range(8):
        stage_ref[i] = dot3(basis, split(field_ref[i]), (1, 1))
    base = step * per if tails else 0
    rests = []
    for j in range(size):
        at = j * plan.count
        turned = jnp.swapaxes(stage_ref[:, at : at + plan.count, :], 0, 1)
        out_ref[:, base + j] = turned[:, :, :LANES]
        rests.append(turned[:, :, LANES:])
    for piece in range(size // plan.group):
        some = rests[piece * plan.group : (piece + 1) * plan.group]
        out_ref[:, base + size + piece] = jnp.concatenate(some, axis=2)
    if tails:
        some = jnp.concatenate(rests[size - part :], axis=2)
        for place in range(fit):

            @pl.when(step % fit == place)
            def _():
                lanes = slice(place * width, (place + 1) * width)
                out_ref[:, plan.tiles * per + step // fit, :, lanes] = some


def forward_z(plan, chunk, field, basis):
    start, rows = plan.rows(chunk)
    basis = basis[start : start + rows]
    message = plan.message(chunk)
    _, per, _, tails, _, _ = plan.shape_of(chunk)
    if tails:
        out_spec = pl.BlockSpec(message, lambda t: (0, 0, 0, 0))
    else:
        out_spec = pl.BlockSpec((message[0], per) + message[2:], lambda t: (0, t, 0, 0))
    return pl.pallas_call(
        functools.partial(forward_kernel, plan, chunk),
        grid=(plan.tiles,),
        in_specs=[
            pl.BlockSpec((8, plan.cells_y, plan.cells_z), lambda t: (t, 0, 0)),
            pl.BlockSpec(basis.shape, lambda t: (0, 0)),
        ],
        out_specs=out_spec,
        out_shape=jax.ShapeDtypeStruct(message, jnp.float32),
        scratch_shapes=[
            pltpu.VMEM(basis.shape, jnp.bfloat16),
            pltpu.VMEM(basis.shape, jnp.bfloat16),
            pltpu.VMEM((8, rows, plan.cells_y), jnp.float32),
        ],
        compiler_params=pltpu.CompilerParams(vmem_limit_bytes=50 * MIB),
        cost_estimate=pl.CostEstimate(
            flops=6 * field.size * rows, bytes_accessed=8 * field.size, transcendentals=0
        ),
        name="forward_z",
    )(field, basis)


def add_chunk(plan, chunk, tile, part_ref, tail_ref, stage_ref):
    size, _, part, tails, fit, width = plan.shape_of(chunk)
    if tails:
        tail = tail_ref[:, 0]
        for place in range(1, fit):
            turned = pltpu.roll(tail_ref[:, 0], LANES - place * width, 2)
            tail = jnp.where(tile % fit == place, turned, tail)
    for j in range(size):
        at, q = j * plan.count, j % plan.group
        lanes = slice(q * plan.rest, (q + 1) * plan.rest)
        stage_ref[:, at : at + plan.count, :LANES] = jnp.swapaxes(part_ref[:, j], 0, 1)
        if j < size - part:
            rest = part_ref[:, size + j // plan.group, :, lanes]
        else:
            rest = tail[:, :, lanes]
        stage_ref[:, at : at + plan.count, LANES:] = jnp.swapaxes(rest, 0, 1)


def base_kernel(plan, chunk, part_ref, basis_ref, out_ref, high_ref, low_ref, stage_ref):
    step = pl.program_id(0)

    @pl.when(step == 0)
    def _():
        high_ref[...], low_ref[...] = split(basis_ref[...])

    add_chunk(plan, chunk, step, part_ref, None, stage_ref)
    basis = (high_ref[...], low_ref[...])
    for i in range(8):
        out_ref[i] = dot3(split(stage_ref[i].T), basis, (1, 0))


def final_kernel(plan, chunk, ends, pick, *refs):
    part_ref, tail_ref, last_ref, basis_ref, base_ref, old_ref, before_ref = refs[:7]
    if ends:
        out_ref, now_ref, high_ref, low_ref, stage_ref = refs[7:]
    else:
        done_ref, out_ref, high_ref, low_ref, stage_ref = refs[7:]
    step = pl.program_id(0)

    @pl.when(step == 0)
    def _():
        high_ref[...], low_ref[...] = split(basis_ref[...])

    def work():
        add_chunk(plan, chunk, pick(step), part_ref, tail_ref, stage_ref)
        now = jnp.sum(last_ref[:, 0, 0, LANES - 1 :], axis=0, keepdims=True)
        beta = now / before_ref[...]
        basis = (high_ref[...], low_ref[...])
        for i in range(8):
            value = dot3(split(stage_ref[i].T), basis, (1, 0))
            out_ref[i] = base_ref[i] + value + beta * old_ref[i]
        if ends:
            now_ref[...] = jnp.broadcast_to(now, now_ref.shape)

    if ends:
        work()
    else:
        inner = (step > 0) & (step < plan.tiles - 1)
        pl.when(inner)(work)

        @pl.when(jnp.logical_not(inner))
        def _():
            out_ref[...] = done_ref[...]


def inverse_scratch(plan, basis):
    return [
        pltpu.VMEM(basis.shape, jnp.bfloat16),
        pltpu.VMEM(basis.shape, jnp.bfloat16),
        pltpu.VMEM((8, basis.shape[0], plan.cells_y), jnp.float32),
    ]


def inverse_cost(plan, basis, tiles):
    size = tiles * 8 * plan.cells_y * plan.cells_z
    return pl.CostEstimate(
        flops=6 * size * basis.shape[0], bytes_accessed=12 * size, transcendentals=0
    )


def inverse_base(plan, chunk, part, basis):
    start, rows = plan.rows(chunk)
    per = plan.shape_of(chunk)[1]
    basis = basis[start : start + rows]
    return pl.pallas_call(
        functools.partial(base_kernel, plan, chunk),
        grid=(plan.tiles,),
        in_specs=[
            pl.BlockSpec((plan.count, per, 8, LANES), lambda t: (0, t, 0, 0)),
            pl.BlockSpec(basis.shape, lambda t: (0, 0)),
        ],
        out_specs=pl.BlockSpec((8, plan.cells_y, plan.cells_z), lambda t: (t, 0, 0)),
        out_shape=jax.ShapeDtypeStruct((plan.cells_x, plan.cells_y, plan.cells_z), jnp.float32),
        scratch_shapes=inverse_scratch(plan, basis),
        compiler_params=pltpu.CompilerParams(vmem_limit_bytes=50 * MIB),
        cost_estimate=inverse_cost(plan, basis, plan.tiles),
        name="inverse_base",
    )(part, basis)


def inverse_final(plan, chunk, part, basis, base, old, before, done=None):
    ends = done is None
    start, rows = plan.rows(chunk)
    basis = basis[start : start + rows]
    last = plan.tiles - 1
    if ends:
        pick = lambda t: t * last
    else:
        pick = lambda t: jnp.clip(t, 1, last - 1)
    tile = (8, plan.cells_y, plan.cells_z)
    brick = pl.BlockSpec(tile, lambda t: (pick(t), 0, 0))
    _, per, _, _, fit, _ = plan.shape_of(chunk)
    in_specs = [
        pl.BlockSpec((plan.count, per, 8, LANES), lambda t: (0, pick(t), 0, 0)),
        pl.BlockSpec(
            (plan.count, 1, 8, LANES), lambda t: (0, plan.tiles * per + pick(t) // fit, 0, 0)
        ),
        pl.BlockSpec((plan.count, 1, 8, LANES), lambda t: (0, part.shape[1] - 1, 0, 0)),
        pl.BlockSpec(basis.shape, lambda t: (0, 0)),
        brick,
        brick,
        pl.BlockSpec((1, 1), lambda t: (0, 0)),
    ]
    operands = [part, part, part, basis, base, old, before.reshape(1, 1)]
    out_specs = pl.BlockSpec(tile, lambda t: (t, 0, 0))
    if ends:
        out_specs = [out_specs, pl.BlockSpec((8, LANES), lambda t: (0, 0))]
        out_shape = [
            jax.ShapeDtypeStruct((16,) + base.shape[1:], jnp.float32),
            jax.ShapeDtypeStruct((8, LANES), jnp.float32),
        ]
    else:
        in_specs.append(pl.BlockSpec(tile, lambda t: (t // last, 0, 0)))
        operands.append(done)
        out_shape = jax.ShapeDtypeStruct(base.shape, jnp.float32)
    return pl.pallas_call(
        functools.partial(final_kernel, plan, chunk, ends, pick),
        grid=(2 if ends else plan.tiles,),
        in_specs=in_specs,
        out_specs=out_specs,
        out_shape=out_shape,
        scratch_shapes=inverse_scratch(plan, basis),
        compiler_params=pltpu.CompilerParams(vmem_limit_bytes=50 * MIB),
        cost_estimate=inverse_cost(plan, basis, 2 if ends else plan.tiles - 2),
        name="inverse_ends" if ends else "inverse_inner",
    )(*operands)


def middle_kernel(plan, chunk, *refs):
    (
        in_ref,
        basis_x_ref,
        turned_x_ref,
        main_y_ref,
        rest_y_ref,
        eigen_x_ref,
        shift_ref,
        total_ref,
        out_ref,
        sum_ref,
        bx_high,
        bx_low,
        tx_high,
        tx_low,
        my_high,
        my_low,
        ry_high,
        ry_low,
        u_high,
        u_low,
        q_high,
        q_low,
        rest_acc,
    ) = refs
    size, per, part, tails, fit, lanes = plan.shape_of(chunk)
    full = size // plan.group
    last = chunk == len(plan.chunks) - 1
    wide, narrow, tiles = plan.wide, plan.narrow, plan.tiles
    half = plan.total_x // 2
    lump = wide // 2
    span = plan.total_y + LANES // 2
    width = 2 * plan.total_y
    bx_high[...], bx_low[...] = split(basis_x_ref[...])
    tx_high[...], tx_low[...] = split(turned_x_ref[...])
    my_high[...], my_low[...] = split(main_y_ref[...])
    ry_high[...], ry_low[...] = split(rest_y_ref[...])
    rest_acc[...] = jnp.zeros_like(rest_acc)

    def gathered(h, places):
        rows = pl.ds(h * lump, lump)
        sides = []
        for n in range(narrow):
            some = []
            for t in range(tiles):
                piece, turn = places(t)
                value = in_ref[rows, n, piece]
                some.append(pltpu.roll(value, LANES - turn, 2) if turn else value)
            sides.append(jnp.stack(some, axis=1).reshape(half, LANES))
        return jnp.concatenate(sides, axis=1)

    def pair(in_tail, p, total):
        for h in range(2):
            if in_tail:
                rest = gathered(h, lambda t: (tiles * per + t // fit, t % fit * lanes))
            else:
                rest = gathered(h, lambda t: (t * per + size + 2 * p // plan.group, 0))
            rest = split(rest)
            parts = []
            for s in range(2):
                j = 2 * p + s
                q = lax.rem(j, plan.group)
                parts.append(
                    dot3(split(gathered(h, lambda t: (t * per + j, 0))), (my_high[s], my_low[s]), (1, 0))
                    + dot3(rest, (ry_high[q], ry_low[q]), (1, 0))
                )
            cut = span - LANES
            joined = jnp.concatenate(
                [
                    parts[0][:, :cut],
                    parts[0][:, cut:] + parts[1][:, :LANES],
                    parts[1][:, LANES:],
                ],
                axis=1,
            )
            rows = pl.ds(h * half, half)
            u_high[rows, :], u_low[rows, :] = split(joined)
        shift = shift_ref[p]
        for h in range(2):
            rows = pl.ds(h * half, half)
            spectral = dot3(
                (tx_high[rows, :], tx_low[rows, :]), (u_high[...], u_low[...]), (1, 0)
            )
            scaled = spectral / (eigen_x_ref[rows, :] + shift)
            total = total + jnp.sum((spectral * scaled).reshape(half // 8, 8, width), axis=0)
            q_high[rows, :], q_low[rows, :] = split(scaled)
        for h in range(2):
            rows = pl.ds(h * half, half)
            value = dot3((bx_high[rows, :], bx_low[rows, :]), (q_high[...], q_low[...]), (1, 0))
            for s in range(2):
                j = 2 * p + s
                mine = split(value[:, s * (width - span) : s * (width - span) + span])
                main = dot3(mine, (my_high[s], my_low[s]), (1, 1))
                q = lax.rem(j, plan.group)
                rest_acc[2 * p // plan.group, rows, :] += dot3(
                    mine, (ry_high[q], ry_low[q]), (1, 1)
                )
                for n in range(narrow):
                    side = main[:, n * LANES : (n + 1) * LANES].reshape(lump, tiles, 8, LANES)
                    for t in range(tiles):
                        out_ref[pl.ds(h * lump, lump), n, t * per + j] = side[:, t]
        return total

    total = jnp.zeros((8, width), jnp.float32)
    total = lax.fori_loop(0, (size - part) // 2, functools.partial(pair, False), total)
    if tails:
        total = lax.fori_loop((size - part) // 2, size // 2, functools.partial(pair, True), total)
    value = total_ref[...] + jnp.sum(total)
    sum_ref[...] = value
    for n in range(narrow):
        side = slice(n * LANES, (n + 1) * LANES)
        for piece in range(full):
            rest = rest_acc[piece, :, side].reshape(wide, tiles, 8, LANES)
            for t in range(tiles):
                out_ref[:, n, t * per + size + piece] = rest[:, t]
        for tail in range(tails):
            rest = rest_acc[full, :, side].reshape(wide, tiles, 8, LANES)
            joined = rest[:, tail * fit]
            for t in range(tail * fit + 1, min(tail * fit + fit, tiles)):
                joined = joined + pltpu.roll(rest[:, t], t % fit * lanes, 2)
            if last and tail == tails - 1:
                lane = lax.broadcasted_iota(jnp.int32, joined.shape, 2)
                joined = jnp.where(lane == LANES - 1, value[:1, :][None], joined)
            out_ref[:, n, tiles * per + tail] = joined


def middle(plan, chunk, message, basis_x, turned_x, main_y, rest_y, eigen_x, shift, total):
    size = plan.chunks[chunk][1]
    pieces = -(-size // plan.group)
    shape = (plan.wide, plan.narrow) + message.shape[1:]
    square = (plan.total_x, plan.total_x)
    pencil = (plan.total_x, 2 * plan.total_y)
    half = jnp.bfloat16
    out, total = pl.pallas_call(
        functools.partial(middle_kernel, plan, chunk),
        out_shape=[
            jax.ShapeDtypeStruct(shape, jnp.float32),
            jax.ShapeDtypeStruct((8, LANES), jnp.float32),
        ],
        in_specs=[pl.BlockSpec(memory_space=pltpu.VMEM)] * 8,
        out_specs=[pl.BlockSpec(memory_space=pltpu.VMEM)] * 2,
        scratch_shapes=[
            pltpu.VMEM(square, half),
            pltpu.VMEM(square, half),
            pltpu.VMEM(square, half),
            pltpu.VMEM(square, half),
            pltpu.VMEM(main_y.shape, half),
            pltpu.VMEM(main_y.shape, half),
            pltpu.VMEM(rest_y.shape, half),
            pltpu.VMEM(rest_y.shape, half),
            pltpu.VMEM(pencil, half),
            pltpu.VMEM(pencil, half),
            pltpu.VMEM(pencil, half),
            pltpu.VMEM(pencil, half),
            pltpu.VMEM((pieces, plan.total_x, plan.narrow * LANES), jnp.float32),
        ],
        compiler_params=pltpu.CompilerParams(vmem_limit_bytes=44 * MIB),
        cost_estimate=pl.CostEstimate(
            flops=12 * size * plan.total_x * plan.total_y * (plan.total_x + plan.total_y),
            bytes_accessed=8 * message.size,
            transcendentals=0,
        ),
        name="middle",
    )(message.reshape(shape), basis_x, turned_x, main_y, rest_y, eigen_x, shift, total)
    return out.reshape(message.shape), total


def shifted(x, step, axis):
    count = lax.axis_size(axis)
    pairs = [(i + step, i) for i in range(count) if 0 <= i + step < count]
    return lax.ppermute(x, axis, pairs)


def from_sides(low, high, axis):
    if lax.axis_size(axis) != 2:
        return shifted(high, -1, axis), shifted(low, 1, axis)
    second = lax.axis_index(axis) == 1
    got = lax.ppermute(jnp.where(second, low, high), axis, [(0, 1), (1, 0)])
    return jnp.where(second, got, 0.0), jnp.where(second, 0.0, got)


mass_scale, stiff_scale = 5040.0, 120.0
CUT = LANES + LANES // 2
GROUP = 4


def band_matrices(cells_z):
    offset = np.arange(cells_z)[:, None] - np.arange(cells_z)[None, :]
    near = np.abs(offset) <= HALO
    tables = []
    for band, scale in ((mass_band, mass_scale), (stiff_band, stiff_scale)):
        whole = np.rint(np.asarray(band) * scale)
        full = np.where(near, whole[np.clip(offset + HALO, 0, 2 * HALO)], 0.0)
        first = np.zeros((2 * LANES, 2 * LANES))
        first[:, :CUT] = full[: 2 * LANES, :CUT]
        second = np.zeros((2 * LANES, 2 * LANES))
        second[: cells_z - LANES, CUT - LANES : cells_z - LANES] = full[LANES:, CUT:]
        tables.append(np.stack([first, second]).astype(np.float32))
    mass, stiff = tables
    high = mass.astype(ml_dtypes.bfloat16)
    low = (mass - high.astype(np.float32)).astype(ml_dtypes.bfloat16)
    return np.stack([high, low, stiff.astype(ml_dtypes.bfloat16)])


def stencil_kernel(plan, *refs):
    own, before_x, after_x, before_y, after_y, bands_ref, image_ref, sum_ref = refs[:8]
    field, f_high, f_low, s_high, s_low, h_a, h_b, total, sems = refs[8:]
    cells_x, cells_y, cells_z = plan.cells_x, plan.cells_y, plan.cells_z
    tiles = plan.tiles
    padded_y = cells_y + 2 * EDGE
    own_y = pl.ds(EDGE, cells_y)
    step = pl.program_id(0)

    def tile_copy(t):
        return pltpu.make_async_copy(
            own.at[pl.ds(8 * t, 8)], field.at[pl.ds(HALO + 8 * t, 8), own_y, :], sems.at[t]
        )

    first_copy = pltpu.make_async_copy(
        before_x, field.at[pl.ds(0, HALO), own_y, :], sems.at[tiles]
    )
    last_copy = pltpu.make_async_copy(
        after_x, field.at[pl.ds(HALO + cells_x, HALO), own_y, :], sems.at[tiles + 1]
    )

    @pl.when(step == 0)
    def _():
        first_copy.start()
        for t in range(tiles):
            tile_copy(t).start()
        last_copy.start()
        total[...] = jnp.zeros_like(total)
        field[:, EDGE - HALO : EDGE, :] = jnp.swapaxes(before_y[...], 0, 1)
        field[:, EDGE + cells_y : EDGE + cells_y + HALO, :] = jnp.swapaxes(after_y[...], 0, 1)
        first_copy.wait()
        tile_copy(0).wait()

    @pl.when(step < tiles - 1)
    def _():
        tile_copy(step + 1).wait()

    @pl.when(step == tiles - 1)
    def _():
        last_copy.wait()

    blocks = h_a.shape[0]
    ratio = stiff_scale / mass_scale

    def one(left, right):
        return lax.dot_general(
            left, right, (((1,), (0,)), ((), ())), preferred_element_type=jnp.float32
        )

    def planes(g, carry):
        for i in range(GROUP):
            x = step * 8 + g * GROUP + i
            middle_plane = field[x + HALO]
            first = ratio * stiff_band[HALO] * middle_plane
            second = mass_band[HALO] * middle_plane
            for o in range(1, HALO + 1):
                around = field[x + HALO - o] + field[x + HALO + o]
                first = first + ratio * stiff_band[HALO + o] * around
                second = second + mass_band[HALO + o] * around
            rows = pl.ds(i * padded_y, padded_y)
            f_high[rows, :], f_low[rows, :] = split(first)
            s_high[rows, :], s_low[rows, :] = split(second)
        window_a, window_b = [], []
        for w, lanes in enumerate((pl.ds(0, 2 * LANES), pl.ds(LANES, cells_z - LANES))):
            high, low, stiff = (bands_ref[k, w, : lanes.size, :] for k in range(3))
            fh, fl, sh, sl = (ref[:, lanes] for ref in (f_high, f_low, s_high, s_low))
            window_a.append(
                one(fh, high) + one(fl, high) + one(fh, low) + one(sh, stiff) + one(sl, stiff)
            )
            window_b.append(one(sh, high) + one(sl, high) + one(sh, low))
        for ref, (left, right) in ((h_a, window_a), (h_b, window_b)):
            ref[0] = left[:, :LANES]
            ref[1] = left[:, LANES:] + right[:, :LANES]
            ref[2] = right[:, LANES:]
        for i in range(GROUP):
            plane = g * GROUP + i
            for k in range(blocks):
                lanes = min(LANES, cells_z - k * LANES)
                at = lambda ref, o: ref[k, pl.ds(i * padded_y + EDGE + o, cells_y), :]
                image = (mass_band[HALO] / stiff_scale) * at(h_a, 0)
                image = image + (stiff_band[HALO] / mass_scale) * at(h_b, 0)
                for o in range(1, HALO + 1):
                    image = image + (mass_band[HALO + o] / stiff_scale) * (at(h_a, -o) + at(h_a, o))
                    image = image + (stiff_band[HALO + o] / mass_scale) * (at(h_b, -o) + at(h_b, o))
                here = pl.ds(k * LANES, lanes)
                image_ref[plane, :, here] = image[:, :lanes]
                product = image[:, :lanes] * field[step * 8 + plane + HALO, own_y, here]
                total[:, here] += jnp.sum(product.reshape(cells_y // 8, 8, lanes), axis=0)
        return carry

    lax.fori_loop(0, 8 // GROUP, planes, 0)

    @pl.when(step == pl.num_programs(0) - 1)
    def _():
        sum_ref[...] = jnp.full(sum_ref.shape, jnp.sum(total[...]), jnp.float32)


def stencil(plan, direction, before_x, after_x):
    cells_x, cells_y, cells_z = direction.shape

    def strip(rows):
        parts = [jnp.swapaxes(v[:, rows], 0, 1) for v in (before_x, direction, after_x)]
        return jnp.concatenate(parts, axis=1)

    before_y, after_y = from_sides(
        strip(slice(0, HALO)), strip(slice(cells_y - HALO, cells_y)), "narrow"
    )
    bands = band_matrices(cells_z)
    padded_y = cells_y + 2 * EDGE
    blocks = -(-cells_z // LANES)
    lump = (GROUP * padded_y, cells_z)
    return pl.pallas_call(
        functools.partial(stencil_kernel, plan),
        grid=(cells_x // 8,),
        in_specs=[pl.BlockSpec(memory_space=pl.ANY)] * 3
        + [pl.BlockSpec(before_y.shape, lambda t: (0, 0, 0))] * 2
        + [pl.BlockSpec(bands.shape, lambda t: (0, 0, 0, 0))],
        out_specs=[
            pl.BlockSpec((8, cells_y, cells_z), lambda t: (t, 0, 0)),
            pl.BlockSpec((plan.count, 8, LANES), lambda t: (0, 0, 0)),
        ],
        out_shape=[
            jax.ShapeDtypeStruct(direction.shape, jnp.float32),
            jax.ShapeDtypeStruct((plan.count, 8, LANES), jnp.float32),
        ],
        scratch_shapes=[
            pltpu.VMEM((cells_x + 2 * HALO, padded_y, cells_z), jnp.float32),
            pltpu.VMEM(lump, jnp.bfloat16),
            pltpu.VMEM(lump, jnp.bfloat16),
            pltpu.VMEM(lump, jnp.bfloat16),
            pltpu.VMEM(lump, jnp.bfloat16),
            pltpu.VMEM((blocks, GROUP * padded_y, LANES), jnp.float32),
            pltpu.VMEM((blocks, GROUP * padded_y, LANES), jnp.float32),
            pltpu.VMEM((8, cells_z), jnp.float32),
            pltpu.SemaphoreType.DMA((plan.tiles + 2,)),
        ],
        compiler_params=pltpu.CompilerParams(vmem_limit_bytes=50 * MIB),
        cost_estimate=pl.CostEstimate(
            flops=8 * direction.size * cells_z, bytes_accessed=8 * direction.size, transcendentals=0
        ),
        name="stencil",
    )(direction, before_x, after_x, before_y, after_y, bands)


def update_kernel(now_ref, parts_ref, solution_ref, residual_ref, direction_ref, image_ref, *outs):
    curvature = jnp.sum(parts_ref[:, 0, :1], axis=0, keepdims=True)
    alpha = (now_ref[:1, :1] / curvature)[None]
    outs[0][...] = solution_ref[...] + alpha * direction_ref[...]
    outs[1][...] = residual_ref[...] - alpha * image_ref[...]


def update(now, parts, solution, residual, direction, image):
    brick = pl.BlockSpec((4,) + image.shape[1:], lambda t: (t, 0, 0))
    return pl.pallas_call(
        update_kernel,
        grid=(image.shape[0] // 4,),
        in_specs=[
            pl.BlockSpec(now.shape, lambda t: (0, 0)),
            pl.BlockSpec(parts.shape, lambda t: (0, 0, 0)),
        ]
        + [brick] * 4,
        out_specs=[brick] * 2,
        out_shape=[jax.ShapeDtypeStruct(image.shape, jnp.float32)] * 2,
        compiler_params=pltpu.CompilerParams(vmem_limit_bytes=50 * MIB),
        name="update",
    )(now, parts, solution, residual, direction, image)


def scatter(x):
    return lax.all_to_all(x, both, split_axis=0, concat_axis=0, tiled=True)


def dealt(plan, whole_z):
    columns = whole_z.T.reshape(plan.count, plan.share, plan.cells_z)
    return jnp.swapaxes(columns, 0, 1).reshape(plan.cells_z, plan.cells_z)


def basis_y_blocks(plan, whole_y):
    by_owner = whole_y.reshape(plan.narrow, plan.cells_y, plan.total_y)
    main = by_owner[:, :LANES].reshape(plan.narrow * LANES, plan.total_y)
    rest = by_owner[:, LANES:]
    half = LANES // 2
    sides = [(0, half), (half, 0)]
    mains = jnp.stack([jnp.pad(main, ((0, 0), s)) for s in sides])
    rests = []
    for q in range(plan.group):
        after = LANES - (q + 1) * plan.rest
        padded = jnp.pad(rest, ((0, 0), (q * plan.rest, after), sides[q % 2]))
        rests.append(padded.reshape(plan.narrow * LANES, plan.total_y + half))
    return mains, jnp.stack(rests)


def by_pencils(
    plan,
    solution,
    residual,
    direction,
    previous_product,
    basis_x,
    basis_y,
    basis_z,
    eigen_x,
    eigen_y,
    eigen_z,
):
    whole_z = lax.all_gather(basis_z, "narrow", axis=0, tiled=True)
    turned_z = dealt(plan, whole_z)
    whole_y = lax.all_gather(basis_y, "narrow", axis=0, tiled=True)
    whole_x = lax.all_gather(basis_x, "wide", axis=0, tiled=True)
    sent = [forward_z(plan, k, residual, turned_z) for k in range(2)]
    arrived = [scatter(sent[0])]
    later, whole_x, whole_y = lax.optimization_barrier((sent[1], whole_x, whole_y))
    arrived.append(scatter(later))
    main_y, rest_y = basis_y_blocks(plan, whole_y)
    turned_x = whole_x.T
    index = lax.axis_index("wide") * plan.narrow + lax.axis_index("narrow")
    mine_z = lax.dynamic_slice_in_dim(eigen_z, index * plan.share, plan.share)
    shifts = (mine_z[:, None] + eigen_y[None, :]).reshape(plan.share // 2, 1, 2 * plan.total_y)
    total = jnp.zeros((8, LANES), jnp.float32)
    returned = []
    for k, (start, size) in enumerate(plan.chunks):
        shift = shifts[start // 2 : (start + size) // 2]
        back, total = middle(
            plan,
            k,
            arrived[k],
            whole_x,
            turned_x,
            main_y,
            rest_y,
            eigen_x.reshape(-1, 1),
            shift,
            total,
        )
        returned.append(scatter(back))
    base = inverse_base(plan, 0, returned[0], turned_z)
    inverse = functools.partial(
        inverse_final, plan, 1, returned[1], turned_z, base, direction, previous_product
    )
    ends, now = inverse()
    before_x = shifted(ends[16 - HALO :], -1, "wide")
    after_x = shifted(ends[:HALO], 1, "wide")
    direction = inverse(ends)
    image, part = stencil(plan, direction, before_x, after_x)
    solution, residual = update(now, scatter(part), solution, residual, direction, image)
    return solution, residual, direction


def padded_2(x, sides, width):
    for axis, dim in sides:
        count, length = (lax.axis_size(axis), x.shape[dim])
        up = [(i, (i + 1) % count) for i in range(count - 1)]
        down = [(j, i) for i, j in up]
        last = lax.slice_in_dim(x, length - width, length, axis=dim)
        leading = lax.slice_in_dim(x, 0, width, axis=dim)
        before = lax.ppermute(last, axis, up)
        after = lax.ppermute(leading, axis, down)
        x = jnp.concatenate([before, x, after], axis=dim)
    return x


def banded(field, coeffs, axis, length):
    total = coeffs[0] * lax.slice_in_dim(field, 0, length, axis=axis)
    for offset in range(1, 7):
        total = total + coeffs[offset] * lax.slice_in_dim(field, offset, offset + length, axis=axis)
    return total


def apply_padded(padded, length_x, length_y):
    length_z = padded.shape[2]
    along_z = jnp.pad(padded, ((0, 0), (0, 0), (3, 3)))
    mass_z = banded(along_z, mass_band, 2, length_z)
    stiff_z = banded(along_z, stiff_band, 2, length_z)
    first = banded(mass_z, mass_band, 1, length_y)
    second = banded(mass_z, stiff_band, 1, length_y) + banded(stiff_z, mass_band, 1, length_y)
    return banded(first, stiff_band, 0, length_x) + banded(second, mass_band, 0, length_x)


def contract_first(left, right):
    return lax.dot_general(left, right, (((0,), (0,)), ((), ())), precision=highest)


def contract_last(left, right):
    return lax.dot_general(left, right, (((1,), (1,)), ((), ())), precision=highest)


def general(
    solution,
    residual,
    direction,
    previous_product,
    basis_x,
    basis_y,
    basis_z,
    eigen_x,
    eigen_y,
    eigen_z,
):
    whole_x = lax.all_gather(basis_x, "wide", axis=0, tiled=True)
    whole_y, whole_z = (
        lax.all_gather(basis_y, "narrow", axis=0, tiled=True),
        lax.all_gather(basis_z, "narrow", axis=0, tiled=True),
    )
    count_wide = lax.axis_size("wide")
    count_narrow = lax.axis_size("narrow")
    index_wide = lax.axis_index("wide")
    index_narrow = lax.axis_index("narrow")
    cells_x, cells_y, cells_z = residual.shape
    total_x = whole_x.shape[0]
    total_y = whole_y.shape[0]
    product_before = previous_product[0]
    spectral = jnp.dot(residual.reshape(cells_x * cells_y, cells_z), whole_z, precision=highest)
    flat = jnp.transpose(spectral.reshape(cells_x, cells_y, cells_z), (1, 2, 0)).reshape(
        cells_y, cells_z * cells_x
    )
    pencil = contract_first(
        whole_y, lax.all_to_all(flat, "narrow", split_axis=1, concat_axis=0, tiled=True)
    )
    rows_y = total_y // count_wide
    part_z = cells_z // count_narrow
    moved = lax.all_to_all(pencil, "wide", split_axis=0, concat_axis=1, tiled=True)
    lined = jnp.transpose(moved.reshape(rows_y, count_wide, part_z, cells_x), (0, 2, 1, 3))
    lined = lined.reshape(rows_y * part_z, total_x)
    spectral_x = jnp.dot(lined, whole_x, precision=highest)
    shift_y = lax.dynamic_slice_in_dim(eigen_y, index_wide * rows_y, rows_y)
    shift_z = lax.dynamic_slice_in_dim(eigen_z, index_narrow * part_z, part_z)
    shift_yz = (shift_y[:, None] + shift_z[None, :]).reshape(rows_y * part_z, 1)
    scaled = spectral_x / (eigen_x[None, :] + shift_yz)
    inverse_x = contract_last(scaled, whole_x)
    unlined = jnp.transpose(inverse_x.reshape(rows_y, part_z, count_wide, cells_x), (0, 2, 1, 3))
    unlined = unlined.reshape(rows_y, count_wide * part_z * cells_x)
    pencil = lax.all_to_all(unlined, "wide", split_axis=1, concat_axis=0, tiled=True)
    pencil = jnp.dot(whole_y, pencil, precision=highest)
    back = lax.all_to_all(pencil, "narrow", split_axis=0, concat_axis=1, tiled=True)
    brick = jnp.transpose(back.reshape(cells_y, cells_z, cells_x), (2, 0, 1))
    result = contract_last(brick.reshape(cells_x * cells_y, cells_z), whole_z)
    precond = result.reshape(cells_x, cells_y, cells_z)
    product_now = lax.psum(jnp.sum(residual * precond), ("wide", "narrow"))
    direction = precond + product_now / product_before * direction
    padded = padded_2(direction, (("wide", 0), ("narrow", 1)), 3)
    image = apply_padded(padded, cells_x, cells_y)
    curvature = lax.psum(jnp.sum(direction * image), ("wide", "narrow"))
    alpha = product_now / curvature
    solution = solution + alpha * direction
    residual = residual - alpha * image
    return (solution, residual, direction)


def per_device(*arrays):
    residual, basis_x, basis_y = arrays[1], arrays[4], arrays[5]
    wide, narrow = lax.axis_size("wide"), lax.axis_size("narrow")
    plan = Plan(*residual.shape, basis_x.shape[1], basis_y.shape[1], wide, narrow)
    if plan.fits:
        return by_pencils(plan, *arrays)
    return general(*arrays)


def solution(mesh):
    placed = (
        P("wide", "narrow", None),
        P("wide", "narrow", None),
        P("wide", "narrow", None),
        P(),
        P("wide", None),
        P("narrow", None),
        P("narrow", None),
        P(),
        P(),
        P(),
    )
    return jax.shard_map(
        per_device,
        mesh=mesh,
        in_specs=placed,
        out_specs=(P("wide", "narrow", None), P("wide", "narrow", None), P("wide", "narrow", None)),
        check_vma=False,
    )
```

```python
import functools

import jax
import jax.numpy as jnp
import ml_dtypes
import numpy as np
from jax import lax
from jax.experimental import pallas as pl
from jax.experimental.pallas import tpu as pltpu
from jax.sharding import PartitionSpec as P

mass_band = (
    1.0 / 5040.0,
    1.0 / 42.0,
    397.0 / 1680.0,
    151.0 / 315.0,
    397.0 / 1680.0,
    1.0 / 42.0,
    1.0 / 5040.0,
)
stiff_band = (-1.0 / 120.0, -0.2, -0.125, 2.0 / 3.0, -0.125, -0.2, -1.0 / 120.0)
highest = lax.Precision.HIGHEST
LANES = 128
HALO = 3
EDGE = 8
both = ("wide", "narrow")
MIB = 1024 * 1024


def split(x):
    high = x.astype(jnp.bfloat16)
    low = (x - high.astype(jnp.float32)).astype(jnp.bfloat16)
    return high, low


def dot3(left, right, over):
    dims = ((over[:1], over[1:]), ((), ()))
    one = functools.partial(
        lax.dot_general, dimension_numbers=dims, preferred_element_type=jnp.float32
    )
    return one(left[0], right[0]) + one(left[1], right[0]) + one(left[0], right[1])


class Plan:
    def __init__(self, cells_x, cells_y, cells_z, total_x, total_y, wide, narrow):
        self.cells_x, self.cells_y, self.cells_z = cells_x, cells_y, cells_z
        self.total_x, self.total_y = total_x, total_y
        self.wide, self.narrow, self.count = wide, narrow, wide * narrow
        self.rest = cells_y - LANES
        self.fits = (
            cells_z % self.count == 0
            and cells_x % 8 == 0
            and self.rest > 0
            and LANES % self.rest == 0
            and self.rest < LANES
            and total_y % LANES == LANES // 2
            and wide % 2 == 0
            and (total_x // 2) % 16 == 0
            and self.count % 8 == 0
        )
        if not self.fits:
            return
        self.share = cells_z // self.count
        self.group = LANES // self.rest
        self.tiles = cells_x // 8
        self.chunks = [(0, self.group), (self.group, self.share - self.group)]
        self.fits = (
            self.group % 2 == 0
            and self.share % 2 == 0
            and self.share > self.group
            and self.share % self.group != 0
            and self.tiles >= 3
            and 2 * LANES < cells_z <= 3 * LANES
        )
        if self.fits:
            _, _, _, _, fit, width = self.shape_of(1)
            self.fits = self.tiles % fit != 0 or fit * width < LANES

    def rows(self, chunk):
        start, size = self.chunks[chunk]
        return start * self.count, size * self.count

    def shape_of(self, chunk):
        size = self.chunks[chunk][1]
        part = size % self.group
        width = part * self.rest
        fit = LANES // width if part else 1
        tails = -(-self.tiles // fit) if part else 0
        return size, size + size // self.group, part, tails, fit, width

    def message(self, chunk):
        _, per, _, tails, _, _ = self.shape_of(chunk)
        return (self.count, self.tiles * per + tails, 8, LANES)


def forward_kernel(plan, chunk, field_ref, basis_ref, out_ref, high_ref, low_ref, stage_ref):
    size, per, part, tails, fit, width = plan.shape_of(chunk)
    step = pl.program_id(0)

    @pl.when(step == 0)
    def _():
        high_ref[...], low_ref[...] = split(basis_ref[...])
        if tails:
            out_ref[:, plan.tiles * per :] = jnp.zeros((plan.count, tails, 8, LANES), jnp.float32)

    basis = (high_ref[...], low_ref[...])
    for i in range(8):
        stage_ref[i] = dot3(basis, split(field_ref[i]), (1, 1))
    base = step * per if tails else 0
    rests = []
    for j in range(size):
        at = j * plan.count
        turned = jnp.swapaxes(stage_ref[:, at : at + plan.count, :], 0, 1)
        out_ref[:, base + j] = turned[:, :, :LANES]
        rests.append(turned[:, :, LANES:])
    for piece in range(size // plan.group):
        some = rests[piece * plan.group : (piece + 1) * plan.group]
        out_ref[:, base + size + piece] = jnp.concatenate(some, axis=2)
    if tails:
        some = jnp.concatenate(rests[size - part :], axis=2)
        for place in range(fit):

            @pl.when(step % fit == place)
            def _():
                lanes = slice(place * width, (place + 1) * width)
                out_ref[:, plan.tiles * per + step // fit, :, lanes] = some


def forward_z(plan, chunk, field, basis):
    start, rows = plan.rows(chunk)
    basis = basis[start : start + rows]
    message = plan.message(chunk)
    _, per, _, tails, _, _ = plan.shape_of(chunk)
    if tails:
        out_spec = pl.BlockSpec(message, lambda t: (0, 0, 0, 0))
    else:
        out_spec = pl.BlockSpec((message[0], per) + message[2:], lambda t: (0, t, 0, 0))
    return pl.pallas_call(
        functools.partial(forward_kernel, plan, chunk),
        grid=(plan.tiles,),
        in_specs=[
            pl.BlockSpec((8, plan.cells_y, plan.cells_z), lambda t: (t, 0, 0)),
            pl.BlockSpec(basis.shape, lambda t: (0, 0)),
        ],
        out_specs=out_spec,
        out_shape=jax.ShapeDtypeStruct(message, jnp.float32),
        scratch_shapes=[
            pltpu.VMEM(basis.shape, jnp.bfloat16),
            pltpu.VMEM(basis.shape, jnp.bfloat16),
            pltpu.VMEM((8, rows, plan.cells_y), jnp.float32),
        ],
        compiler_params=pltpu.CompilerParams(vmem_limit_bytes=50 * MIB),
        cost_estimate=pl.CostEstimate(
            flops=6 * field.size * rows, bytes_accessed=8 * field.size, transcendentals=0
        ),
        name="forward_z",
    )(field, basis)


def add_chunk(plan, chunk, tile, part_ref, tail_ref, stage_ref):
    size, _, part, tails, fit, width = plan.shape_of(chunk)
    if tails:
        tail = tail_ref[:, 0]
        for place in range(1, fit):
            turned = pltpu.roll(tail_ref[:, 0], LANES - place * width, 2)
            tail = jnp.where(tile % fit == place, turned, tail)
    for j in range(size):
        at, q = j * plan.count, j % plan.group
        lanes = slice(q * plan.rest, (q + 1) * plan.rest)
        stage_ref[:, at : at + plan.count, :LANES] = jnp.swapaxes(part_ref[:, j], 0, 1)
        if j < size - part:
            rest = part_ref[:, size + j // plan.group, :, lanes]
        else:
            rest = tail[:, :, lanes]
        stage_ref[:, at : at + plan.count, LANES:] = jnp.swapaxes(rest, 0, 1)


def base_kernel(plan, chunk, part_ref, basis_ref, out_ref, high_ref, low_ref, stage_ref):
    step = pl.program_id(0)

    @pl.when(step == 0)
    def _():
        high_ref[...], low_ref[...] = split(basis_ref[...])

    add_chunk(plan, chunk, step, part_ref, None, stage_ref)
    basis = (high_ref[...], low_ref[...])
    for i in range(8):
        out_ref[i] = dot3(split(stage_ref[i].T), basis, (1, 0))


def final_kernel(plan, chunk, ends, pick, *refs):
    part_ref, tail_ref, last_ref, basis_ref, base_ref, old_ref, before_ref = refs[:7]
    if ends:
        out_ref, now_ref, high_ref, low_ref, stage_ref = refs[7:]
    else:
        _, out_ref, high_ref, low_ref, stage_ref = refs[7:]
    step = pl.program_id(0)

    @pl.when(step == 0)
    def _():
        high_ref[...], low_ref[...] = split(basis_ref[...])

    def work():
        add_chunk(plan, chunk, pick(step), part_ref, tail_ref, stage_ref)
        now = jnp.sum(last_ref[:, 0, 0, LANES - 1 :], axis=0, keepdims=True)
        beta = now / before_ref[...]
        basis = (high_ref[...], low_ref[...])
        for i in range(8):
            value = dot3(split(stage_ref[i].T), basis, (1, 0))
            out_ref[i] = base_ref[i] + value + beta * old_ref[i]
        if ends:
            now_ref[...] = jnp.broadcast_to(now, now_ref.shape)

    work()


def inverse_scratch(plan, basis):
    return [
        pltpu.VMEM(basis.shape, jnp.bfloat16),
        pltpu.VMEM(basis.shape, jnp.bfloat16),
        pltpu.VMEM((8, basis.shape[0], plan.cells_y), jnp.float32),
    ]


def inverse_cost(plan, basis, tiles):
    size = tiles * 8 * plan.cells_y * plan.cells_z
    return pl.CostEstimate(
        flops=6 * size * basis.shape[0], bytes_accessed=12 * size, transcendentals=0
    )


def inverse_base(plan, chunk, part, basis):
    start, rows = plan.rows(chunk)
    per = plan.shape_of(chunk)[1]
    basis = basis[start : start + rows]
    return pl.pallas_call(
        functools.partial(base_kernel, plan, chunk),
        grid=(plan.tiles,),
        in_specs=[
            pl.BlockSpec((plan.count, per, 8, LANES), lambda t: (0, t, 0, 0)),
            pl.BlockSpec(basis.shape, lambda t: (0, 0)),
        ],
        out_specs=pl.BlockSpec((8, plan.cells_y, plan.cells_z), lambda t: (t, 0, 0)),
        out_shape=jax.ShapeDtypeStruct((plan.cells_x, plan.cells_y, plan.cells_z), jnp.float32),
        scratch_shapes=inverse_scratch(plan, basis),
        compiler_params=pltpu.CompilerParams(vmem_limit_bytes=50 * MIB),
        cost_estimate=inverse_cost(plan, basis, plan.tiles),
        name="inverse_base",
    )(part, basis)


def inverse_final(plan, chunk, part, basis, base, old, before, done=None):
    ends = done is None
    start, rows = plan.rows(chunk)
    basis = basis[start : start + rows]
    last = plan.tiles - 1
    if ends:
        pick = lambda t: t * last
    else:
        pick = lambda t: t + 1
    tile = (8, plan.cells_y, plan.cells_z)
    brick = pl.BlockSpec(tile, lambda t: (pick(t), 0, 0))
    _, per, _, _, fit, _ = plan.shape_of(chunk)
    in_specs = [
        pl.BlockSpec((plan.count, per, 8, LANES), lambda t: (0, pick(t), 0, 0)),
        pl.BlockSpec(
            (plan.count, 1, 8, LANES), lambda t: (0, plan.tiles * per + pick(t) // fit, 0, 0)
        ),
        pl.BlockSpec((plan.count, 1, 8, LANES), lambda t: (0, part.shape[1] - 1, 0, 0)),
        pl.BlockSpec(basis.shape, lambda t: (0, 0)),
        brick,
        brick,
        pl.BlockSpec((1, 1), lambda t: (0, 0)),
    ]
    operands = [part, part, part, basis, base, old, before.reshape(1, 1)]
    out_specs = brick
    if ends:
        out_specs = [out_specs, pl.BlockSpec((8, LANES), lambda t: (0, 0))]
        out_shape = [
            jax.ShapeDtypeStruct(base.shape, jnp.float32),
            jax.ShapeDtypeStruct((8, LANES), jnp.float32),
        ]
    else:
        in_specs.append(pl.BlockSpec(memory_space=pl.ANY))
        operands.append(done)
        out_shape = jax.ShapeDtypeStruct(base.shape, jnp.float32)
    return pl.pallas_call(
        functools.partial(final_kernel, plan, chunk, ends, pick),
        grid=(2 if ends else plan.tiles - 2,),
        input_output_aliases={} if ends else {len(operands) - 1: 0},
        in_specs=in_specs,
        out_specs=out_specs,
        out_shape=out_shape,
        scratch_shapes=inverse_scratch(plan, basis),
        compiler_params=pltpu.CompilerParams(vmem_limit_bytes=50 * MIB),
        cost_estimate=inverse_cost(plan, basis, 2 if ends else plan.tiles - 2),
        name="inverse_ends" if ends else "inverse_inner",
    )(*operands)


def middle_kernel(plan, chunk, *refs):
    (
        in_ref,
        basis_x_ref,
        turned_x_ref,
        main_y_ref,
        rest_y_ref,
        eigen_x_ref,
        shift_ref,
        total_ref,
        out_ref,
        sum_ref,
        bx_high,
        bx_low,
        tx_high,
        tx_low,
        my_high,
        my_low,
        ry_high,
        ry_low,
        u_high,
        u_low,
        q_high,
        q_low,
        rest_acc,
    ) = refs
    size, per, part, tails, fit, lanes = plan.shape_of(chunk)
    full = size // plan.group
    last = chunk == len(plan.chunks) - 1
    wide, narrow, tiles = plan.wide, plan.narrow, plan.tiles
    half = plan.total_x // 2
    lump = wide // 2
    span = plan.total_y + LANES // 2
    width = 2 * plan.total_y
    bx_high[...], bx_low[...] = split(basis_x_ref[...])
    tx_high[...], tx_low[...] = split(turned_x_ref[...])
    my_high[...], my_low[...] = split(main_y_ref[...])
    ry_high[...], ry_low[...] = split(rest_y_ref[...])
    rest_acc[...] = jnp.zeros_like(rest_acc)

    def gathered(h, places):
        rows = pl.ds(h * lump, lump)
        sides = []
        for n in range(narrow):
            some = []
            for t in range(tiles):
                piece, turn = places(t)
                value = in_ref[rows, n, piece]
                some.append(pltpu.roll(value, LANES - turn, 2) if turn else value)
            sides.append(jnp.stack(some, axis=1).reshape(half, LANES))
        return jnp.concatenate(sides, axis=1)

    def pair(in_tail, p, total):
        for h in range(2):
            if in_tail:
                rest = gathered(h, lambda t: (tiles * per + t // fit, t % fit * lanes))
            else:
                rest = gathered(h, lambda t: (t * per + size + 2 * p // plan.group, 0))
            rest = split(rest)
            parts = []
            for s in range(2):
                j = 2 * p + s
                q = lax.rem(j, plan.group)
                parts.append(
                    dot3(split(gathered(h, lambda t: (t * per + j, 0))), (my_high[s], my_low[s]), (1, 0))
                    + dot3(rest, (ry_high[q], ry_low[q]), (1, 0))
                )
            cut = span - LANES
            joined = jnp.concatenate(
                [
                    parts[0][:, :cut],
                    parts[0][:, cut:] + parts[1][:, :LANES],
                    parts[1][:, LANES:],
                ],
                axis=1,
            )
            rows = pl.ds(h * half, half)
            u_high[rows, :], u_low[rows, :] = split(joined)
        shift = shift_ref[p]
        for h in range(2):
            rows = pl.ds(h * half, half)
            spectral = dot3(
                (tx_high[rows, :], tx_low[rows, :]), (u_high[...], u_low[...]), (1, 0)
            )
            scaled = spectral / (eigen_x_ref[rows, :] + shift)
            total = total + jnp.sum((spectral * scaled).reshape(half // 8, 8, width), axis=0)
            q_high[rows, :], q_low[rows, :] = split(scaled)
        for h in range(2):
            rows = pl.ds(h * half, half)
            value = dot3((bx_high[rows, :], bx_low[rows, :]), (q_high[...], q_low[...]), (1, 0))
            for s in range(2):
                j = 2 * p + s
                mine = split(value[:, s * (width - span) : s * (width - span) + span])
                main = dot3(mine, (my_high[s], my_low[s]), (1, 1))
                q = lax.rem(j, plan.group)
                rest_acc[2 * p // plan.group, rows, :] += dot3(
                    mine, (ry_high[q], ry_low[q]), (1, 1)
                )
                for n in range(narrow):
                    side = main[:, n * LANES : (n + 1) * LANES].reshape(lump, tiles, 8, LANES)
                    for t in range(tiles):
                        out_ref[pl.ds(h * lump, lump), n, t * per + j] = side[:, t]
        return total

    total = jnp.zeros((8, width), jnp.float32)
    total = lax.fori_loop(0, (size - part) // 2, functools.partial(pair, False), total)
    if tails:
        total = lax.fori_loop((size - part) // 2, size // 2, functools.partial(pair, True), total)
    value = total_ref[...] + jnp.sum(total)
    sum_ref[...] = value
    for n in range(narrow):
        side = slice(n * LANES, (n + 1) * LANES)
        for piece in range(full):
            rest = rest_acc[piece, :, side].reshape(wide, tiles, 8, LANES)
            for t in range(tiles):
                out_ref[:, n, t * per + size + piece] = rest[:, t]
        for tail in range(tails):
            rest = rest_acc[full, :, side].reshape(wide, tiles, 8, LANES)
            joined = rest[:, tail * fit]
            for t in range(tail * fit + 1, min(tail * fit + fit, tiles)):
                joined = joined + pltpu.roll(rest[:, t], t % fit * lanes, 2)
            if last and tail == tails - 1:
                lane = lax.broadcasted_iota(jnp.int32, joined.shape, 2)
                joined = jnp.where(lane == LANES - 1, value[:1, :][None], joined)
            out_ref[:, n, tiles * per + tail] = joined


def middle(plan, chunk, message, basis_x, turned_x, main_y, rest_y, eigen_x, shift, total):
    size = plan.chunks[chunk][1]
    pieces = -(-size // plan.group)
    shape = (plan.wide, plan.narrow) + message.shape[1:]
    square = (plan.total_x, plan.total_x)
    pencil = (plan.total_x, 2 * plan.total_y)
    half = jnp.bfloat16
    out, total = pl.pallas_call(
        functools.partial(middle_kernel, plan, chunk),
        out_shape=[
            jax.ShapeDtypeStruct(shape, jnp.float32),
            jax.ShapeDtypeStruct((8, LANES), jnp.float32),
        ],
        in_specs=[pl.BlockSpec(memory_space=pltpu.VMEM)] * 8,
        out_specs=[pl.BlockSpec(memory_space=pltpu.VMEM)] * 2,
        scratch_shapes=[
            pltpu.VMEM(square, half),
            pltpu.VMEM(square, half),
            pltpu.VMEM(square, half),
            pltpu.VMEM(square, half),
            pltpu.VMEM(main_y.shape, half),
            pltpu.VMEM(main_y.shape, half),
            pltpu.VMEM(rest_y.shape, half),
            pltpu.VMEM(rest_y.shape, half),
            pltpu.VMEM(pencil, half),
            pltpu.VMEM(pencil, half),
            pltpu.VMEM(pencil, half),
            pltpu.VMEM(pencil, half),
            pltpu.VMEM((pieces, plan.total_x, plan.narrow * LANES), jnp.float32),
        ],
        compiler_params=pltpu.CompilerParams(vmem_limit_bytes=44 * MIB),
        cost_estimate=pl.CostEstimate(
            flops=12 * size * plan.total_x * plan.total_y * (plan.total_x + plan.total_y),
            bytes_accessed=8 * message.size,
            transcendentals=0,
        ),
        name="middle",
    )(message.reshape(shape), basis_x, turned_x, main_y, rest_y, eigen_x, shift, total)
    return out.reshape(message.shape), total


def shifted(x, step, axis):
    count = lax.axis_size(axis)
    pairs = [(i + step, i) for i in range(count) if 0 <= i + step < count]
    return lax.ppermute(x, axis, pairs)


def from_sides(low, high, axis):
    if lax.axis_size(axis) != 2:
        return shifted(high, -1, axis), shifted(low, 1, axis)
    second = lax.axis_index(axis) == 1
    got = lax.ppermute(jnp.where(second, low, high), axis, [(0, 1), (1, 0)])
    return jnp.where(second, got, 0.0), jnp.where(second, 0.0, got)


mass_scale, stiff_scale = 5040.0, 120.0
CUT = LANES + LANES // 2
GROUP = 4


def band_matrices(cells_z):
    offset = np.arange(cells_z)[:, None] - np.arange(cells_z)[None, :]
    near = np.abs(offset) <= HALO
    tables = []
    for band, scale in ((mass_band, mass_scale), (stiff_band, stiff_scale)):
        whole = np.rint(np.asarray(band) * scale)
        full = np.where(near, whole[np.clip(offset + HALO, 0, 2 * HALO)], 0.0)
        first = np.zeros((2 * LANES, 2 * LANES))
        first[:, :CUT] = full[: 2 * LANES, :CUT]
        second = np.zeros((2 * LANES, 2 * LANES))
        second[: cells_z - LANES, CUT - LANES : cells_z - LANES] = full[LANES:, CUT:]
        tables.append(np.stack([first, second]).astype(np.float32))
    mass, stiff = tables
    high = mass.astype(ml_dtypes.bfloat16)
    low = (mass - high.astype(np.float32)).astype(ml_dtypes.bfloat16)
    return np.stack([high, low, stiff.astype(ml_dtypes.bfloat16)])


def stencil_kernel(plan, *refs):
    own, before_x, after_x, before_y, after_y, bands_ref, out, sum_ref = refs[:8]
    field, image_ref, f_high, f_low, s_high, s_low, h_a, h_b, total, sems, out_sems = refs[8:]
    cells_x, cells_y, cells_z = plan.cells_x, plan.cells_y, plan.cells_z
    tiles = plan.tiles
    padded_y = cells_y + 2 * EDGE
    own_y = pl.ds(EDGE, cells_y)
    groups = cells_x // GROUP
    blocks = h_a.shape[1]
    ratio = stiff_scale / mass_scale

    def tile_copy(t):
        return pltpu.make_async_copy(
            own.at[pl.ds(8 * t, 8)], field.at[pl.ds(HALO + 8 * t, 8), own_y, :], sems.at[t]
        )

    first_copy = pltpu.make_async_copy(
        before_x, field.at[pl.ds(0, HALO), own_y, :], sems.at[tiles]
    )
    last_copy = pltpu.make_async_copy(
        after_x, field.at[pl.ds(HALO + cells_x, HALO), own_y, :], sems.at[tiles + 1]
    )

    def out_copy(t):
        rows = pl.ds(8 * t, 8)
        return pltpu.make_async_copy(image_ref.at[rows], out.at[rows], out_sems.at[t])

    def one(left, right):
        return lax.dot_general(
            left, right, (((1,), (0,)), ((), ())), preferred_element_type=jnp.float32
        )

    def bands_x(g, slot):
        for i in range(GROUP):
            x = g * GROUP + i
            middle_plane = field[x + HALO]
            first = ratio * stiff_band[HALO] * middle_plane
            second = mass_band[HALO] * middle_plane
            for o in range(1, HALO + 1):
                around = field[x + HALO - o] + field[x + HALO + o]
                first = first + ratio * stiff_band[HALO + o] * around
                second = second + mass_band[HALO + o] * around
            rows = pl.ds(i * padded_y, padded_y)
            f_high[slot, rows, :], f_low[slot, rows, :] = split(first)
            s_high[slot, rows, :], s_low[slot, rows, :] = split(second)

    def bands_z(slot):
        window_a, window_b = [], []
        for w, lanes in enumerate((pl.ds(0, 2 * LANES), pl.ds(LANES, cells_z - LANES))):
            high, low, stiff = (bands_ref[k, w, : lanes.size, :] for k in range(3))
            fh, fl, sh, sl = (ref[slot, :, lanes] for ref in (f_high, f_low, s_high, s_low))
            window_a.append(
                one(fh, high) + one(fl, high) + one(fh, low) + one(sh, stiff) + one(sl, stiff)
            )
            window_b.append(one(sh, high) + one(sl, high) + one(sh, low))
        for ref, (left, right) in ((h_a, window_a), (h_b, window_b)):
            ref[slot, 0] = left[:, :LANES]
            ref[slot, 1] = left[:, LANES:] + right[:, :LANES]
            ref[slot, 2] = right[:, LANES:]

    def bands_y(g, slot, valid=None):
        for i in range(GROUP):
            x = g * GROUP + i
            for k in range(blocks):
                lanes = min(LANES, cells_z - k * LANES)
                at = lambda ref, o: ref[slot, k, pl.ds(i * padded_y + EDGE + o, cells_y), :]
                image = (mass_band[HALO] / stiff_scale) * at(h_a, 0)
                image = image + (stiff_band[HALO] / mass_scale) * at(h_b, 0)
                for o in range(1, HALO + 1):
                    image = image + (mass_band[HALO + o] / stiff_scale) * (at(h_a, -o) + at(h_a, o))
                    image = image + (stiff_band[HALO + o] / mass_scale) * (at(h_b, -o) + at(h_b, o))
                here = pl.ds(k * LANES, lanes)
                image_ref[x, :, here] = image[:, :lanes]
                product = image[:, :lanes] * field[x + HALO, own_y, here]
                product = jnp.sum(product.reshape(cells_y // 8, 8, lanes), axis=0)
                if valid is not None:
                    product = jnp.where(valid, product, 0.0)
                total[:, here] += product

    first_copy.start()
    for t in range(tiles):
        tile_copy(t).start()
    last_copy.start()
    total[...] = jnp.zeros_like(total)
    field[:, EDGE - HALO : EDGE, :] = jnp.swapaxes(before_y[...], 0, 1)
    field[:, EDGE + cells_y : EDGE + cells_y + HALO, :] = jnp.swapaxes(after_y[...], 0, 1)
    first_copy.wait()
    tile_copy(0).wait()
    bands_x(0, 0)

    def step(k, carry):
        @pl.when(k < tiles - 1)
        def _():
            tile_copy(k + 1).wait()

        @pl.when(k == tiles - 1)
        def _():
            last_copy.wait()

        bands_z(0)
        bands_x(2 * k + 1, 1)
        bands_y(jnp.maximum(2 * k - 1, 0), 1, k > 0)

        @pl.when(k > 0)
        def _():
            out_copy(k - 1).start()

        bands_z(1)
        bands_x(jnp.minimum(2 * k + 2, groups - 1), 0)
        bands_y(2 * k, 0)
        return carry

    lax.fori_loop(0, tiles, step, 0)
    bands_y(groups - 1, 1)
    out_copy(tiles - 1).start()
    sum_ref[...] = jnp.full(sum_ref.shape, jnp.sum(total[...]), jnp.float32)
    for t in range(tiles):
        out_copy(t).wait()


def stencil(plan, direction, before_x, after_x):
    cells_x, cells_y, cells_z = direction.shape

    def strip(rows):
        parts = [jnp.swapaxes(v[:, rows], 0, 1) for v in (before_x, direction, after_x)]
        return jnp.concatenate(parts, axis=1)

    before_y, after_y = from_sides(
        strip(slice(0, HALO)), strip(slice(cells_y - HALO, cells_y)), "narrow"
    )
    bands = band_matrices(cells_z)
    padded_y = cells_y + 2 * EDGE
    blocks = -(-cells_z // LANES)
    lump = (2, GROUP * padded_y, cells_z)
    rows = (2, blocks, GROUP * padded_y, LANES)
    whole = pl.BlockSpec(memory_space=pltpu.VMEM)
    return pl.pallas_call(
        functools.partial(stencil_kernel, plan),
        in_specs=[pl.BlockSpec(memory_space=pl.ANY)] * 3 + [whole] * 3,
        out_specs=[pl.BlockSpec(memory_space=pl.ANY), whole],
        out_shape=[
            jax.ShapeDtypeStruct(direction.shape, jnp.float32),
            jax.ShapeDtypeStruct((plan.count, 8, LANES), jnp.float32),
        ],
        scratch_shapes=[
            pltpu.VMEM((cells_x + 2 * HALO, padded_y, cells_z), jnp.float32),
            pltpu.VMEM(direction.shape, jnp.float32),
            pltpu.VMEM(lump, jnp.bfloat16),
            pltpu.VMEM(lump, jnp.bfloat16),
            pltpu.VMEM(lump, jnp.bfloat16),
            pltpu.VMEM(lump, jnp.bfloat16),
            pltpu.VMEM(rows, jnp.float32),
            pltpu.VMEM(rows, jnp.float32),
            pltpu.VMEM((8, cells_z), jnp.float32),
            pltpu.SemaphoreType.DMA((plan.tiles + 2,)),
            pltpu.SemaphoreType.DMA((plan.tiles,)),
        ],
        compiler_params=pltpu.CompilerParams(vmem_limit_bytes=50 * MIB),
        cost_estimate=pl.CostEstimate(
            flops=8 * direction.size * cells_z, bytes_accessed=8 * direction.size, transcendentals=0
        ),
        name="stencil",
    )(direction, before_x, after_x, before_y, after_y, bands)


def update_kernel(now_ref, parts_ref, solution_ref, residual_ref, direction_ref, image_ref, *outs):
    curvature = jnp.sum(parts_ref[:, 0, :1], axis=0, keepdims=True)
    alpha = (now_ref[:1, :1] / curvature)[None]
    outs[0][...] = solution_ref[...] + alpha * direction_ref[...]
    outs[1][...] = residual_ref[...] - alpha * image_ref[...]


def update(now, parts, solution, residual, direction, image):
    brick = pl.BlockSpec((4,) + image.shape[1:], lambda t: (t, 0, 0))
    return pl.pallas_call(
        update_kernel,
        grid=(image.shape[0] // 4,),
        in_specs=[
            pl.BlockSpec(now.shape, lambda t: (0, 0)),
            pl.BlockSpec(parts.shape, lambda t: (0, 0, 0)),
        ]
        + [brick] * 4,
        out_specs=[brick] * 2,
        out_shape=[jax.ShapeDtypeStruct(image.shape, jnp.float32)] * 2,
        compiler_params=pltpu.CompilerParams(vmem_limit_bytes=50 * MIB),
        name="update",
    )(now, parts, solution, residual, direction, image)


def scatter(x):
    return lax.all_to_all(x, both, split_axis=0, concat_axis=0, tiled=True)


def dealt(plan, whole_z):
    columns = whole_z.T.reshape(plan.count, plan.share, plan.cells_z)
    return jnp.swapaxes(columns, 0, 1).reshape(plan.cells_z, plan.cells_z)


def basis_y_blocks(plan, whole_y):
    by_owner = whole_y.reshape(plan.narrow, plan.cells_y, plan.total_y)
    main = by_owner[:, :LANES].reshape(plan.narrow * LANES, plan.total_y)
    rest = by_owner[:, LANES:]
    half = LANES // 2
    sides = [(0, half), (half, 0)]
    mains = jnp.stack([jnp.pad(main, ((0, 0), s)) for s in sides])
    rests = []
    for q in range(plan.group):
        after = LANES - (q + 1) * plan.rest
        padded = jnp.pad(rest, ((0, 0), (q * plan.rest, after), sides[q % 2]))
        rests.append(padded.reshape(plan.narrow * LANES, plan.total_y + half))
    return mains, jnp.stack(rests)


def by_pencils(
    plan,
    solution,
    residual,
    direction,
    previous_product,
    basis_x,
    basis_y,
    basis_z,
    eigen_x,
    eigen_y,
    eigen_z,
):
    whole_z = lax.all_gather(basis_z, "narrow", axis=0, tiled=True)
    turned_z = dealt(plan, whole_z)
    whole_y = lax.all_gather(basis_y, "narrow", axis=0, tiled=True)
    whole_x = lax.all_gather(basis_x, "wide", axis=0, tiled=True)
    sent = [forward_z(plan, k, residual, turned_z) for k in range(2)]
    arrived = [scatter(sent[0])]
    later, whole_x, whole_y = lax.optimization_barrier((sent[1], whole_x, whole_y))
    arrived.append(scatter(later))
    main_y, rest_y = basis_y_blocks(plan, whole_y)
    turned_x = whole_x.T
    index = lax.axis_index("wide") * plan.narrow + lax.axis_index("narrow")
    mine_z = lax.dynamic_slice_in_dim(eigen_z, index * plan.share, plan.share)
    shifts = (mine_z[:, None] + eigen_y[None, :]).reshape(plan.share // 2, 1, 2 * plan.total_y)
    total = jnp.zeros((8, LANES), jnp.float32)
    returned = []
    for k, (start, size) in enumerate(plan.chunks):
        shift = shifts[start // 2 : (start + size) // 2]
        back, total = middle(
            plan,
            k,
            arrived[k],
            whole_x,
            turned_x,
            main_y,
            rest_y,
            eigen_x.reshape(-1, 1),
            shift,
            total,
        )
        returned.append(scatter(back))
    base = inverse_base(plan, 0, returned[0], turned_z)
    inverse = functools.partial(
        inverse_final, plan, 1, returned[1], turned_z, base, direction, previous_product
    )
    ends, now = inverse()
    before_x = shifted(ends[plan.cells_x - HALO :], -1, "wide")
    after_x = shifted(ends[:HALO], 1, "wide")
    direction = inverse(ends)
    image, part = stencil(plan, direction, before_x, after_x)
    solution, residual = update(now, scatter(part), solution, residual, direction, image)
    return solution, residual, direction


def padded_2(x, sides, width):
    for axis, dim in sides:
        count, length = (lax.axis_size(axis), x.shape[dim])
        up = [(i, (i + 1) % count) for i in range(count - 1)]
        down = [(j, i) for i, j in up]
        last = lax.slice_in_dim(x, length - width, length, axis=dim)
        leading = lax.slice_in_dim(x, 0, width, axis=dim)
        before = lax.ppermute(last, axis, up)
        after = lax.ppermute(leading, axis, down)
        x = jnp.concatenate([before, x, after], axis=dim)
    return x


def banded(field, coeffs, axis, length):
    total = coeffs[0] * lax.slice_in_dim(field, 0, length, axis=axis)
    for offset in range(1, 7):
        total = total + coeffs[offset] * lax.slice_in_dim(field, offset, offset + length, axis=axis)
    return total


def apply_padded(padded, length_x, length_y):
    length_z = padded.shape[2]
    along_z = jnp.pad(padded, ((0, 0), (0, 0), (3, 3)))
    mass_z = banded(along_z, mass_band, 2, length_z)
    stiff_z = banded(along_z, stiff_band, 2, length_z)
    first = banded(mass_z, mass_band, 1, length_y)
    second = banded(mass_z, stiff_band, 1, length_y) + banded(stiff_z, mass_band, 1, length_y)
    return banded(first, stiff_band, 0, length_x) + banded(second, mass_band, 0, length_x)


def contract_first(left, right):
    return lax.dot_general(left, right, (((0,), (0,)), ((), ())), precision=highest)


def contract_last(left, right):
    return lax.dot_general(left, right, (((1,), (1,)), ((), ())), precision=highest)


def general(
    solution,
    residual,
    direction,
    previous_product,
    basis_x,
    basis_y,
    basis_z,
    eigen_x,
    eigen_y,
    eigen_z,
):
    whole_x = lax.all_gather(basis_x, "wide", axis=0, tiled=True)
    whole_y, whole_z = (
        lax.all_gather(basis_y, "narrow", axis=0, tiled=True),
        lax.all_gather(basis_z, "narrow", axis=0, tiled=True),
    )
    count_wide = lax.axis_size("wide")
    count_narrow = lax.axis_size("narrow")
    index_wide = lax.axis_index("wide")
    index_narrow = lax.axis_index("narrow")
    cells_x, cells_y, cells_z = residual.shape
    total_x = whole_x.shape[0]
    total_y = whole_y.shape[0]
    product_before = previous_product[0]
    spectral = jnp.dot(residual.reshape(cells_x * cells_y, cells_z), whole_z, precision=highest)
    flat = jnp.transpose(spectral.reshape(cells_x, cells_y, cells_z), (1, 2, 0)).reshape(
        cells_y, cells_z * cells_x
    )
    pencil = contract_first(
        whole_y, lax.all_to_all(flat, "narrow", split_axis=1, concat_axis=0, tiled=True)
    )
    rows_y = total_y // count_wide
    part_z = cells_z // count_narrow
    moved = lax.all_to_all(pencil, "wide", split_axis=0, concat_axis=1, tiled=True)
    lined = jnp.transpose(moved.reshape(rows_y, count_wide, part_z, cells_x), (0, 2, 1, 3))
    lined = lined.reshape(rows_y * part_z, total_x)
    spectral_x = jnp.dot(lined, whole_x, precision=highest)
    shift_y = lax.dynamic_slice_in_dim(eigen_y, index_wide * rows_y, rows_y)
    shift_z = lax.dynamic_slice_in_dim(eigen_z, index_narrow * part_z, part_z)
    shift_yz = (shift_y[:, None] + shift_z[None, :]).reshape(rows_y * part_z, 1)
    scaled = spectral_x / (eigen_x[None, :] + shift_yz)
    inverse_x = contract_last(scaled, whole_x)
    unlined = jnp.transpose(inverse_x.reshape(rows_y, part_z, count_wide, cells_x), (0, 2, 1, 3))
    unlined = unlined.reshape(rows_y, count_wide * part_z * cells_x)
    pencil = lax.all_to_all(unlined, "wide", split_axis=1, concat_axis=0, tiled=True)
    pencil = jnp.dot(whole_y, pencil, precision=highest)
    back = lax.all_to_all(pencil, "narrow", split_axis=0, concat_axis=1, tiled=True)
    brick = jnp.transpose(back.reshape(cells_y, cells_z, cells_x), (2, 0, 1))
    result = contract_last(brick.reshape(cells_x * cells_y, cells_z), whole_z)
    precond = result.reshape(cells_x, cells_y, cells_z)
    product_now = lax.psum(jnp.sum(residual * precond), ("wide", "narrow"))
    direction = precond + product_now / product_before * direction
    padded = padded_2(direction, (("wide", 0), ("narrow", 1)), 3)
    image = apply_padded(padded, cells_x, cells_y)
    curvature = lax.psum(jnp.sum(direction * image), ("wide", "narrow"))
    alpha = product_now / curvature
    solution = solution + alpha * direction
    residual = residual - alpha * image
    return (solution, residual, direction)


def per_device(*arrays):
    residual, basis_x, basis_y = arrays[1], arrays[4], arrays[5]
    wide, narrow = lax.axis_size("wide"), lax.axis_size("narrow")
    plan = Plan(*residual.shape, basis_x.shape[1], basis_y.shape[1], wide, narrow)
    if plan.fits:
        return by_pencils(plan, *arrays)
    return general(*arrays)


def solution(mesh):
    placed = (
        P("wide", "narrow", None),
        P("wide", "narrow", None),
        P("wide", "narrow", None),
        P(),
        P("wide", None),
        P("narrow", None),
        P("narrow", None),
        P(),
        P(),
        P(),
    )
    return jax.shard_map(
        per_device,
        mesh=mesh,
        in_specs=placed,
        out_specs=(P("wide", "narrow", None), P("wide", "narrow", None), P("wide", "narrow", None)),
        check_vma=False,
    )
```

```python
import functools

import jax
import jax.numpy as jnp
import ml_dtypes
import numpy as np
from jax import lax
from jax.experimental import pallas as pl
from jax.experimental.pallas import tpu as pltpu
from jax.sharding import PartitionSpec as P

mass_band = (
    1.0 / 5040.0,
    1.0 / 42.0,
    397.0 / 1680.0,
    151.0 / 315.0,
    397.0 / 1680.0,
    1.0 / 42.0,
    1.0 / 5040.0,
)
stiff_band = (-1.0 / 120.0, -0.2, -0.125, 2.0 / 3.0, -0.125, -0.2, -1.0 / 120.0)
highest = lax.Precision.HIGHEST
LANES = 128
HALO = 3
EDGE = 8
both = ("wide", "narrow")
MIB = 1024 * 1024


def split(x):
    high = x.astype(jnp.bfloat16)
    low = (x - high.astype(jnp.float32)).astype(jnp.bfloat16)
    return high, low


def dot3(left, right, over):
    dims = ((over[:1], over[1:]), ((), ()))
    one = functools.partial(
        lax.dot_general, dimension_numbers=dims, preferred_element_type=jnp.float32
    )
    return one(left[0], right[0]) + one(left[1], right[0]) + one(left[0], right[1])


class Plan:
    def __init__(self, cells_x, cells_y, cells_z, total_x, total_y, wide, narrow):
        self.cells_x, self.cells_y, self.cells_z = cells_x, cells_y, cells_z
        self.total_x, self.total_y = total_x, total_y
        self.wide, self.narrow, self.count = wide, narrow, wide * narrow
        self.rest = cells_y - LANES
        self.fits = (
            cells_z % self.count == 0
            and cells_x % 8 == 0
            and self.rest > 0
            and LANES % self.rest == 0
            and self.rest < LANES
            and total_y % LANES == LANES // 2
            and wide % 2 == 0
            and (total_x // 2) % 16 == 0
            and self.count % 8 == 0
        )
        if not self.fits:
            return
        self.share = cells_z // self.count
        self.group = LANES // self.rest
        self.tiles = cells_x // 8
        self.chunks = [(0, self.group), (self.group, self.share - self.group)]
        self.fits = (
            self.group % 2 == 0
            and self.share % 2 == 0
            and self.share > self.group
            and self.share % self.group != 0
            and self.tiles >= 3
            and 2 * LANES < cells_z <= 3 * LANES
        )
        if self.fits:
            _, _, _, _, fit, width = self.shape_of(1)
            self.fits = self.tiles % fit != 0 or fit * width < LANES

    def rows(self, chunk):
        start, size = self.chunks[chunk]
        return start * self.count, size * self.count

    def shape_of(self, chunk):
        size = self.chunks[chunk][1]
        part = size % self.group
        width = part * self.rest
        fit = LANES // width if part else 1
        tails = -(-self.tiles // fit) if part else 0
        return size, size + size // self.group, part, tails, fit, width

    def message(self, chunk):
        _, per, _, tails, _, _ = self.shape_of(chunk)
        return (self.count, self.tiles * per + tails, 8, LANES)


def forward_kernel(plan, chunk, field_ref, basis_ref, out_ref, high_ref, low_ref, stage_ref):
    size, per, part, tails, fit, width = plan.shape_of(chunk)
    step = pl.program_id(0)

    @pl.when(step == 0)
    def _():
        high_ref[...], low_ref[...] = split(basis_ref[...])
        if tails:
            out_ref[:, plan.tiles * per :] = jnp.zeros((plan.count, tails, 8, LANES), jnp.float32)

    basis = (high_ref[...], low_ref[...])
    for i in range(8):
        stage_ref[i] = dot3(basis, split(field_ref[i]), (1, 1))
    base = step * per if tails else 0
    rests = []
    for j in range(size):
        at = j * plan.count
        turned = jnp.swapaxes(stage_ref[:, at : at + plan.count, :], 0, 1)
        out_ref[:, base + j] = turned[:, :, :LANES]
        rests.append(turned[:, :, LANES:])
    for piece in range(size // plan.group):
        some = rests[piece * plan.group : (piece + 1) * plan.group]
        out_ref[:, base + size + piece] = jnp.concatenate(some, axis=2)
    if tails:
        some = jnp.concatenate(rests[size - part :], axis=2)
        for place in range(fit):

            @pl.when(step % fit == place)
            def _():
                lanes = slice(place * width, (place + 1) * width)
                out_ref[:, plan.tiles * per + step // fit, :, lanes] = some


def forward_z(plan, chunk, field, basis):
    start, rows = plan.rows(chunk)
    basis = basis[start : start + rows]
    message = plan.message(chunk)
    _, per, _, tails, _, _ = plan.shape_of(chunk)
    if tails:
        out_spec = pl.BlockSpec(message, lambda t: (0, 0, 0, 0))
    else:
        out_spec = pl.BlockSpec((message[0], per) + message[2:], lambda t: (0, t, 0, 0))
    return pl.pallas_call(
        functools.partial(forward_kernel, plan, chunk),
        grid=(plan.tiles,),
        in_specs=[
            pl.BlockSpec((8, plan.cells_y, plan.cells_z), lambda t: (t, 0, 0)),
            pl.BlockSpec(basis.shape, lambda t: (0, 0)),
        ],
        out_specs=out_spec,
        out_shape=jax.ShapeDtypeStruct(message, jnp.float32),
        scratch_shapes=[
            pltpu.VMEM(basis.shape, jnp.bfloat16),
            pltpu.VMEM(basis.shape, jnp.bfloat16),
            pltpu.VMEM((8, rows, plan.cells_y), jnp.float32),
        ],
        compiler_params=pltpu.CompilerParams(vmem_limit_bytes=50 * MIB),
        cost_estimate=pl.CostEstimate(
            flops=6 * field.size * rows, bytes_accessed=8 * field.size, transcendentals=0
        ),
        name="forward_z",
    )(field, basis)


def add_chunk(plan, chunk, tile, part_ref, tail_ref, stage_ref):
    size, _, part, tails, fit, width = plan.shape_of(chunk)
    if tails:
        tail = tail_ref[:, 0]
        for place in range(1, fit):
            turned = pltpu.roll(tail_ref[:, 0], LANES - place * width, 2)
            tail = jnp.where(tile % fit == place, turned, tail)
    for j in range(size):
        at, q = j * plan.count, j % plan.group
        lanes = slice(q * plan.rest, (q + 1) * plan.rest)
        stage_ref[:, at : at + plan.count, :LANES] = jnp.swapaxes(part_ref[:, j], 0, 1)
        if j < size - part:
            rest = part_ref[:, size + j // plan.group, :, lanes]
        else:
            rest = tail[:, :, lanes]
        stage_ref[:, at : at + plan.count, LANES:] = jnp.swapaxes(rest, 0, 1)


def base_kernel(plan, chunk, part_ref, basis_ref, out_ref, high_ref, low_ref, stage_ref):
    step = pl.program_id(0)

    @pl.when(step == 0)
    def _():
        high_ref[...], low_ref[...] = split(basis_ref[...])

    add_chunk(plan, chunk, step, part_ref, None, stage_ref)
    basis = (high_ref[...], low_ref[...])
    for i in range(8):
        out_ref[i] = dot3(split(stage_ref[i].T), basis, (1, 0))


def final_kernel(plan, chunk, ends, pick, *refs):
    part_ref, tail_ref, last_ref, basis_ref, base_ref, old_ref, before_ref = refs[:7]
    if ends:
        out_ref, now_ref, high_ref, low_ref, stage_ref = refs[7:]
    else:
        _, out_ref, high_ref, low_ref, stage_ref = refs[7:]
    step = pl.program_id(0)

    @pl.when(step == 0)
    def _():
        high_ref[...], low_ref[...] = split(basis_ref[...])

    def work():
        add_chunk(plan, chunk, pick(step), part_ref, tail_ref, stage_ref)
        now = jnp.sum(last_ref[:, 0, 0, LANES - 1 :], axis=0, keepdims=True)
        beta = now / before_ref[...]
        basis = (high_ref[...], low_ref[...])
        for i in range(8):
            value = dot3(split(stage_ref[i].T), basis, (1, 0))
            out_ref[i] = base_ref[i] + value + beta * old_ref[i]
        if ends:
            now_ref[...] = jnp.broadcast_to(now, now_ref.shape)

    work()


def inverse_scratch(plan, basis):
    return [
        pltpu.VMEM(basis.shape, jnp.bfloat16),
        pltpu.VMEM(basis.shape, jnp.bfloat16),
        pltpu.VMEM((8, basis.shape[0], plan.cells_y), jnp.float32),
    ]


def inverse_cost(plan, basis, tiles):
    size = tiles * 8 * plan.cells_y * plan.cells_z
    return pl.CostEstimate(
        flops=6 * size * basis.shape[0], bytes_accessed=12 * size, transcendentals=0
    )


def inverse_base(plan, chunk, part, basis):
    start, rows = plan.rows(chunk)
    per = plan.shape_of(chunk)[1]
    basis = basis[start : start + rows]
    return pl.pallas_call(
        functools.partial(base_kernel, plan, chunk),
        grid=(plan.tiles,),
        in_specs=[
            pl.BlockSpec((plan.count, per, 8, LANES), lambda t: (0, t, 0, 0)),
            pl.BlockSpec(basis.shape, lambda t: (0, 0)),
        ],
        out_specs=pl.BlockSpec((8, plan.cells_y, plan.cells_z), lambda t: (t, 0, 0)),
        out_shape=jax.ShapeDtypeStruct((plan.cells_x, plan.cells_y, plan.cells_z), jnp.float32),
        scratch_shapes=inverse_scratch(plan, basis),
        compiler_params=pltpu.CompilerParams(vmem_limit_bytes=50 * MIB),
        cost_estimate=inverse_cost(plan, basis, plan.tiles),
        name="inverse_base",
    )(part, basis)


def inverse_final(plan, chunk, part, basis, base, old, before, done=None):
    ends = done is None
    start, rows = plan.rows(chunk)
    basis = basis[start : start + rows]
    last = plan.tiles - 1
    if ends:
        pick = lambda t: t * last
    else:
        pick = lambda t: t + 1
    tile = (8, plan.cells_y, plan.cells_z)
    brick = pl.BlockSpec(tile, lambda t: (pick(t), 0, 0))
    _, per, _, _, fit, _ = plan.shape_of(chunk)
    in_specs = [
        pl.BlockSpec((plan.count, per, 8, LANES), lambda t: (0, pick(t), 0, 0)),
        pl.BlockSpec(
            (plan.count, 1, 8, LANES), lambda t: (0, plan.tiles * per + pick(t) // fit, 0, 0)
        ),
        pl.BlockSpec((plan.count, 1, 8, LANES), lambda t: (0, part.shape[1] - 1, 0, 0)),
        pl.BlockSpec(basis.shape, lambda t: (0, 0)),
        brick,
        brick,
        pl.BlockSpec((1, 1), lambda t: (0, 0)),
    ]
    operands = [part, part, part, basis, base, old, before.reshape(1, 1)]
    out_specs = brick
    if ends:
        out_specs = [out_specs, pl.BlockSpec((8, LANES), lambda t: (0, 0))]
        out_shape = [
            jax.ShapeDtypeStruct(base.shape, jnp.float32),
            jax.ShapeDtypeStruct((8, LANES), jnp.float32),
        ]
    else:
        in_specs.append(pl.BlockSpec(memory_space=pl.ANY))
        operands.append(done)
        out_shape = jax.ShapeDtypeStruct(base.shape, jnp.float32)
    return pl.pallas_call(
        functools.partial(final_kernel, plan, chunk, ends, pick),
        grid=(2 if ends else plan.tiles - 2,),
        input_output_aliases={} if ends else {len(operands) - 1: 0},
        in_specs=in_specs,
        out_specs=out_specs,
        out_shape=out_shape,
        scratch_shapes=inverse_scratch(plan, basis),
        compiler_params=pltpu.CompilerParams(vmem_limit_bytes=50 * MIB),
        cost_estimate=inverse_cost(plan, basis, 2 if ends else plan.tiles - 2),
        name="inverse_ends" if ends else "inverse_inner",
    )(*operands)


def middle_kernel(plan, chunk, *refs):
    (
        in_ref,
        basis_x_ref,
        turned_x_ref,
        main_y_ref,
        rest_y_ref,
        eigen_x_ref,
        shift_ref,
        total_ref,
        out_ref,
        sum_ref,
        bx_high,
        bx_low,
        tx_high,
        tx_low,
        my_high,
        my_low,
        ry_high,
        ry_low,
        u_high,
        u_low,
        q_high,
        q_low,
        rest_acc,
    ) = refs
    size, per, part, tails, fit, lanes = plan.shape_of(chunk)
    full = size // plan.group
    last = chunk == len(plan.chunks) - 1
    wide, narrow, tiles = plan.wide, plan.narrow, plan.tiles
    half = plan.total_x // 2
    lump = wide // 2
    span = plan.total_y + LANES // 2
    width = 2 * plan.total_y
    bx_high[...], bx_low[...] = split(basis_x_ref[...])
    tx_high[...], tx_low[...] = split(turned_x_ref[...])
    my_high[...], my_low[...] = split(main_y_ref[...])
    ry_high[...], ry_low[...] = split(rest_y_ref[...])
    rest_acc[...] = jnp.zeros_like(rest_acc)

    def gathered(h, places):
        rows = pl.ds(h * lump, lump)
        sides = []
        for n in range(narrow):
            some = []
            for t in range(tiles):
                piece, turn = places(t)
                value = in_ref[rows, n, piece]
                some.append(pltpu.roll(value, LANES - turn, 2) if turn else value)
            sides.append(jnp.stack(some, axis=1).reshape(half, LANES))
        return jnp.concatenate(sides, axis=1)

    def pair(in_tail, p, total):
        for h in range(2):
            if in_tail:
                rest = gathered(h, lambda t: (tiles * per + t // fit, t % fit * lanes))
            else:
                rest = gathered(h, lambda t: (t * per + size + 2 * p // plan.group, 0))
            rest = split(rest)
            parts = []
            for s in range(2):
                j = 2 * p + s
                q = lax.rem(j, plan.group)
                parts.append(
                    dot3(split(gathered(h, lambda t: (t * per + j, 0))), (my_high[s], my_low[s]), (1, 0))
                    + dot3(rest, (ry_high[q], ry_low[q]), (1, 0))
                )
            cut = span - LANES
            joined = jnp.concatenate(
                [
                    parts[0][:, :cut],
                    parts[0][:, cut:] + parts[1][:, :LANES],
                    parts[1][:, LANES:],
                ],
                axis=1,
            )
            rows = pl.ds(h * half, half)
            u_high[rows, :], u_low[rows, :] = split(joined)
        shift = shift_ref[p]
        for h in range(2):
            rows = pl.ds(h * half, half)
            spectral = dot3(
                (tx_high[rows, :], tx_low[rows, :]), (u_high[...], u_low[...]), (1, 0)
            )
            scaled = spectral / (eigen_x_ref[rows, :] + shift)
            total = total + jnp.sum((spectral * scaled).reshape(half // 8, 8, width), axis=0)
            q_high[rows, :], q_low[rows, :] = split(scaled)
        for h in range(2):
            rows = pl.ds(h * half, half)
            value = dot3((bx_high[rows, :], bx_low[rows, :]), (q_high[...], q_low[...]), (1, 0))
            for s in range(2):
                j = 2 * p + s
                mine = split(value[:, s * (width - span) : s * (width - span) + span])
                main = dot3(mine, (my_high[s], my_low[s]), (1, 1))
                q = lax.rem(j, plan.group)
                rest_acc[2 * p // plan.group, rows, :] += dot3(
                    mine, (ry_high[q], ry_low[q]), (1, 1)
                )
                for n in range(narrow):
                    side = main[:, n * LANES : (n + 1) * LANES].reshape(lump, tiles, 8, LANES)
                    for t in range(tiles):
                        out_ref[pl.ds(h * lump, lump), n, t * per + j] = side[:, t]
        return total

    total = jnp.zeros((8, width), jnp.float32)
    total = lax.fori_loop(0, (size - part) // 2, functools.partial(pair, False), total)
    if tails:
        total = lax.fori_loop((size - part) // 2, size // 2, functools.partial(pair, True), total)
    value = total_ref[...] + jnp.sum(total)
    sum_ref[...] = value
    for n in range(narrow):
        side = slice(n * LANES, (n + 1) * LANES)
        for piece in range(full):
            rest = rest_acc[piece, :, side].reshape(wide, tiles, 8, LANES)
            for t in range(tiles):
                out_ref[:, n, t * per + size + piece] = rest[:, t]
        for tail in range(tails):
            rest = rest_acc[full, :, side].reshape(wide, tiles, 8, LANES)
            joined = rest[:, tail * fit]
            for t in range(tail * fit + 1, min(tail * fit + fit, tiles)):
                joined = joined + pltpu.roll(rest[:, t], t % fit * lanes, 2)
            if last and tail == tails - 1:
                lane = lax.broadcasted_iota(jnp.int32, joined.shape, 2)
                joined = jnp.where(lane == LANES - 1, value[:1, :][None], joined)
            out_ref[:, n, tiles * per + tail] = joined


def middle(plan, chunk, message, basis_x, turned_x, main_y, rest_y, eigen_x, shift, total):
    size = plan.chunks[chunk][1]
    pieces = -(-size // plan.group)
    shape = (plan.wide, plan.narrow) + message.shape[1:]
    square = (plan.total_x, plan.total_x)
    pencil = (plan.total_x, 2 * plan.total_y)
    half = jnp.bfloat16
    out, total = pl.pallas_call(
        functools.partial(middle_kernel, plan, chunk),
        out_shape=[
            jax.ShapeDtypeStruct(shape, jnp.float32),
            jax.ShapeDtypeStruct((8, LANES), jnp.float32),
        ],
        in_specs=[pl.BlockSpec(memory_space=pltpu.VMEM)] * 8,
        out_specs=[pl.BlockSpec(memory_space=pltpu.VMEM)] * 2,
        scratch_shapes=[
            pltpu.VMEM(square, half),
            pltpu.VMEM(square, half),
            pltpu.VMEM(square, half),
            pltpu.VMEM(square, half),
            pltpu.VMEM(main_y.shape, half),
            pltpu.VMEM(main_y.shape, half),
            pltpu.VMEM(rest_y.shape, half),
            pltpu.VMEM(rest_y.shape, half),
            pltpu.VMEM(pencil, half),
            pltpu.VMEM(pencil, half),
            pltpu.VMEM(pencil, half),
            pltpu.VMEM(pencil, half),
            pltpu.VMEM((pieces, plan.total_x, plan.narrow * LANES), jnp.float32),
        ],
        compiler_params=pltpu.CompilerParams(vmem_limit_bytes=44 * MIB),
        cost_estimate=pl.CostEstimate(
            flops=12 * size * plan.total_x * plan.total_y * (plan.total_x + plan.total_y),
            bytes_accessed=8 * message.size,
            transcendentals=0,
        ),
        name="middle",
    )(message.reshape(shape), basis_x, turned_x, main_y, rest_y, eigen_x, shift, total)
    return out.reshape(message.shape), total


def shifted(x, step, axis):
    count = lax.axis_size(axis)
    pairs = [(i + step, i) for i in range(count) if 0 <= i + step < count]
    return lax.ppermute(x, axis, pairs)


def from_sides(low, high, axis):
    if lax.axis_size(axis) != 2:
        return shifted(high, -1, axis), shifted(low, 1, axis)
    second = lax.axis_index(axis) == 1
    got = lax.ppermute(jnp.where(second, low, high), axis, [(0, 1), (1, 0)])
    return jnp.where(second, got, 0.0), jnp.where(second, 0.0, got)


mass_scale, stiff_scale = 5040.0, 120.0
CUT = LANES + LANES // 2
GROUP = 4


def band_matrices(cells_z):
    offset = np.arange(cells_z)[:, None] - np.arange(cells_z)[None, :]
    near = np.abs(offset) <= HALO
    tables = []
    for band, scale in ((mass_band, mass_scale), (stiff_band, stiff_scale)):
        whole = np.rint(np.asarray(band) * scale)
        full = np.where(near, whole[np.clip(offset + HALO, 0, 2 * HALO)], 0.0)
        first = np.zeros((2 * LANES, 2 * LANES))
        first[:, :CUT] = full[: 2 * LANES, :CUT]
        second = np.zeros((2 * LANES, 2 * LANES))
        second[: cells_z - LANES, CUT - LANES : cells_z - LANES] = full[LANES:, CUT:]
        tables.append(np.stack([first, second]).astype(np.float32))
    mass, stiff = tables
    high = mass.astype(ml_dtypes.bfloat16)
    low = (mass - high.astype(np.float32)).astype(ml_dtypes.bfloat16)
    stiff = stiff.astype(ml_dtypes.bfloat16)
    mixed = np.concatenate([high, high, low, stiff, stiff], axis=1)
    return mixed, np.concatenate([high, high, low], axis=1)


def stencil_kernel(plan, *refs):
    own, before_x, after_x, before_y, after_y, mixed_ref, mass_ref, image_ref, sum_ref = refs[:9]
    field, f_high, f_low, s_high, s_low, h_a, h_b, total, sems = refs[9:]
    cells_x, cells_y, cells_z = plan.cells_x, plan.cells_y, plan.cells_z
    tiles = plan.tiles
    padded_y = cells_y + 2 * EDGE
    own_y = pl.ds(EDGE, cells_y)
    step = pl.program_id(0)

    def tile_copy(t):
        return pltpu.make_async_copy(
            own.at[pl.ds(8 * t, 8)], field.at[pl.ds(HALO + 8 * t, 8), own_y, :], sems.at[t]
        )

    first_copy = pltpu.make_async_copy(
        before_x, field.at[pl.ds(0, HALO), own_y, :], sems.at[tiles]
    )
    last_copy = pltpu.make_async_copy(
        after_x, field.at[pl.ds(HALO + cells_x, HALO), own_y, :], sems.at[tiles + 1]
    )

    @pl.when(step == 0)
    def _():
        first_copy.start()
        for t in range(tiles):
            tile_copy(t).start()
        last_copy.start()
        total[...] = jnp.zeros_like(total)
        for ref in (f_high, f_low, s_high, s_low):
            ref[:, cells_z:] = jnp.zeros((ref.shape[0], ref.shape[1] - cells_z), ref.dtype)
        field[:, EDGE - HALO : EDGE, :] = jnp.swapaxes(before_y[...], 0, 1)
        field[:, EDGE + cells_y : EDGE + cells_y + HALO, :] = jnp.swapaxes(after_y[...], 0, 1)
        first_copy.wait()
        tile_copy(0).wait()

    @pl.when(step < tiles - 1)
    def _():
        tile_copy(step + 1).wait()

    @pl.when(step == tiles - 1)
    def _():
        last_copy.wait()

    blocks = h_a.shape[0]
    ratio = stiff_scale / mass_scale

    def one(left, right):
        return lax.dot_general(
            left, right, (((1,), (0,)), ((), ())), preferred_element_type=jnp.float32
        )

    def planes(g, carry):
        for i in range(GROUP):
            x = step * 8 + g * GROUP + i
            middle_plane = field[x + HALO]
            first = ratio * stiff_band[HALO] * middle_plane
            second = mass_band[HALO] * middle_plane
            for o in range(1, HALO + 1):
                around = field[x + HALO - o] + field[x + HALO + o]
                first = first + ratio * stiff_band[HALO + o] * around
                second = second + mass_band[HALO + o] * around
            rows = pl.ds(i * padded_y, padded_y)
            f_high[rows, :cells_z], f_low[rows, :cells_z] = split(first)
            s_high[rows, :cells_z], s_low[rows, :cells_z] = split(second)
        window_a, window_b = [], []
        for w in range(2):
            lanes = pl.ds(w * LANES, 2 * LANES)
            fh, fl, sh, sl = (ref[:, lanes] for ref in (f_high, f_low, s_high, s_low))
            window_a.append(one(jnp.concatenate([fh, fl, fh, sh, sl], axis=1), mixed_ref[w]))
            window_b.append(one(jnp.concatenate([sh, sl, sh], axis=1), mass_ref[w]))
        for ref, (left, right) in ((h_a, window_a), (h_b, window_b)):
            ref[0] = left[:, :LANES]
            ref[1] = left[:, LANES:] + right[:, :LANES]
            ref[2] = right[:, LANES:]
        for i in range(GROUP):
            plane = g * GROUP + i
            for k in range(blocks):
                lanes = min(LANES, cells_z - k * LANES)
                at = lambda ref, o: ref[k, pl.ds(i * padded_y + EDGE + o, cells_y), :]
                image = (mass_band[HALO] / stiff_scale) * at(h_a, 0)
                image = image + (stiff_band[HALO] / mass_scale) * at(h_b, 0)
                for o in range(1, HALO + 1):
                    image = image + (mass_band[HALO + o] / stiff_scale) * (at(h_a, -o) + at(h_a, o))
                    image = image + (stiff_band[HALO + o] / mass_scale) * (at(h_b, -o) + at(h_b, o))
                here = pl.ds(k * LANES, lanes)
                image_ref[plane, :, here] = image[:, :lanes]
                product = image[:, :lanes] * field[step * 8 + plane + HALO, own_y, here]
                total[:, here] += jnp.sum(product.reshape(cells_y // 8, 8, lanes), axis=0)
        return carry

    lax.fori_loop(0, 8 // GROUP, planes, 0)

    @pl.when(step == pl.num_programs(0) - 1)
    def _():
        sum_ref[...] = jnp.full(sum_ref.shape, jnp.sum(total[...]), jnp.float32)


def stencil(plan, direction, before_x, after_x):
    cells_x, cells_y, cells_z = direction.shape

    def strip(rows):
        parts = [jnp.swapaxes(v[:, rows], 0, 1) for v in (before_x, direction, after_x)]
        return jnp.concatenate(parts, axis=1)

    before_y, after_y = from_sides(
        strip(slice(0, HALO)), strip(slice(cells_y - HALO, cells_y)), "narrow"
    )
    mixed, mass = band_matrices(cells_z)
    padded_y = cells_y + 2 * EDGE
    blocks = -(-cells_z // LANES)
    lump = (GROUP * padded_y, blocks * LANES)
    return pl.pallas_call(
        functools.partial(stencil_kernel, plan),
        grid=(cells_x // 8,),
        in_specs=[pl.BlockSpec(memory_space=pl.ANY)] * 3
        + [pl.BlockSpec(before_y.shape, lambda t: (0, 0, 0))] * 2
        + [pl.BlockSpec(v.shape, lambda t: (0, 0, 0)) for v in (mixed, mass)],
        out_specs=[
            pl.BlockSpec((8, cells_y, cells_z), lambda t: (t, 0, 0)),
            pl.BlockSpec((plan.count, 8, LANES), lambda t: (0, 0, 0)),
        ],
        out_shape=[
            jax.ShapeDtypeStruct(direction.shape, jnp.float32),
            jax.ShapeDtypeStruct((plan.count, 8, LANES), jnp.float32),
        ],
        scratch_shapes=[
            pltpu.VMEM((cells_x + 2 * HALO, padded_y, cells_z), jnp.float32),
            pltpu.VMEM(lump, jnp.bfloat16),
            pltpu.VMEM(lump, jnp.bfloat16),
            pltpu.VMEM(lump, jnp.bfloat16),
            pltpu.VMEM(lump, jnp.bfloat16),
            pltpu.VMEM((blocks, GROUP * padded_y, LANES), jnp.float32),
            pltpu.VMEM((blocks, GROUP * padded_y, LANES), jnp.float32),
            pltpu.VMEM((8, cells_z), jnp.float32),
            pltpu.SemaphoreType.DMA((plan.tiles + 2,)),
        ],
        compiler_params=pltpu.CompilerParams(vmem_limit_bytes=50 * MIB),
        cost_estimate=pl.CostEstimate(
            flops=8 * direction.size * cells_z, bytes_accessed=8 * direction.size, transcendentals=0
        ),
        name="stencil",
    )(direction, before_x, after_x, before_y, after_y, mixed, mass)


def update_kernel(now_ref, parts_ref, solution_ref, residual_ref, direction_ref, image_ref, *outs):
    curvature = jnp.sum(parts_ref[:, 0, :1], axis=0, keepdims=True)
    alpha = (now_ref[:1, :1] / curvature)[None]
    outs[0][...] = solution_ref[...] + alpha * direction_ref[...]
    outs[1][...] = residual_ref[...] - alpha * image_ref[...]


def update(now, parts, solution, residual, direction, image):
    brick = pl.BlockSpec((4,) + image.shape[1:], lambda t: (t, 0, 0))
    return pl.pallas_call(
        update_kernel,
        grid=(image.shape[0] // 4,),
        in_specs=[
            pl.BlockSpec(now.shape, lambda t: (0, 0)),
            pl.BlockSpec(parts.shape, lambda t: (0, 0, 0)),
        ]
        + [brick] * 4,
        out_specs=[brick] * 2,
        out_shape=[jax.ShapeDtypeStruct(image.shape, jnp.float32)] * 2,
        compiler_params=pltpu.CompilerParams(vmem_limit_bytes=50 * MIB),
        name="update",
    )(now, parts, solution, residual, direction, image)


def scatter(x):
    return lax.all_to_all(x, both, split_axis=0, concat_axis=0, tiled=True)


def dealt(plan, whole_z):
    columns = whole_z.T.reshape(plan.count, plan.share, plan.cells_z)
    return jnp.swapaxes(columns, 0, 1).reshape(plan.cells_z, plan.cells_z)


def basis_y_blocks(plan, whole_y):
    by_owner = whole_y.reshape(plan.narrow, plan.cells_y, plan.total_y)
    main = by_owner[:, :LANES].reshape(plan.narrow * LANES, plan.total_y)
    rest = by_owner[:, LANES:]
    half = LANES // 2
    sides = [(0, half), (half, 0)]
    mains = jnp.stack([jnp.pad(main, ((0, 0), s)) for s in sides])
    rests = []
    for q in range(plan.group):
        after = LANES - (q + 1) * plan.rest
        padded = jnp.pad(rest, ((0, 0), (q * plan.rest, after), sides[q % 2]))
        rests.append(padded.reshape(plan.narrow * LANES, plan.total_y + half))
    return mains, jnp.stack(rests)


def by_pencils(
    plan,
    solution,
    residual,
    direction,
    previous_product,
    basis_x,
    basis_y,
    basis_z,
    eigen_x,
    eigen_y,
    eigen_z,
):
    whole_z = lax.all_gather(basis_z, "narrow", axis=0, tiled=True)
    turned_z = dealt(plan, whole_z)
    whole_y = lax.all_gather(basis_y, "narrow", axis=0, tiled=True)
    whole_x = lax.all_gather(basis_x, "wide", axis=0, tiled=True)
    sent = [forward_z(plan, k, residual, turned_z) for k in range(2)]
    arrived = [scatter(sent[0])]
    later, whole_x, whole_y = lax.optimization_barrier((sent[1], whole_x, whole_y))
    arrived.append(scatter(later))
    main_y, rest_y = basis_y_blocks(plan, whole_y)
    turned_x = whole_x.T
    index = lax.axis_index("wide") * plan.narrow + lax.axis_index("narrow")
    mine_z = lax.dynamic_slice_in_dim(eigen_z, index * plan.share, plan.share)
    shifts = (mine_z[:, None] + eigen_y[None, :]).reshape(plan.share // 2, 1, 2 * plan.total_y)
    total = jnp.zeros((8, LANES), jnp.float32)
    returned = []
    for k, (start, size) in enumerate(plan.chunks):
        shift = shifts[start // 2 : (start + size) // 2]
        back, total = middle(
            plan,
            k,
            arrived[k],
            whole_x,
            turned_x,
            main_y,
            rest_y,
            eigen_x.reshape(-1, 1),
            shift,
            total,
        )
        returned.append(scatter(back))
    base = inverse_base(plan, 0, returned[0], turned_z)
    inverse = functools.partial(
        inverse_final, plan, 1, returned[1], turned_z, base, direction, previous_product
    )
    ends, now = inverse()
    before_x = shifted(ends[plan.cells_x - HALO :], -1, "wide")
    after_x = shifted(ends[:HALO], 1, "wide")
    direction = inverse(ends)
    image, part = stencil(plan, direction, before_x, after_x)
    solution, residual = update(now, scatter(part), solution, residual, direction, image)
    return solution, residual, direction


def padded_2(x, sides, width):
    for axis, dim in sides:
        count, length = (lax.axis_size(axis), x.shape[dim])
        up = [(i, (i + 1) % count) for i in range(count - 1)]
        down = [(j, i) for i, j in up]
        last = lax.slice_in_dim(x, length - width, length, axis=dim)
        leading = lax.slice_in_dim(x, 0, width, axis=dim)
        before = lax.ppermute(last, axis, up)
        after = lax.ppermute(leading, axis, down)
        x = jnp.concatenate([before, x, after], axis=dim)
    return x


def banded(field, coeffs, axis, length):
    total = coeffs[0] * lax.slice_in_dim(field, 0, length, axis=axis)
    for offset in range(1, 7):
        total = total + coeffs[offset] * lax.slice_in_dim(field, offset, offset + length, axis=axis)
    return total


def apply_padded(padded, length_x, length_y):
    length_z = padded.shape[2]
    along_z = jnp.pad(padded, ((0, 0), (0, 0), (3, 3)))
    mass_z = banded(along_z, mass_band, 2, length_z)
    stiff_z = banded(along_z, stiff_band, 2, length_z)
    first = banded(mass_z, mass_band, 1, length_y)
    second = banded(mass_z, stiff_band, 1, length_y) + banded(stiff_z, mass_band, 1, length_y)
    return banded(first, stiff_band, 0, length_x) + banded(second, mass_band, 0, length_x)


def contract_first(left, right):
    return lax.dot_general(left, right, (((0,), (0,)), ((), ())), precision=highest)


def contract_last(left, right):
    return lax.dot_general(left, right, (((1,), (1,)), ((), ())), precision=highest)


def general(
    solution,
    residual,
    direction,
    previous_product,
    basis_x,
    basis_y,
    basis_z,
    eigen_x,
    eigen_y,
    eigen_z,
):
    whole_x = lax.all_gather(basis_x, "wide", axis=0, tiled=True)
    whole_y, whole_z = (
        lax.all_gather(basis_y, "narrow", axis=0, tiled=True),
        lax.all_gather(basis_z, "narrow", axis=0, tiled=True),
    )
    count_wide = lax.axis_size("wide")
    count_narrow = lax.axis_size("narrow")
    index_wide = lax.axis_index("wide")
    index_narrow = lax.axis_index("narrow")
    cells_x, cells_y, cells_z = residual.shape
    total_x = whole_x.shape[0]
    total_y = whole_y.shape[0]
    product_before = previous_product[0]
    spectral = jnp.dot(residual.reshape(cells_x * cells_y, cells_z), whole_z, precision=highest)
    flat = jnp.transpose(spectral.reshape(cells_x, cells_y, cells_z), (1, 2, 0)).reshape(
        cells_y, cells_z * cells_x
    )
    pencil = contract_first(
        whole_y, lax.all_to_all(flat, "narrow", split_axis=1, concat_axis=0, tiled=True)
    )
    rows_y = total_y // count_wide
    part_z = cells_z // count_narrow
    moved = lax.all_to_all(pencil, "wide", split_axis=0, concat_axis=1, tiled=True)
    lined = jnp.transpose(moved.reshape(rows_y, count_wide, part_z, cells_x), (0, 2, 1, 3))
    lined = lined.reshape(rows_y * part_z, total_x)
    spectral_x = jnp.dot(lined, whole_x, precision=highest)
    shift_y = lax.dynamic_slice_in_dim(eigen_y, index_wide * rows_y, rows_y)
    shift_z = lax.dynamic_slice_in_dim(eigen_z, index_narrow * part_z, part_z)
    shift_yz = (shift_y[:, None] + shift_z[None, :]).reshape(rows_y * part_z, 1)
    scaled = spectral_x / (eigen_x[None, :] + shift_yz)
    inverse_x = contract_last(scaled, whole_x)
    unlined = jnp.transpose(inverse_x.reshape(rows_y, part_z, count_wide, cells_x), (0, 2, 1, 3))
    unlined = unlined.reshape(rows_y, count_wide * part_z * cells_x)
    pencil = lax.all_to_all(unlined, "wide", split_axis=1, concat_axis=0, tiled=True)
    pencil = jnp.dot(whole_y, pencil, precision=highest)
    back = lax.all_to_all(pencil, "narrow", split_axis=0, concat_axis=1, tiled=True)
    brick = jnp.transpose(back.reshape(cells_y, cells_z, cells_x), (2, 0, 1))
    result = contract_last(brick.reshape(cells_x * cells_y, cells_z), whole_z)
    precond = result.reshape(cells_x, cells_y, cells_z)
    product_now = lax.psum(jnp.sum(residual * precond), ("wide", "narrow"))
    direction = precond + product_now / product_before * direction
    padded = padded_2(direction, (("wide", 0), ("narrow", 1)), 3)
    image = apply_padded(padded, cells_x, cells_y)
    curvature = lax.psum(jnp.sum(direction * image), ("wide", "narrow"))
    alpha = product_now / curvature
    solution = solution + alpha * direction
    residual = residual - alpha * image
    return (solution, residual, direction)


def per_device(*arrays):
    residual, basis_x, basis_y = arrays[1], arrays[4], arrays[5]
    wide, narrow = lax.axis_size("wide"), lax.axis_size("narrow")
    plan = Plan(*residual.shape, basis_x.shape[1], basis_y.shape[1], wide, narrow)
    if plan.fits:
        return by_pencils(plan, *arrays)
    return general(*arrays)


def solution(mesh):
    placed = (
        P("wide", "narrow", None),
        P("wide", "narrow", None),
        P("wide", "narrow", None),
        P(),
        P("wide", None),
        P("narrow", None),
        P("narrow", None),
        P(),
        P(),
        P(),
    )
    return jax.shard_map(
        per_device,
        mesh=mesh,
        in_specs=placed,
        out_specs=(P("wide", "narrow", None), P("wide", "narrow", None), P("wide", "narrow", None)),
        check_vma=False,
    )
```

```python
import functools

import jax
import jax.numpy as jnp
import ml_dtypes
import numpy as np
from jax import lax
from jax.experimental import pallas as pl
from jax.experimental.pallas import tpu as pltpu
from jax.sharding import PartitionSpec as P

mass_band = (
    1.0 / 5040.0,
    1.0 / 42.0,
    397.0 / 1680.0,
    151.0 / 315.0,
    397.0 / 1680.0,
    1.0 / 42.0,
    1.0 / 5040.0,
)
stiff_band = (-1.0 / 120.0, -0.2, -0.125, 2.0 / 3.0, -0.125, -0.2, -1.0 / 120.0)
highest = lax.Precision.HIGHEST
LANES = 128
HALO = 3
EDGE = 8
both = ("wide", "narrow")
MIB = 1024 * 1024


def split(x):
    high = x.astype(jnp.bfloat16)
    low = (x - high.astype(jnp.float32)).astype(jnp.bfloat16)
    return high, low


def dot3(left, right, over):
    dims = ((over[:1], over[1:]), ((), ()))
    one = functools.partial(
        lax.dot_general, dimension_numbers=dims, preferred_element_type=jnp.float32
    )
    return one(left[0], right[0]) + one(left[1], right[0]) + one(left[0], right[1])


class Plan:
    def __init__(self, cells_x, cells_y, cells_z, total_x, total_y, wide, narrow):
        self.cells_x, self.cells_y, self.cells_z = cells_x, cells_y, cells_z
        self.total_x, self.total_y = total_x, total_y
        self.wide, self.narrow, self.count = wide, narrow, wide * narrow
        self.rest = cells_y - LANES
        self.fits = (
            cells_z % self.count == 0
            and cells_x % 8 == 0
            and self.rest > 0
            and LANES % self.rest == 0
            and self.rest < LANES
            and total_y % LANES == LANES // 2
            and wide % 2 == 0
            and (total_x // 2) % 16 == 0
            and self.count % 8 == 0
        )
        if not self.fits:
            return
        self.share = cells_z // self.count
        self.group = LANES // self.rest
        self.tiles = cells_x // 8
        self.chunks = [(0, self.group), (self.group, self.share - self.group)]
        self.fits = (
            self.group % 2 == 0
            and self.share % 2 == 0
            and self.share > self.group
            and self.share % self.group != 0
            and self.tiles >= 3
            and 2 * LANES < cells_z <= 3 * LANES
        )
        if self.fits:
            _, _, _, _, fit, width = self.shape_of(1)
            self.fits = self.tiles % fit != 0 or fit * width < LANES

    def rows(self, chunk):
        start, size = self.chunks[chunk]
        return start * self.count, size * self.count

    def shape_of(self, chunk):
        size = self.chunks[chunk][1]
        part = size % self.group
        width = part * self.rest
        fit = LANES // width if part else 1
        tails = -(-self.tiles // fit) if part else 0
        return size, size + size // self.group, part, tails, fit, width

    def message(self, chunk):
        _, per, _, tails, _, _ = self.shape_of(chunk)
        return (self.count, self.tiles * per + tails, 8, LANES)


def forward_kernel(plan, chunk, field_ref, basis_ref, out_ref, high_ref, low_ref, stage_ref):
    size, per, part, tails, fit, width = plan.shape_of(chunk)
    step = pl.program_id(0)

    @pl.when(step == 0)
    def _():
        high_ref[...], low_ref[...] = split(basis_ref[...])
        if tails:
            out_ref[:, plan.tiles * per :] = jnp.zeros((plan.count, tails, 8, LANES), jnp.float32)

    basis = (high_ref[...], low_ref[...])
    for i in range(8):
        stage_ref[i] = dot3(basis, split(field_ref[i]), (1, 1))
    base = step * per if tails else 0
    rests = []
    for j in range(size):
        at = j * plan.count
        turned = jnp.swapaxes(stage_ref[:, at : at + plan.count, :], 0, 1)
        out_ref[:, base + j] = turned[:, :, :LANES]
        rests.append(turned[:, :, LANES:])
    for piece in range(size // plan.group):
        some = rests[piece * plan.group : (piece + 1) * plan.group]
        out_ref[:, base + size + piece] = jnp.concatenate(some, axis=2)
    if tails:
        some = jnp.concatenate(rests[size - part :], axis=2)
        for place in range(fit):

            @pl.when(step % fit == place)
            def _():
                lanes = slice(place * width, (place + 1) * width)
                out_ref[:, plan.tiles * per + step // fit, :, lanes] = some


def forward_z(plan, chunk, field, basis):
    start, rows = plan.rows(chunk)
    basis = basis[start : start + rows]
    message = plan.message(chunk)
    _, per, _, tails, _, _ = plan.shape_of(chunk)
    if tails:
        out_spec = pl.BlockSpec(message, lambda t: (0, 0, 0, 0))
    else:
        out_spec = pl.BlockSpec((message[0], per) + message[2:], lambda t: (0, t, 0, 0))
    return pl.pallas_call(
        functools.partial(forward_kernel, plan, chunk),
        grid=(plan.tiles,),
        in_specs=[
            pl.BlockSpec((8, plan.cells_y, plan.cells_z), lambda t: (t, 0, 0)),
            pl.BlockSpec(basis.shape, lambda t: (0, 0)),
        ],
        out_specs=out_spec,
        out_shape=jax.ShapeDtypeStruct(message, jnp.float32),
        scratch_shapes=[
            pltpu.VMEM(basis.shape, jnp.bfloat16),
            pltpu.VMEM(basis.shape, jnp.bfloat16),
            pltpu.VMEM((8, rows, plan.cells_y), jnp.float32),
        ],
        compiler_params=pltpu.CompilerParams(vmem_limit_bytes=50 * MIB),
        cost_estimate=pl.CostEstimate(
            flops=6 * field.size * rows, bytes_accessed=8 * field.size, transcendentals=0
        ),
        name="forward_z",
    )(field, basis)


def add_chunk(plan, chunk, tile, part_ref, tail_ref, stage_ref):
    size, _, part, tails, fit, width = plan.shape_of(chunk)
    if tails:
        tail = tail_ref[:, 0]
        for place in range(1, fit):
            turned = pltpu.roll(tail_ref[:, 0], LANES - place * width, 2)
            tail = jnp.where(tile % fit == place, turned, tail)
    for j in range(size):
        at, q = j * plan.count, j % plan.group
        lanes = slice(q * plan.rest, (q + 1) * plan.rest)
        stage_ref[:, at : at + plan.count, :LANES] = jnp.swapaxes(part_ref[:, j], 0, 1)
        if j < size - part:
            rest = part_ref[:, size + j // plan.group, :, lanes]
        else:
            rest = tail[:, :, lanes]
        stage_ref[:, at : at + plan.count, LANES:] = jnp.swapaxes(rest, 0, 1)


def base_kernel(plan, chunk, part_ref, basis_ref, out_ref, high_ref, low_ref, stage_ref):
    step = pl.program_id(0)

    @pl.when(step == 0)
    def _():
        high_ref[...], low_ref[...] = split(basis_ref[...])

    add_chunk(plan, chunk, step, part_ref, None, stage_ref)
    basis = (high_ref[...], low_ref[...])
    for i in range(8):
        out_ref[i] = dot3(split(stage_ref[i].T), basis, (1, 0))


def final_kernel(plan, chunk, ends, pick, *refs):
    part_ref, tail_ref, last_ref, basis_ref, base_ref, old_ref, before_ref = refs[:7]
    if ends:
        out_ref, now_ref, high_ref, low_ref, stage_ref = refs[7:]
    else:
        _, out_ref, high_ref, low_ref, stage_ref = refs[7:]
    step = pl.program_id(0)

    @pl.when(step == 0)
    def _():
        high_ref[...], low_ref[...] = split(basis_ref[...])

    def work():
        add_chunk(plan, chunk, pick(step), part_ref, tail_ref, stage_ref)
        now = jnp.sum(last_ref[:, 0, 0, LANES - 1 :], axis=0, keepdims=True)
        beta = now / before_ref[...]
        basis = (high_ref[...], low_ref[...])
        for i in range(8):
            value = dot3(split(stage_ref[i].T), basis, (1, 0))
            out_ref[i] = base_ref[i] + value + beta * old_ref[i]
        if ends:
            now_ref[...] = jnp.broadcast_to(now, now_ref.shape)

    work()


def inverse_scratch(plan, basis):
    return [
        pltpu.VMEM(basis.shape, jnp.bfloat16),
        pltpu.VMEM(basis.shape, jnp.bfloat16),
        pltpu.VMEM((8, basis.shape[0], plan.cells_y), jnp.float32),
    ]


def inverse_cost(plan, basis, tiles):
    size = tiles * 8 * plan.cells_y * plan.cells_z
    return pl.CostEstimate(
        flops=6 * size * basis.shape[0], bytes_accessed=12 * size, transcendentals=0
    )


def inverse_base(plan, chunk, part, basis):
    start, rows = plan.rows(chunk)
    per = plan.shape_of(chunk)[1]
    basis = basis[start : start + rows]
    return pl.pallas_call(
        functools.partial(base_kernel, plan, chunk),
        grid=(plan.tiles,),
        in_specs=[
            pl.BlockSpec((plan.count, per, 8, LANES), lambda t: (0, t, 0, 0)),
            pl.BlockSpec(basis.shape, lambda t: (0, 0)),
        ],
        out_specs=pl.BlockSpec((8, plan.cells_y, plan.cells_z), lambda t: (t, 0, 0)),
        out_shape=jax.ShapeDtypeStruct((plan.cells_x, plan.cells_y, plan.cells_z), jnp.float32),
        scratch_shapes=inverse_scratch(plan, basis),
        compiler_params=pltpu.CompilerParams(vmem_limit_bytes=50 * MIB),
        cost_estimate=inverse_cost(plan, basis, plan.tiles),
        name="inverse_base",
    )(part, basis)


def inverse_final(plan, chunk, part, basis, base, old, before, done=None):
    ends = done is None
    start, rows = plan.rows(chunk)
    basis = basis[start : start + rows]
    last = plan.tiles - 1
    if ends:
        pick = lambda t: t * last
    else:
        pick = lambda t: t + 1
    tile = (8, plan.cells_y, plan.cells_z)
    brick = pl.BlockSpec(tile, lambda t: (pick(t), 0, 0))
    _, per, _, _, fit, _ = plan.shape_of(chunk)
    in_specs = [
        pl.BlockSpec((plan.count, per, 8, LANES), lambda t: (0, pick(t), 0, 0)),
        pl.BlockSpec(
            (plan.count, 1, 8, LANES), lambda t: (0, plan.tiles * per + pick(t) // fit, 0, 0)
        ),
        pl.BlockSpec((plan.count, 1, 8, LANES), lambda t: (0, part.shape[1] - 1, 0, 0)),
        pl.BlockSpec(basis.shape, lambda t: (0, 0)),
        brick,
        brick,
        pl.BlockSpec((1, 1), lambda t: (0, 0)),
    ]
    operands = [part, part, part, basis, base, old, before.reshape(1, 1)]
    out_specs = brick
    if ends:
        out_specs = [out_specs, pl.BlockSpec((8, LANES), lambda t: (0, 0))]
        out_shape = [
            jax.ShapeDtypeStruct(base.shape, jnp.float32),
            jax.ShapeDtypeStruct((8, LANES), jnp.float32),
        ]
    else:
        in_specs.append(pl.BlockSpec(memory_space=pl.ANY))
        operands.append(done)
        out_shape = jax.ShapeDtypeStruct(base.shape, jnp.float32)
    return pl.pallas_call(
        functools.partial(final_kernel, plan, chunk, ends, pick),
        grid=(2 if ends else plan.tiles - 2,),
        input_output_aliases={} if ends else {len(operands) - 1: 0},
        in_specs=in_specs,
        out_specs=out_specs,
        out_shape=out_shape,
        scratch_shapes=inverse_scratch(plan, basis),
        compiler_params=pltpu.CompilerParams(vmem_limit_bytes=50 * MIB),
        cost_estimate=inverse_cost(plan, basis, 2 if ends else plan.tiles - 2),
        name="inverse_ends" if ends else "inverse_inner",
    )(*operands)


def middle_kernel(plan, chunk, *refs):
    (
        in_ref,
        basis_x_ref,
        turned_x_ref,
        main_y_ref,
        rest_y_ref,
        eigen_x_ref,
        shift_ref,
        total_ref,
        out_ref,
        sum_ref,
        bx_high,
        bx_low,
        tx_high,
        tx_low,
        my_high,
        my_low,
        ry_high,
        ry_low,
        u_high,
        u_low,
        q_high,
        q_low,
        rest_acc,
    ) = refs
    size, per, part, tails, fit, lanes = plan.shape_of(chunk)
    full = size // plan.group
    last = chunk == len(plan.chunks) - 1
    wide, narrow, tiles = plan.wide, plan.narrow, plan.tiles
    half = plan.total_x // 2
    lump = wide // 2
    span = plan.total_y + LANES // 2
    width = 2 * plan.total_y
    bx_high[...], bx_low[...] = split(basis_x_ref[...])
    tx_high[...], tx_low[...] = split(turned_x_ref[...])
    my_high[...], my_low[...] = split(main_y_ref[...])
    ry_high[...], ry_low[...] = split(rest_y_ref[...])
    rest_acc[...] = jnp.zeros_like(rest_acc)

    def gathered(h, places):
        rows = pl.ds(h * lump, lump)
        sides = []
        for n in range(narrow):
            some = []
            for t in range(tiles):
                piece, turn = places(t)
                value = in_ref[rows, n, piece]
                some.append(pltpu.roll(value, LANES - turn, 2) if turn else value)
            sides.append(jnp.stack(some, axis=1).reshape(half, LANES))
        return jnp.concatenate(sides, axis=1)

    def pair(in_tail, p, total):
        for h in range(2):
            if in_tail:
                rest = gathered(h, lambda t: (tiles * per + t // fit, t % fit * lanes))
            else:
                rest = gathered(h, lambda t: (t * per + size + 2 * p // plan.group, 0))
            rest = split(rest)
            parts = []
            for s in range(2):
                j = 2 * p + s
                q = lax.rem(j, plan.group)
                parts.append(
                    dot3(split(gathered(h, lambda t: (t * per + j, 0))), (my_high[s], my_low[s]), (1, 0))
                    + dot3(rest, (ry_high[q], ry_low[q]), (1, 0))
                )
            cut = span - LANES
            joined = jnp.concatenate(
                [
                    parts[0][:, :cut],
                    parts[0][:, cut:] + parts[1][:, :LANES],
                    parts[1][:, LANES:],
                ],
                axis=1,
            )
            rows = pl.ds(h * half, half)
            u_high[rows, :], u_low[rows, :] = split(joined)
        shift = shift_ref[p]
        for h in range(2):
            rows = pl.ds(h * half, half)
            spectral = dot3(
                (tx_high[rows, :], tx_low[rows, :]), (u_high[...], u_low[...]), (1, 0)
            )
            scaled = spectral / (eigen_x_ref[rows, :] + shift)
            total = total + jnp.sum((spectral * scaled).reshape(half // 8, 8, width), axis=0)
            q_high[rows, :], q_low[rows, :] = split(scaled)
        for h in range(2):
            rows = pl.ds(h * half, half)
            value = dot3((bx_high[rows, :], bx_low[rows, :]), (q_high[...], q_low[...]), (1, 0))
            for s in range(2):
                j = 2 * p + s
                mine = split(value[:, s * (width - span) : s * (width - span) + span])
                main = dot3(mine, (my_high[s], my_low[s]), (1, 1))
                q = lax.rem(j, plan.group)
                rest_acc[2 * p // plan.group, rows, :] += dot3(
                    mine, (ry_high[q], ry_low[q]), (1, 1)
                )
                for n in range(narrow):
                    side = main[:, n * LANES : (n + 1) * LANES].reshape(lump, tiles, 8, LANES)
                    for t in range(tiles):
                        out_ref[pl.ds(h * lump, lump), n, t * per + j] = side[:, t]
        return total

    total = jnp.zeros((8, width), jnp.float32)
    total = lax.fori_loop(0, (size - part) // 2, functools.partial(pair, False), total)
    if tails:
        total = lax.fori_loop((size - part) // 2, size // 2, functools.partial(pair, True), total)
    value = total_ref[...] + jnp.sum(total)
    sum_ref[...] = value
    for n in range(narrow):
        side = slice(n * LANES, (n + 1) * LANES)
        for piece in range(full):
            rest = rest_acc[piece, :, side].reshape(wide, tiles, 8, LANES)
            for t in range(tiles):
                out_ref[:, n, t * per + size + piece] = rest[:, t]
        for tail in range(tails):
            rest = rest_acc[full, :, side].reshape(wide, tiles, 8, LANES)
            joined = rest[:, tail * fit]
            for t in range(tail * fit + 1, min(tail * fit + fit, tiles)):
                joined = joined + pltpu.roll(rest[:, t], t % fit * lanes, 2)
            if last and tail == tails - 1:
                lane = lax.broadcasted_iota(jnp.int32, joined.shape, 2)
                joined = jnp.where(lane == LANES - 1, value[:1, :][None], joined)
            out_ref[:, n, tiles * per + tail] = joined


def middle(plan, chunk, message, basis_x, turned_x, main_y, rest_y, eigen_x, shift, total):
    size = plan.chunks[chunk][1]
    pieces = -(-size // plan.group)
    shape = (plan.wide, plan.narrow) + message.shape[1:]
    square = (plan.total_x, plan.total_x)
    pencil = (plan.total_x, 2 * plan.total_y)
    half = jnp.bfloat16
    out, total = pl.pallas_call(
        functools.partial(middle_kernel, plan, chunk),
        out_shape=[
            jax.ShapeDtypeStruct(shape, jnp.float32),
            jax.ShapeDtypeStruct((8, LANES), jnp.float32),
        ],
        in_specs=[pl.BlockSpec(memory_space=pltpu.VMEM)] * 8,
        out_specs=[pl.BlockSpec(memory_space=pltpu.VMEM)] * 2,
        scratch_shapes=[
            pltpu.VMEM(square, half),
            pltpu.VMEM(square, half),
            pltpu.VMEM(square, half),
            pltpu.VMEM(square, half),
            pltpu.VMEM(main_y.shape, half),
            pltpu.VMEM(main_y.shape, half),
            pltpu.VMEM(rest_y.shape, half),
            pltpu.VMEM(rest_y.shape, half),
            pltpu.VMEM(pencil, half),
            pltpu.VMEM(pencil, half),
            pltpu.VMEM(pencil, half),
            pltpu.VMEM(pencil, half),
            pltpu.VMEM((pieces, plan.total_x, plan.narrow * LANES), jnp.float32),
        ],
        compiler_params=pltpu.CompilerParams(vmem_limit_bytes=44 * MIB),
        cost_estimate=pl.CostEstimate(
            flops=12 * size * plan.total_x * plan.total_y * (plan.total_x + plan.total_y),
            bytes_accessed=8 * message.size,
            transcendentals=0,
        ),
        name="middle",
    )(message.reshape(shape), basis_x, turned_x, main_y, rest_y, eigen_x, shift, total)
    return out.reshape(message.shape), total


def shifted(x, step, axis):
    count = lax.axis_size(axis)
    pairs = [(i + step, i) for i in range(count) if 0 <= i + step < count]
    return lax.ppermute(x, axis, pairs)


def from_sides(low, high, axis):
    if lax.axis_size(axis) != 2:
        return shifted(high, -1, axis), shifted(low, 1, axis)
    second = lax.axis_index(axis) == 1
    got = lax.ppermute(jnp.where(second, low, high), axis, [(0, 1), (1, 0)])
    return jnp.where(second, got, 0.0), jnp.where(second, 0.0, got)


mass_scale, stiff_scale = 5040.0, 120.0
CUT = LANES + LANES // 2
GROUP = 4


def band_matrices(cells_z):
    offset = np.arange(cells_z)[:, None] - np.arange(cells_z)[None, :]
    near = np.abs(offset) <= HALO
    tables = []
    for band, scale in ((mass_band, mass_scale), (stiff_band, stiff_scale)):
        whole = np.rint(np.asarray(band) * scale)
        full = np.where(near, whole[np.clip(offset + HALO, 0, 2 * HALO)], 0.0)
        first = np.zeros((2 * LANES, 2 * LANES))
        first[:, :CUT] = full[: 2 * LANES, :CUT]
        second = np.zeros((2 * LANES, 2 * LANES))
        second[: cells_z - LANES, CUT - LANES : cells_z - LANES] = full[LANES:, CUT:]
        tables.append(np.stack([first, second]).astype(np.float32))
    mass, stiff = tables
    high = mass.astype(ml_dtypes.bfloat16)
    low = (mass - high.astype(np.float32)).astype(ml_dtypes.bfloat16)
    stiff = stiff.astype(ml_dtypes.bfloat16)
    mixed = np.concatenate([high, high, low, stiff, stiff], axis=1)
    return mixed, np.concatenate([high, high, low], axis=1)


def stencil_kernel(plan, *refs):
    own, before_x, after_x, before_y, after_y, mixed_ref, mass_ref, image_ref, sum_ref = refs[:9]
    field, f_high, f_low, s_high, s_low, mixes, total, sems = refs[9:]
    cells_x, cells_y, cells_z = plan.cells_x, plan.cells_y, plan.cells_z
    tiles = plan.tiles
    padded_y = cells_y + 2 * EDGE
    own_y = pl.ds(EDGE, cells_y)
    step = pl.program_id(0)

    def tile_copy(t):
        return pltpu.make_async_copy(
            own.at[pl.ds(8 * t, 8)], field.at[pl.ds(HALO + 8 * t, 8), own_y, :], sems.at[t]
        )

    first_copy = pltpu.make_async_copy(
        before_x, field.at[pl.ds(0, HALO), own_y, :], sems.at[tiles]
    )
    last_copy = pltpu.make_async_copy(
        after_x, field.at[pl.ds(HALO + cells_x, HALO), own_y, :], sems.at[tiles + 1]
    )

    @pl.when(step == 0)
    def _():
        first_copy.start()
        for t in range(tiles):
            tile_copy(t).start()
        last_copy.start()
        total[...] = jnp.zeros_like(total)
        for ref in (f_high, f_low, s_high, s_low):
            ref[:, cells_z:] = jnp.zeros((ref.shape[0], ref.shape[1] - cells_z), ref.dtype)
        field[:, EDGE - HALO : EDGE, :] = jnp.swapaxes(before_y[...], 0, 1)
        field[:, EDGE + cells_y : EDGE + cells_y + HALO, :] = jnp.swapaxes(after_y[...], 0, 1)
        first_copy.wait()
        tile_copy(0).wait()

    @pl.when(step < tiles - 1)
    def _():
        tile_copy(step + 1).wait()

    @pl.when(step == tiles - 1)
    def _():
        last_copy.wait()

    blocks = mixes.shape[1]
    ratio = stiff_scale / mass_scale

    def one(left, right):
        return lax.dot_general(
            left, right, (((1,), (0,)), ((), ())), preferred_element_type=jnp.float32
        )

    def planes(g, carry):
        for i in range(GROUP):
            x = step * 8 + g * GROUP + i
            middle_plane = field[x + HALO]
            first = ratio * stiff_band[HALO] * middle_plane
            second = mass_band[HALO] * middle_plane
            for o in range(1, HALO + 1):
                around = field[x + HALO - o] + field[x + HALO + o]
                first = first + ratio * stiff_band[HALO + o] * around
                second = second + mass_band[HALO + o] * around
            rows = pl.ds(i * padded_y, padded_y)
            f_high[rows, :cells_z], f_low[rows, :cells_z] = split(first)
            s_high[rows, :cells_z], s_low[rows, :cells_z] = split(second)
        window_a, window_b = [], []
        for w in range(2):
            lanes = pl.ds(w * LANES, 2 * LANES)
            fh, fl, sh, sl = (ref[:, lanes] for ref in (f_high, f_low, s_high, s_low))
            window_a.append(one(jnp.concatenate([fh, fl, fh, sh, sl], axis=1), mixed_ref[w]))
            window_b.append(one(jnp.concatenate([sh, sl, sh], axis=1), mass_ref[w]))
        (a_left, a_right), (b_left, b_right) = window_a, window_b
        a = (a_left[:, :LANES], a_left[:, LANES:] + a_right[:, :LANES], a_right[:, LANES:])
        b = (b_left[:, :LANES], b_left[:, LANES:] + b_right[:, :LANES], b_right[:, LANES:])
        for k in range(blocks):
            for o in range(HALO + 1):
                mass = mass_band[HALO + o] / stiff_scale
                mixes[o, k] = mass * a[k] + (stiff_band[HALO + o] / mass_scale) * b[k]
        for i in range(GROUP):
            plane = g * GROUP + i
            for k in range(blocks):
                lanes = min(LANES, cells_z - k * LANES)
                at = lambda o, by: mixes[o, k, pl.ds(i * padded_y + EDGE + by, cells_y), :]
                image = at(0, 0)
                for o in range(1, HALO + 1):
                    image = image + (at(o, -o) + at(o, o))
                here = pl.ds(k * LANES, lanes)
                image_ref[plane, :, here] = image[:, :lanes]
                product = image[:, :lanes] * field[step * 8 + plane + HALO, own_y, here]
                total[:, here] += jnp.sum(product.reshape(cells_y // 8, 8, lanes), axis=0)
        return carry

    lax.fori_loop(0, 8 // GROUP, planes, 0)

    @pl.when(step == pl.num_programs(0) - 1)
    def _():
        sum_ref[...] = jnp.full(sum_ref.shape, jnp.sum(total[...]), jnp.float32)


def stencil(plan, direction, before_x, after_x):
    cells_x, cells_y, cells_z = direction.shape

    def strip(rows):
        parts = [jnp.swapaxes(v[:, rows], 0, 1) for v in (before_x, direction, after_x)]
        return jnp.concatenate(parts, axis=1)

    before_y, after_y = from_sides(
        strip(slice(0, HALO)), strip(slice(cells_y - HALO, cells_y)), "narrow"
    )
    mixed, mass = band_matrices(cells_z)
    padded_y = cells_y + 2 * EDGE
    blocks = -(-cells_z // LANES)
    lump = (GROUP * padded_y, blocks * LANES)
    return pl.pallas_call(
        functools.partial(stencil_kernel, plan),
        grid=(cells_x // 8,),
        in_specs=[pl.BlockSpec(memory_space=pl.ANY)] * 3
        + [pl.BlockSpec(before_y.shape, lambda t: (0, 0, 0))] * 2
        + [pl.BlockSpec(v.shape, lambda t: (0, 0, 0)) for v in (mixed, mass)],
        out_specs=[
            pl.BlockSpec((8, cells_y, cells_z), lambda t: (t, 0, 0)),
            pl.BlockSpec((plan.count, 8, LANES), lambda t: (0, 0, 0)),
        ],
        out_shape=[
            jax.ShapeDtypeStruct(direction.shape, jnp.float32),
            jax.ShapeDtypeStruct((plan.count, 8, LANES), jnp.float32),
        ],
        scratch_shapes=[
            pltpu.VMEM((cells_x + 2 * HALO, padded_y, cells_z), jnp.float32),
            pltpu.VMEM(lump, jnp.bfloat16),
            pltpu.VMEM(lump, jnp.bfloat16),
            pltpu.VMEM(lump, jnp.bfloat16),
            pltpu.VMEM(lump, jnp.bfloat16),
            pltpu.VMEM((HALO + 1, blocks, GROUP * padded_y, LANES), jnp.float32),
            pltpu.VMEM((8, cells_z), jnp.float32),
            pltpu.SemaphoreType.DMA((plan.tiles + 2,)),
        ],
        compiler_params=pltpu.CompilerParams(vmem_limit_bytes=50 * MIB),
        cost_estimate=pl.CostEstimate(
            flops=8 * direction.size * cells_z, bytes_accessed=8 * direction.size, transcendentals=0
        ),
        name="stencil",
    )(direction, before_x, after_x, before_y, after_y, mixed, mass)


def update_kernel(now_ref, parts_ref, solution_ref, residual_ref, direction_ref, image_ref, *outs):
    curvature = jnp.sum(parts_ref[:, 0, :1], axis=0, keepdims=True)
    alpha = (now_ref[:1, :1] / curvature)[None]
    outs[0][...] = solution_ref[...] + alpha * direction_ref[...]
    outs[1][...] = residual_ref[...] - alpha * image_ref[...]


def update(now, parts, solution, residual, direction, image):
    brick = pl.BlockSpec((4,) + image.shape[1:], lambda t: (t, 0, 0))
    return pl.pallas_call(
        update_kernel,
        grid=(image.shape[0] // 4,),
        in_specs=[
            pl.BlockSpec(now.shape, lambda t: (0, 0)),
            pl.BlockSpec(parts.shape, lambda t: (0, 0, 0)),
        ]
        + [brick] * 4,
        out_specs=[brick] * 2,
        out_shape=[jax.ShapeDtypeStruct(image.shape, jnp.float32)] * 2,
        compiler_params=pltpu.CompilerParams(vmem_limit_bytes=50 * MIB),
        name="update",
    )(now, parts, solution, residual, direction, image)


def scatter(x):
    return lax.all_to_all(x, both, split_axis=0, concat_axis=0, tiled=True)


def dealt(plan, whole_z):
    columns = whole_z.T.reshape(plan.count, plan.share, plan.cells_z)
    return jnp.swapaxes(columns, 0, 1).reshape(plan.cells_z, plan.cells_z)


def basis_y_blocks(plan, whole_y):
    by_owner = whole_y.reshape(plan.narrow, plan.cells_y, plan.total_y)
    main = by_owner[:, :LANES].reshape(plan.narrow * LANES, plan.total_y)
    rest = by_owner[:, LANES:]
    half = LANES // 2
    sides = [(0, half), (half, 0)]
    mains = jnp.stack([jnp.pad(main, ((0, 0), s)) for s in sides])
    rests = []
    for q in range(plan.group):
        after = LANES - (q + 1) * plan.rest
        padded = jnp.pad(rest, ((0, 0), (q * plan.rest, after), sides[q % 2]))
        rests.append(padded.reshape(plan.narrow * LANES, plan.total_y + half))
    return mains, jnp.stack(rests)


def by_pencils(
    plan,
    solution,
    residual,
    direction,
    previous_product,
    basis_x,
    basis_y,
    basis_z,
    eigen_x,
    eigen_y,
    eigen_z,
):
    whole_z = lax.all_gather(basis_z, "narrow", axis=0, tiled=True)
    turned_z = dealt(plan, whole_z)
    whole_y = lax.all_gather(basis_y, "narrow", axis=0, tiled=True)
    whole_x = lax.all_gather(basis_x, "wide", axis=0, tiled=True)
    sent = [forward_z(plan, k, residual, turned_z) for k in range(2)]
    arrived = [scatter(sent[0])]
    later, whole_x, whole_y = lax.optimization_barrier((sent[1], whole_x, whole_y))
    arrived.append(scatter(later))
    main_y, rest_y = basis_y_blocks(plan, whole_y)
    turned_x = whole_x.T
    index = lax.axis_index("wide") * plan.narrow + lax.axis_index("narrow")
    mine_z = lax.dynamic_slice_in_dim(eigen_z, index * plan.share, plan.share)
    shifts = (mine_z[:, None] + eigen_y[None, :]).reshape(plan.share // 2, 1, 2 * plan.total_y)
    total = jnp.zeros((8, LANES), jnp.float32)
    returned = []
    for k, (start, size) in enumerate(plan.chunks):
        shift = shifts[start // 2 : (start + size) // 2]
        back, total = middle(
            plan,
            k,
            arrived[k],
            whole_x,
            turned_x,
            main_y,
            rest_y,
            eigen_x.reshape(-1, 1),
            shift,
            total,
        )
        returned.append(scatter(back))
    base = inverse_base(plan, 0, returned[0], turned_z)
    inverse = functools.partial(
        inverse_final, plan, 1, returned[1], turned_z, base, direction, previous_product
    )
    ends, now = inverse()
    before_x = shifted(ends[plan.cells_x - HALO :], -1, "wide")
    after_x = shifted(ends[:HALO], 1, "wide")
    direction = inverse(ends)
    image, part = stencil(plan, direction, before_x, after_x)
    solution, residual = update(now, scatter(part), solution, residual, direction, image)
    return solution, residual, direction


def padded_2(x, sides, width):
    for axis, dim in sides:
        count, length = (lax.axis_size(axis), x.shape[dim])
        up = [(i, (i + 1) % count) for i in range(count - 1)]
        down = [(j, i) for i, j in up]
        last = lax.slice_in_dim(x, length - width, length, axis=dim)
        leading = lax.slice_in_dim(x, 0, width, axis=dim)
        before = lax.ppermute(last, axis, up)
        after = lax.ppermute(leading, axis, down)
        x = jnp.concatenate([before, x, after], axis=dim)
    return x


def banded(field, coeffs, axis, length):
    total = coeffs[0] * lax.slice_in_dim(field, 0, length, axis=axis)
    for offset in range(1, 7):
        total = total + coeffs[offset] * lax.slice_in_dim(field, offset, offset + length, axis=axis)
    return total


def apply_padded(padded, length_x, length_y):
    length_z = padded.shape[2]
    along_z = jnp.pad(padded, ((0, 0), (0, 0), (3, 3)))
    mass_z = banded(along_z, mass_band, 2, length_z)
    stiff_z = banded(along_z, stiff_band, 2, length_z)
    first = banded(mass_z, mass_band, 1, length_y)
    second = banded(mass_z, stiff_band, 1, length_y) + banded(stiff_z, mass_band, 1, length_y)
    return banded(first, stiff_band, 0, length_x) + banded(second, mass_band, 0, length_x)


def contract_first(left, right):
    return lax.dot_general(left, right, (((0,), (0,)), ((), ())), precision=highest)


def contract_last(left, right):
    return lax.dot_general(left, right, (((1,), (1,)), ((), ())), precision=highest)


def general(
    solution,
    residual,
    direction,
    previous_product,
    basis_x,
    basis_y,
    basis_z,
    eigen_x,
    eigen_y,
    eigen_z,
):
    whole_x = lax.all_gather(basis_x, "wide", axis=0, tiled=True)
    whole_y, whole_z = (
        lax.all_gather(basis_y, "narrow", axis=0, tiled=True),
        lax.all_gather(basis_z, "narrow", axis=0, tiled=True),
    )
    count_wide = lax.axis_size("wide")
    count_narrow = lax.axis_size("narrow")
    index_wide = lax.axis_index("wide")
    index_narrow = lax.axis_index("narrow")
    cells_x, cells_y, cells_z = residual.shape
    total_x = whole_x.shape[0]
    total_y = whole_y.shape[0]
    product_before = previous_product[0]
    spectral = jnp.dot(residual.reshape(cells_x * cells_y, cells_z), whole_z, precision=highest)
    flat = jnp.transpose(spectral.reshape(cells_x, cells_y, cells_z), (1, 2, 0)).reshape(
        cells_y, cells_z * cells_x
    )
    pencil = contract_first(
        whole_y, lax.all_to_all(flat, "narrow", split_axis=1, concat_axis=0, tiled=True)
    )
    rows_y = total_y // count_wide
    part_z = cells_z // count_narrow
    moved = lax.all_to_all(pencil, "wide", split_axis=0, concat_axis=1, tiled=True)
    lined = jnp.transpose(moved.reshape(rows_y, count_wide, part_z, cells_x), (0, 2, 1, 3))
    lined = lined.reshape(rows_y * part_z, total_x)
    spectral_x = jnp.dot(lined, whole_x, precision=highest)
    shift_y = lax.dynamic_slice_in_dim(eigen_y, index_wide * rows_y, rows_y)
    shift_z = lax.dynamic_slice_in_dim(eigen_z, index_narrow * part_z, part_z)
    shift_yz = (shift_y[:, None] + shift_z[None, :]).reshape(rows_y * part_z, 1)
    scaled = spectral_x / (eigen_x[None, :] + shift_yz)
    inverse_x = contract_last(scaled, whole_x)
    unlined = jnp.transpose(inverse_x.reshape(rows_y, part_z, count_wide, cells_x), (0, 2, 1, 3))
    unlined = unlined.reshape(rows_y, count_wide * part_z * cells_x)
    pencil = lax.all_to_all(unlined, "wide", split_axis=1, concat_axis=0, tiled=True)
    pencil = jnp.dot(whole_y, pencil, precision=highest)
    back = lax.all_to_all(pencil, "narrow", split_axis=0, concat_axis=1, tiled=True)
    brick = jnp.transpose(back.reshape(cells_y, cells_z, cells_x), (2, 0, 1))
    result = contract_last(brick.reshape(cells_x * cells_y, cells_z), whole_z)
    precond = result.reshape(cells_x, cells_y, cells_z)
    product_now = lax.psum(jnp.sum(residual * precond), ("wide", "narrow"))
    direction = precond + product_now / product_before * direction
    padded = padded_2(direction, (("wide", 0), ("narrow", 1)), 3)
    image = apply_padded(padded, cells_x, cells_y)
    curvature = lax.psum(jnp.sum(direction * image), ("wide", "narrow"))
    alpha = product_now / curvature
    solution = solution + alpha * direction
    residual = residual - alpha * image
    return (solution, residual, direction)


def per_device(*arrays):
    residual, basis_x, basis_y = arrays[1], arrays[4], arrays[5]
    wide, narrow = lax.axis_size("wide"), lax.axis_size("narrow")
    plan = Plan(*residual.shape, basis_x.shape[1], basis_y.shape[1], wide, narrow)
    if plan.fits:
        return by_pencils(plan, *arrays)
    return general(*arrays)


def solution(mesh):
    placed = (
        P("wide", "narrow", None),
        P("wide", "narrow", None),
        P("wide", "narrow", None),
        P(),
        P("wide", None),
        P("narrow", None),
        P("narrow", None),
        P(),
        P(),
        P(),
    )
    return jax.shard_map(
        per_device,
        mesh=mesh,
        in_specs=placed,
        out_specs=(P("wide", "narrow", None), P("wide", "narrow", None), P("wide", "narrow", None)),
        check_vma=False,
    )
```
